32 devices in a mesh: plane: 4 (over z), slab: 8 (over y, x, core).
Axes of the slice: x: 2, y: 2, z: 4, core: 2. Of those that a mesh axis runs over, the one named last changes fastest.
Arguments:
- potential: float32 [20, 48, 4096], P('plane', None, 'slab'), may hold values from -1.5 to 1.5
- mixing: float32 [20], P('plane'), may hold values from 1.05 to 1.6
- lens_weight: float32 [20], P('plane'), may hold values from 0.02 to 0.08
- observed: float32 [20, 3, 48, 4096], P('plane', None, 'slab'), may hold values from -6 to 6
- noise_weight: float32 [20, 48, 4096], P('plane', 'slab'), may hold values from 0.3 to 3
Outputs:
- deflection: float32 [20, 2, 48, 4096], P('plane', None, 'slab')
- shear: float32 [20, 3, 48, 4096], P('plane', None, 'slab')
- potential_grad: float32 [20, 48, 4096], P('plane', None, 'slab')
The draws below stay inside these ranges and needn't reach their ends.
All inputs are finite; a program needn't handle non-finite values.
Results may differ from the reference program's by a relative error of at most 0.00013.
Values sent between devices are 32-bit elements; how exact they have to be, the bound alone decides.
No kernel may reach another device: no remote copies, remote signals or barrier semaphores. Data moves between devices by JAX's collectives and lax.ppermute only.
A program may use at most 256 MiB of HBM per device.

```python
import math
import jax
import jax.numpy as jnp
from jax import lax

W = 4096
PLANES = 20
NR = 48


def level_of(own_key, shape, cuts, smallest, high):
    def one(dim, shards_of):
        steps = jax.random.uniform(jax.random.fold_in(jax.random.fold_in(own_key, 6), dim), (shards_of,), jnp.float32, smallest / len(cuts), high / len(cuts))
        return jnp.repeat(jnp.exp(steps), shape[dim] // shards_of).reshape((-1,) + (1,) * (len(shape) - dim - 1))

    loudness = one(*cuts[0])
    for cut in cuts[1:]:
        loudness = loudness * one(*cut)
    return loudness


def noise(stream_key, dims, spread, limit, shards=(), dtype=jnp.bfloat16):
    entries = jax.random.normal(stream_key, dims, jnp.float32) * spread
    if len(shards) > 0:
        entries = level_of(stream_key, dims, shards, -0.22, 0.18) * entries
    return jnp.clip(entries, min=-limit, max=limit).astype(dtype)


def setup_inputs(seed: int = 0) -> dict:
    streams_of = jax.random.split(jax.random.key(seed), 6)
    return {
        "potential": noise(streams_of[0], (PLANES, NR, W), 0.25, 1.5, ((0, 4), (2, 8)), jnp.float32),
        "mixing": jnp.clip(jnp.exp(math.log(1.6) - 0.42121353 * jax.random.uniform(streams_of[1], (PLANES,), jnp.float32) ** level_of(streams_of[1], (PLANES,), ((0, 4),), -0.2, 0.2)), 1.05, 1.6),
        "lens_weight": jnp.clip(jnp.exp(math.log(0.08) - 1.3862944 * jax.random.uniform(streams_of[2], (PLANES,), jnp.float32) ** level_of(streams_of[2], (PLANES,), ((0, 4),), -0.2, 0.2)), 0.02, 0.08),
        "observed": noise(streams_of[3], (PLANES, 3, NR, W), 1.0, 6.0, ((0, 4), (2, 8)), jnp.float32),
        "noise_weight": jnp.clip(jnp.exp(math.log(3.0) - 2.3025851 * jax.random.uniform(streams_of[4], (PLANES, NR, W), jnp.float32) ** level_of(streams_of[4], (PLANES, NR, W), ((0, 4), (1, 8)), -0.2, 0.2)), 0.3, 3.0),
    }


def wrap_pad(array, dim):
    extent = array.shape[dim]
    leading = lax.slice_in_dim(array, 0, 1, axis=dim)
    trailing = lax.slice_in_dim(array, extent - 1, extent, axis=dim)
    return jnp.concatenate([trailing, array, leading], axis=dim)


def five_fields(padded):
    center = padded[..., 1:-1, 1:-1]
    row_next = padded[..., 2:, 1:-1]
    row_prev = padded[..., :-2, 1:-1]
    col_next = padded[..., 1:-1, 2:]
    col_prev = padded[..., 1:-1, :-2]
    mixed = 0.25 * (padded[..., 2:, 2:] - padded[..., 2:, :-2] - padded[..., :-2, 2:] + padded[..., :-2, :-2])
    return jnp.stack([0.5 * (row_next - row_prev), 0.5 * (col_next - col_prev),
                      row_next - 2.0 * center + row_prev, col_next - 2.0 * center + col_prev, mixed], axis=-3)


def adjoint_fields(padded):
    rows_part = padded[..., 0, 2:, 1:-1] - 2.0 * padded[..., 0, 1:-1, 1:-1] + padded[..., 0, :-2, 1:-1]
    cols_part = padded[..., 1, 1:-1, 2:] - 2.0 * padded[..., 1, 1:-1, 1:-1] + padded[..., 1, 1:-1, :-2]
    mixed_part = 0.25 * (padded[..., 2, 2:, 2:] - padded[..., 2, 2:, :-2] - padded[..., 2, :-2, 2:] + padded[..., 2, :-2, :-2])
    return rows_part + cols_part + mixed_part


def plane_forward(a_now, a_before, defl_now, defl_before, fields, mix, weight):
    diag_first = mix - weight * fields[2]
    diag_second = mix - weight * fields[3]
    off_diag = -weight * fields[4]
    keep = 1.0 - mix
    new_a = jnp.stack([diag_first * a_now[0] + off_diag * a_now[2] + keep * a_before[0],
                       diag_first * a_now[1] + off_diag * a_now[3] + keep * a_before[1],
                       off_diag * a_now[0] + diag_second * a_now[2] + keep * a_before[2],
                       off_diag * a_now[1] + diag_second * a_now[3] + keep * a_before[3]])
    new_defl = mix * defl_now + keep * defl_before - weight * fields[0:2]
    return new_a, new_defl


def shear_of(distort):
    return jnp.stack([1.0 - 0.5 * (distort[0] + distort[3]), 0.5 * (distort[3] - distort[0]), -0.5 * (distort[1] + distort[2])])


def source_adjoint(residual):
    return jnp.stack([-0.5 * (residual[..., 0, :, :] + residual[..., 1, :, :]), -0.5 * residual[..., 2, :, :],
                      -0.5 * residual[..., 2, :, :], -0.5 * (residual[..., 0, :, :] - residual[..., 1, :, :])], axis=-3)


def plane_adjoint(p_full, q_state, a_now, fields, mix, weight):
    diag_first = mix - weight * fields[2]
    diag_second = mix - weight * fields[3]
    off_diag = -weight * fields[4]
    keep = 1.0 - mix
    new_p = jnp.stack([diag_first * p_full[0] + off_diag * p_full[2],
                       diag_first * p_full[1] + off_diag * p_full[3],
                       off_diag * p_full[0] + diag_second * p_full[2],
                       off_diag * p_full[1] + diag_second * p_full[3]]) + q_state
    new_q = keep * p_full
    cot = jnp.stack([-weight * (p_full[0] * a_now[0] + p_full[1] * a_now[1]),
                     -weight * (p_full[2] * a_now[2] + p_full[3] * a_now[3]),
                     -weight * (p_full[0] * a_now[2] + p_full[1] * a_now[3] + p_full[2] * a_now[0] + p_full[3] * a_now[1])])
    return new_p, new_q, cot


def reference(potential, mixing, lens_weight, observed, noise_weight):
    fields = five_fields(wrap_pad(wrap_pad(potential, 1), 2))
    map_shape = potential.shape[1:]
    ones_map = jnp.ones(map_shape, jnp.float32)
    zeros_map = jnp.zeros(map_shape, jnp.float32)
    a_now = jnp.stack([ones_map, zeros_map, zeros_map, ones_map])
    a_before = a_now
    defl_now = jnp.zeros((2,) + map_shape, jnp.float32)
    defl_before = defl_now
    stored = []
    deflections = []
    shears = []
    for plane_index in range(PLANES):
        stored.append(a_now)
        new_a, new_defl = plane_forward(a_now, a_before, defl_now, defl_before, fields[plane_index],
                                        mixing[plane_index], lens_weight[plane_index])
        a_before, a_now = a_now, new_a
        defl_before, defl_now = defl_now, new_defl
        deflections.append(new_defl)
        shears.append(shear_of(new_a))
    deflection = jnp.stack(deflections)
    shear = jnp.stack(shears)
    residual = noise_weight[:, None] * (shear - observed)
    sources = source_adjoint(residual)
    p_state = jnp.zeros((4,) + map_shape, jnp.float32)
    q_state = jnp.zeros((4,) + map_shape, jnp.float32)
    cotangents = [None] * PLANES
    for plane_index in reversed(range(PLANES)):
        p_full = p_state + sources[plane_index]
        p_state, q_state, cotangents[plane_index] = plane_adjoint(p_full, q_state, stored[plane_index], fields[plane_index],
                                                                  mixing[plane_index], lens_weight[plane_index])
    cot = jnp.stack(cotangents)
    potential_grad = adjoint_fields(wrap_pad(wrap_pad(cot, 2), 3))
    return deflection, shear, potential_grad
```

```python
import functools

import jax
import jax.numpy as jnp
from jax import lax
from jax.experimental import pallas as pl
from jax.experimental.pallas import tpu as pltpu
from jax.sharding import PartitionSpec as P

R = 6
SUB = 8
EDGE = 128
F32 = jnp.float32
VMEM_LIMIT = 32 * 1024 * 1024


def pack_kernel(weight_ref, p_ref, out_ref):
    planes, rows, _ = p_ref.shape
    for k in range(planes):
        w = weight_ref[k]
        for s in range(out_ref.shape[0]):
            before = (R * s - 1) % rows
            after = (R * (s + 1)) % rows
            out_ref[s, k] = w * jnp.concatenate(
                [
                    p_ref[k, R * s : R * (s + 1), :],
                    p_ref[k, after : after + 1, :],
                    p_ref[k, before : before + 1, :],
                ],
                axis=0,
            )


def row_up(x):
    return pltpu.roll(x, SUB - 1, 0)


def row_down(x):
    return pltpu.roll(x, 1, 0)


def col_prev(x):
    return pltpu.roll(x, 1, 1)[:, EDGE:-EDGE]


def col_next(x):
    return pltpu.roll(x, x.shape[1] - 1, 1)[:, EDGE:-EDGE]


def transposed_step(m0, m1, off, p, q, keep):
    new_p = [
        m0 * p[0] + off * p[2] + q[0],
        m0 * p[1] + off * p[3] + q[1],
        off * p[0] + m1 * p[2] + q[2],
        off * p[1] + m1 * p[3] + q[3],
    ]
    return (new_p, [keep * x for x in p])


def pack_state(out_ref, fields):
    for j in range(R):
        out_ref[0, j] = jnp.concatenate(
            [fields[j], fields[6][j : j + 1], fields[7][j : j + 1]], axis=0
        )


def unpack_state(in_ref):
    tiles = [in_ref[0, j] for j in range(R)]
    fields = [t[0:R] for t in tiles]
    fields.append(jnp.concatenate([t[6:7] for t in tiles], axis=0))
    fields.append(jnp.concatenate([t[7:8] for t in tiles], axis=0))
    return fields


def forward_kernel(groups, planes, mix_ref, *refs):
    sources = refs[: 3 * groups]
    obs_ref, noise_ref = refs[3 * groups : 3 * groups + 2]
    defl_ref, shear_ref, m_ref, a_ref, src_ref, b_ref = refs[3 * groups + 2 :]
    width = obs_ref.shape[-1]
    one = jnp.ones((SUB, width), F32)
    zero = jnp.zeros((SUB, width), F32)
    a = [one, zero, zero, one]
    a_before = a
    psi = jnp.zeros((SUB, width + 2 * EDGE), F32)
    psi_before = psi
    for group in range(groups):
        mid_ref, left_ref, right_ref = sources[3 * group : 3 * group + 3]
        own = group == groups - 1
        for k in range(planes):
            mix = mix_ref[group * planes + k]
            keep = 1.0 - mix
            mid = mid_ref[0, k]
            ext = jnp.concatenate([left_ref[0, k], mid, right_ref[0, k]], axis=1)
            up = row_up(ext)
            down = row_down(ext)
            across = up - down
            twice = 2.0 * mid
            m0 = mix - ((up + down)[:, EDGE:-EDGE] - twice)
            m1 = mix - (col_next(ext) + col_prev(ext) - twice)
            off = 0.25 * (col_prev(across) - col_next(across))
            if own:
                m_ref[0, 3 * k] = m0
                m_ref[0, 3 * k + 1] = m1
                m_ref[0, 3 * k + 2] = off
                for j in range(4):
                    a_ref[0, 4 * k + j] = a[j]
            new_a = [
                m0 * a[0] + off * a[2] + keep * a_before[0],
                m0 * a[1] + off * a[3] + keep * a_before[1],
                off * a[0] + m1 * a[2] + keep * a_before[2],
                off * a[1] + m1 * a[3] + keep * a_before[3],
            ]
            a_before, a = (a, new_a)
            psi, psi_before = (mix * psi + keep * psi_before - ext, psi)
            if own:
                slope_rows = 0.5 * (row_up(psi) - row_down(psi))[:, EDGE:-EDGE]
                slope_cols = 0.5 * (col_next(psi) - col_prev(psi))
                defl_ref[k, 0] = slope_rows[0:R]
                defl_ref[k, 1] = slope_cols[0:R]
                shear = [
                    1.0 - 0.5 * (a[0] + a[3])[0:R],
                    0.5 * (a[3] - a[0])[0:R],
                    -0.5 * (a[1] + a[2])[0:R],
                ]
                noise = -0.5 * noise_ref[k]
                r = []
                for j in range(3):
                    shear_ref[k, j] = shear[j]
                    r.append(noise * (shear[j] - obs_ref[k, j]))
                src_ref[0, 3 * k, 0:R] = r[0] + r[1]
                src_ref[0, 3 * k + 1, 0:R] = r[2]
                src_ref[0, 3 * k + 2, 0:R] = r[0] - r[1]
    none = jnp.zeros((R, width), F32)
    p = [none] * 4
    q = [none] * 4
    for k in reversed(range(planes)):
        keep = 1.0 - mix_ref[(groups - 1) * planes + k]
        s0, s1, s3 = (src_ref[0, 3 * k + j, 0:R] for j in range(3))
        p = [p[0] + s0, p[1] + s1, p[2] + s1, p[3] + s3]
        m0, m1, off = (m_ref[0, 3 * k + j, 0:R] for j in range(3))
        p, q = transposed_step(m0, m1, off, p, q, keep)
    pack_state(b_ref, p + q)


def carry_kernel(planes, mix_ref, in_ref, b_ref, m_ref, out_ref):
    fields = unpack_state(in_ref)
    p, q = (fields[0:4], fields[4:8])
    for k in reversed(range(planes)):
        m0, m1, off = (m_ref[0, 3 * k + j, 0:R] for j in range(3))
        p, q = transposed_step(m0, m1, off, p, q, 1.0 - mix_ref[k])
    pack_state(out_ref, p + q)
    out_ref[...] += b_ref[...]


def gradient_kernel(planes, mix_ref, weight_ref, in_ref, src_ref, m_ref, a_ref, out_ref, cot_ref):
    step = pl.program_id(0)
    blocks = pl.num_programs(0)
    width = in_ref.shape[-1]
    fields = unpack_state(in_ref)
    p, q = (fields[0:4], fields[4:8])
    blank = jnp.zeros((SUB - R, width), F32)
    for k in reversed(range(planes)):
        s0, s1, s3 = (src_ref[0, 3 * k + j, 0:R] for j in range(3))
        p = [p[0] + s0, p[1] + s1, p[2] + s1, p[3] + s3]
        a = [a_ref[0, 4 * k + j, 0:R] for j in range(4)]
        w = -weight_ref[k]
        cots = [
            w * (p[0] * a[0] + p[1] * a[1]),
            w * (p[2] * a[2] + p[3] * a[3]),
            (0.25 * w) * (p[0] * a[2] + p[1] * a[3] + p[2] * a[0] + p[3] * a[1]),
        ]
        for j in range(3):
            cot_ref[step, 3 * k + j] = jnp.concatenate([cots[j], blank], axis=0)
        m0, m1, off = (m_ref[0, 3 * k + j, 0:R] for j in range(3))
        p, q = transposed_step(m0, m1, off, p, q, 1.0 - mix_ref[k])

    @pl.when(step == blocks - 1)
    def _():
        def block(c, carry):
            before = lax.rem(c + blocks - 1, blocks)
            after = lax.rem(c + 1, blocks)

            def ext(field):
                return jnp.concatenate(
                    [
                        cot_ref[before, field, :, width - EDGE :],
                        cot_ref[c, field],
                        cot_ref[after, field, :, 0:EDGE],
                    ],
                    axis=1,
                )

            for k in range(planes):
                cot_rows = cot_ref[c, 3 * k]
                cot_cols = ext(3 * k + 1)
                cot_mixed = ext(3 * k + 2)
                across = row_up(cot_mixed) - row_down(cot_mixed)
                rows_part = row_up(cot_rows) + row_down(cot_rows) - 2.0 * cot_rows
                cols_part = (
                    col_next(cot_cols) + col_prev(cot_cols) - 2.0 * cot_cols[:, EDGE:-EDGE]
                )
                out_ref[c, k] = rows_part + cols_part + (col_next(across) - col_prev(across))
            return carry

        lax.fori_loop(0, blocks, block, 0)


def combine_kernel(in_ref, out_ref):
    slabs, planes, _, width = in_ref.shape
    blank = jnp.zeros((R - 2, width), F32)
    for k in range(planes):
        for s in range(slabs):
            halo = jnp.concatenate(
                [in_ref[(s - 1) % slabs, k, 6:7], blank, in_ref[(s + 1) % slabs, k, 7:8]], axis=0
            )
            out_ref[k, R * s : R * (s + 1), :] = in_ref[s, k, 0:R] + halo


def shape(*dims):
    return jax.ShapeDtypeStruct(dims, F32)


def params():
    return pltpu.CompilerParams(vmem_limit_bytes=VMEM_LIMIT)


def block_of(*dims):
    return pl.BlockSpec((1,) + dims, lambda c: (c,) + (0,) * len(dims))


SCALARS = pl.BlockSpec(memory_space=pltpu.SMEM)
WHOLE = pl.BlockSpec(memory_space=pltpu.VMEM)


def on_device(potential, mixing, lens_weight, observed, noise_weight):
    groups = lax.axis_size("plane")
    slabs = lax.axis_size("slab")
    planes, rows, width = potential.shape
    assert rows == R * slabs and width % EDGE == 0
    columns = width * slabs
    tiles = width // EDGE
    group = lax.axis_index("plane")

    packed = pl.pallas_call(
        pack_kernel,
        out_shape=shape(slabs, planes, SUB, width),
        in_specs=[SCALARS, WHOLE],
        out_specs=WHOLE,
        compiler_params=params(),
        name="pack",
    )(lens_weight, potential)
    mix_all = lax.all_gather(mixing, "plane", axis=0, tiled=True)
    mix_line = lax.dynamic_slice(
        jnp.concatenate([jnp.ones(((groups - 1) * planes,), F32), mix_all]),
        (group * planes,),
        (groups * planes,),
    )
    strips = [lax.all_to_all(packed, "slab", split_axis=0, concat_axis=0, tiled=True)]
    up_route = [(i, i + 1) for i in range(groups - 1)]
    down_route = [(i + 1, i) for i in range(groups - 1)]
    for hop in range(groups - 1):
        strips.insert(0, lax.ppermute(strips[0], "plane", up_route))

    mid = block_of(planes, SUB, width)
    left = pl.BlockSpec(
        (1, planes, SUB, EDGE), lambda c: (lax.rem(c + slabs - 1, slabs), 0, 0, tiles - 1)
    )
    right = pl.BlockSpec((1, planes, SUB, EDGE), lambda c: (lax.rem(c + 1, slabs), 0, 0, 0))
    three_rows = pl.BlockSpec((planes, 3, R, width), lambda c: (0, 0, 0, c))
    two_rows = pl.BlockSpec((planes, 2, R, width), lambda c: (0, 0, 0, c))
    one_row = pl.BlockSpec((planes, R, width), lambda c: (0, 0, c))
    state = block_of(R, SUB, width)
    triple = block_of(3 * planes, SUB, width)
    quad = block_of(4 * planes, SUB, width)
    deflection, shear, matrices, states, sources, b = pl.pallas_call(
        functools.partial(forward_kernel, groups, planes),
        grid=(slabs,),
        out_shape=(
            shape(planes, 2, R, columns),
            shape(planes, 3, R, columns),
            shape(slabs, 3 * planes, SUB, width),
            shape(slabs, 4 * planes, SUB, width),
            shape(slabs, 3 * planes, SUB, width),
            shape(slabs, R, SUB, width),
        ),
        in_specs=[SCALARS] + [mid, left, right] * groups + [three_rows, one_row],
        out_specs=(two_rows, three_rows, triple, quad, triple, state),
        compiler_params=params(),
        name="forward",
    )(mix_line, *[x for strip in strips for x in (strip,) * 3], observed, noise_weight)

    incoming = lax.ppermute(b, "plane", down_route)
    for hop in range(groups - 2):
        outgoing = pl.pallas_call(
            functools.partial(carry_kernel, planes),
            grid=(slabs,),
            out_shape=shape(slabs, R, SUB, width),
            in_specs=[SCALARS, state, state, triple],
            out_specs=state,
            compiler_params=params(),
            name="carry",
        )(mixing, incoming, b, matrices)
        incoming = lax.ppermute(outgoing, "plane", down_route)

    partial = pl.pallas_call(
        functools.partial(gradient_kernel, planes),
        grid=(slabs,),
        out_shape=shape(slabs, planes, SUB, width),
        in_specs=[SCALARS, SCALARS, state, triple, triple, quad],
        out_specs=pl.BlockSpec((slabs, planes, SUB, width), lambda c: (0, 0, 0, 0)),
        scratch_shapes=[pltpu.VMEM((slabs, 3 * planes, SUB, width), F32)],
        compiler_params=params(),
        name="gradient",
    )(mixing, lens_weight, incoming, sources, matrices, states)
    returned = lax.all_to_all(partial, "slab", split_axis=0, concat_axis=0, tiled=True)
    potential_grad = pl.pallas_call(
        combine_kernel,
        out_shape=shape(planes, rows, width),
        in_specs=[WHOLE],
        out_specs=WHOLE,
        compiler_params=params(),
        name="combine",
    )(returned)
    return (deflection, shear, potential_grad)


def solution(mesh):
    placed = (
        P("plane", None, "slab"),
        P("plane"),
        P("plane"),
        P("plane", None, "slab", None),
        P("plane", "slab", None),
    )
    return jax.shard_map(
        on_device,
        mesh=mesh,
        in_specs=placed,
        out_specs=(
            P("plane", None, "slab", None),
            P("plane", None, "slab", None),
            P("plane", None, "slab"),
        ),
        check_vma=False,
    )
```

```python
import functools

import jax
import jax.numpy as jnp
from jax import lax
from jax.experimental import pallas as pl
from jax.experimental.pallas import tpu as pltpu
from jax.sharding import PartitionSpec as P

R = 6
SUB = 8
EDGE = 128
F32 = jnp.float32
VMEM_LIMIT = 32 * 1024 * 1024
CHUNKS = 4
SPAN = 4
MIX_LANE = 64


def pack_kernel(weight_ref, p_ref, out_ref):
    planes, rows, width = p_ref.shape
    for k in range(planes):
        w = weight_ref[k]
        for s in range(out_ref.shape[0]):
            before = (R * s - 1) % rows
            after = (R * (s + 1)) % rows
            strip = w * jnp.concatenate(
                [
                    p_ref[k, R * s : R * (s + 1), :],
                    p_ref[k, after : after + 1, :],
                    p_ref[k, before : before + 1, :],
                ],
                axis=0,
            )
            for t in range(width // EDGE):
                out_ref[s, t, k] = strip[:, EDGE * t : EDGE * (t + 1)]


def split_kernel(mix_ref, in_ref, *outs):
    tiles, planes = in_ref.shape[0:2]
    length = tiles // len(outs)
    lane = lax.broadcasted_iota(jnp.int32, (SUB, EDGE), 1)
    for c, out_ref in enumerate(outs):
        out_ref[0:length] = in_ref[length * c : length * (c + 1)]
    for k in range(planes):
        edge = jnp.where(lane == MIX_LANE, mix_ref[k] - 1.0, 0.0)
        for c in range(len(outs)):
            after = in_ref[(length * (c + 1)) % tiles, k]
            before = in_ref[(length * c - 1) % tiles, k]
            edge = jnp.where(lane == 2 * c, pltpu.roll(after, 2 * c, 1), edge)
            edge = jnp.where(lane == (2 * c - 1) % EDGE, pltpu.roll(before, 2 * c, 1), edge)
        outs[0][length, k] = edge


def row_up(x):
    return pltpu.roll(x, SUB - 1, 0)


def row_down(x):
    return pltpu.roll(x, 1, 0)


def col_prev(x):
    return pltpu.roll(x, 1, 1)[:, EDGE:-EDGE]


def col_next(x):
    return pltpu.roll(x, x.shape[1] - 1, 1)[:, EDGE:-EDGE]


def transposed_step(m0, m1, off, p, q, keep):
    new_p = [
        m0 * p[0] + off * p[2] + q[0],
        m0 * p[1] + off * p[3] + q[1],
        off * p[0] + m1 * p[2] + q[2],
        off * p[1] + m1 * p[3] + q[3],
    ]
    return (new_p, [keep * x for x in p])


def pack_state(out_ref, fields):
    for j in range(R):
        out_ref[0, j] = jnp.concatenate(
            [fields[j], fields[6][j : j + 1], fields[7][j : j + 1]], axis=0
        )


def unpack_state(in_ref):
    tiles = [in_ref[0, j] for j in range(R)]
    fields = [t[0:R] for t in tiles]
    fields.append(jnp.concatenate([t[6:7] for t in tiles], axis=0))
    fields.append(jnp.concatenate([t[7:8] for t in tiles], axis=0))
    return fields


def forward_kernel(groups, planes, chunk, length, *refs):
    strips = refs[: 2 * groups]
    obs_ref, noise_ref = refs[2 * groups : 2 * groups + 2]
    defl_ref, shear_ref, m_ref, a_ref, src_ref, b_ref = refs[-6:]
    step = pl.program_id(0)
    width = obs_ref.shape[-1]
    span = width // EDGE
    first = step * span
    at_start = first == 0
    at_end = first + span == length
    one = jnp.ones((SUB, width), F32)
    zero = jnp.zeros((SUB, width), F32)
    a = [one, zero, zero, one]
    a_before = a
    psi = jnp.zeros((SUB, width + 2 * EDGE), F32)
    psi_before = psi
    keeps = []
    for group in range(groups):
        strip_ref, edge_ref = strips[2 * group : 2 * group + 2]
        own = group == groups - 1
        for k in range(planes):
            edge = edge_ref[edge_ref.shape[0] - 1, k]
            excess = edge[:, MIX_LANE : MIX_LANE + 1]
            mix = 1.0 + excess
            beside = pltpu.roll(edge, (EDGE - 2 * chunk) % EDGE, 1)
            left = jnp.where(at_start, beside, strip_ref[jnp.maximum(first - 1, 0), k])
            right = jnp.where(at_end, beside, strip_ref[jnp.minimum(first + span, length - 1), k])
            tiles = [strip_ref[first + t, k] for t in range(span)]
            mid = jnp.concatenate(tiles, axis=1)
            ext = jnp.concatenate([left] + tiles + [right], axis=1)
            up = row_up(ext)
            down = row_down(ext)
            across = up - down
            twice = 2.0 * mid
            m0 = mix - ((up + down)[:, EDGE:-EDGE] - twice)
            m1 = mix - (col_next(ext) + col_prev(ext) - twice)
            off = 0.25 * (col_prev(across) - col_next(across))
            if own:
                m_ref[0, 3 * k] = m0
                m_ref[0, 3 * k + 1] = m1
                m_ref[0, 3 * k + 2] = off
                keeps.append(-excess[0:R])
                for j in range(4):
                    a_ref[0, 4 * k + j] = a[j]
            new_a = [
                m0 * a[0] + off * a[2] - excess * a_before[0],
                m0 * a[1] + off * a[3] - excess * a_before[1],
                off * a[0] + m1 * a[2] - excess * a_before[2],
                off * a[1] + m1 * a[3] - excess * a_before[3],
            ]
            a_before, a = (a, new_a)
            psi, psi_before = (mix * psi - excess * psi_before - ext, psi)
            if own:
                slope_rows = 0.5 * (row_up(psi) - row_down(psi))[:, EDGE:-EDGE]
                slope_cols = 0.5 * (col_next(psi) - col_prev(psi))
                defl_ref[k, 0] = slope_rows[0:R]
                defl_ref[k, 1] = slope_cols[0:R]
                shear = [
                    1.0 - 0.5 * (a[0] + a[3])[0:R],
                    0.5 * (a[3] - a[0])[0:R],
                    -0.5 * (a[1] + a[2])[0:R],
                ]
                noise = -0.5 * noise_ref[k]
                r = []
                for j in range(3):
                    shear_ref[k, j] = shear[j]
                    r.append(noise * (shear[j] - obs_ref[k, j]))
                src_ref[0, 3 * k, 0:R] = r[0] + r[1]
                src_ref[0, 3 * k + 1, 0:R] = r[2]
                src_ref[0, 3 * k + 2, 0:R] = r[0] - r[1]
    none = jnp.zeros((R, width), F32)
    p = [none] * 4
    q = [none] * 4
    for k in reversed(range(planes)):
        s0, s1, s3 = (src_ref[0, 3 * k + j, 0:R] for j in range(3))
        p = [p[0] + s0, p[1] + s1, p[2] + s1, p[3] + s3]
        m0, m1, off = (m_ref[0, 3 * k + j, 0:R] for j in range(3))
        p, q = transposed_step(m0, m1, off, p, q, keeps[k])
    pack_state(b_ref, p + q)


def carry_kernel(planes, mix_ref, in_ref, b_ref, m_ref, out_ref):
    fields = unpack_state(in_ref)
    p, q = (fields[0:4], fields[4:8])
    for k in reversed(range(planes)):
        m0, m1, off = (m_ref[0, 3 * k + j, 0:R] for j in range(3))
        p, q = transposed_step(m0, m1, off, p, q, 1.0 - mix_ref[k])
    pack_state(out_ref, p + q)
    out_ref[...] += b_ref[...]


def cotangent_kernel(planes, mix_ref, weight_ref, in_ref, src_ref, m_ref, a_ref, cot_ref):
    width = in_ref.shape[-1]
    fields = unpack_state(in_ref)
    p, q = (fields[0:4], fields[4:8])
    blank = jnp.zeros((SUB - R, width), F32)
    for k in reversed(range(planes)):
        s0, s1, s3 = (src_ref[0, 3 * k + j, 0:R] for j in range(3))
        p = [p[0] + s0, p[1] + s1, p[2] + s1, p[3] + s3]
        a = [a_ref[0, 4 * k + j, 0:R] for j in range(4)]
        w = -weight_ref[k]
        cots = [
            w * (p[0] * a[0] + p[1] * a[1]),
            w * (p[2] * a[2] + p[3] * a[3]),
            (0.25 * w) * (p[0] * a[2] + p[1] * a[3] + p[2] * a[0] + p[3] * a[1]),
        ]
        for j in range(3):
            cot_ref[0, 3 * k + j] = jnp.concatenate([cots[j], blank], axis=0)
        m0, m1, off = (m_ref[0, 3 * k + j, 0:R] for j in range(3))
        p, q = transposed_step(m0, m1, off, p, q, 1.0 - mix_ref[k])


def stencil_kernel(planes, *refs):
    cots, out_ref = (refs[:-1], refs[-1])
    out = out_ref.shape[-1]
    steps, width = (cots[0].shape[0], cots[0].shape[-1])
    blocks = len(cots) * steps

    def cot(block, field):
        return cots[block // steps].at[block % steps, field]

    for c in range(blocks):
        before = (c - 1) % blocks
        after = (c + 1) % blocks

        def ext(field):
            return jnp.concatenate(
                [
                    cot(before, field)[:, width - EDGE :],
                    cot(c, field)[...],
                    cot(after, field)[:, 0:EDGE],
                ],
                axis=1,
            )

        for k in range(planes):
            cot_rows = cot(c, 3 * k)[...]
            cot_cols = ext(3 * k + 1)
            cot_mixed = ext(3 * k + 2)
            across = row_up(cot_mixed) - row_down(cot_mixed)
            rows_part = row_up(cot_rows) + row_down(cot_rows) - 2.0 * cot_rows
            cols_part = col_next(cot_cols) + col_prev(cot_cols) - 2.0 * cot_cols[:, EDGE:-EDGE]
            grad = rows_part + cols_part + (col_next(across) - col_prev(across))
            for part in range(max(1, width // out)):
                place = c * width + part * out
                size = min(out, width)
                start = place % out
                out_ref[place // out, k, :, start : start + size] = grad[
                    :, part * out : part * out + size
                ]


def combine_kernel(in_ref, out_ref):
    slabs, planes, _, width = in_ref.shape
    blank = jnp.zeros((R - 2, width), F32)
    for k in range(planes):
        for s in range(slabs):
            halo = jnp.concatenate(
                [in_ref[(s - 1) % slabs, k, 6:7], blank, in_ref[(s + 1) % slabs, k, 7:8]], axis=0
            )
            out_ref[k, R * s : R * (s + 1), :] = in_ref[s, k, 0:R] + halo


def shape(*dims):
    return jax.ShapeDtypeStruct(dims, F32)


def params():
    return pltpu.CompilerParams(vmem_limit_bytes=VMEM_LIMIT)


def block_of(*dims):
    return pl.BlockSpec((1,) + dims, lambda c: (c,) + (0,) * len(dims))


SCALARS = pl.BlockSpec(memory_space=pltpu.SMEM)
WHOLE = pl.BlockSpec(memory_space=pltpu.VMEM)


def on_device(potential, mixing, lens_weight, observed, noise_weight):
    groups = lax.axis_size("plane")
    slabs = lax.axis_size("slab")
    planes, rows, width = potential.shape
    assert rows == R * slabs and width % EDGE == 0
    columns = width * slabs
    tiles = width // EDGE
    length = tiles * slabs // CHUNKS
    span = SPAN * EDGE
    steps = length // SPAN
    up_route = [(i, i + 1) for i in range(groups - 1)]
    down_route = [(i + 1, i) for i in range(groups - 1)]

    packed = pl.pallas_call(
        pack_kernel,
        out_shape=shape(slabs, tiles, planes, SUB, EDGE),
        in_specs=[SCALARS, WHOLE],
        out_specs=WHOLE,
        compiler_params=params(),
        name="pack",
    )(lens_weight, potential)
    own = lax.all_to_all(packed, "slab", split_axis=0, concat_axis=0, tiled=True)
    own = own.reshape(slabs * tiles, planes, SUB, EDGE)
    pieces = pl.pallas_call(
        split_kernel,
        out_shape=tuple(
            shape(length + (c == 0), planes, SUB, EDGE) for c in range(CHUNKS)
        ),
        in_specs=[SCALARS, WHOLE],
        out_specs=(WHOLE,) * CHUNKS,
        compiler_params=params(),
        name="split",
    )(mixing, own)
    strips = [[piece] for piece in pieces]
    for turn in range(CHUNKS + groups - 2):
        for c in range(CHUNKS):
            if 0 <= turn - c < groups - 1:
                strips[c].insert(0, lax.ppermute(strips[c][0], "plane", up_route))

    state = block_of(R, SUB, span)
    triple = block_of(3 * planes, SUB, span)
    quad = block_of(4 * planes, SUB, span)
    kept = pl.BlockSpec(memory_space=pl.ANY)

    def columns_of(c, *dims):
        return pl.BlockSpec(dims + (span,), lambda i: (0,) * len(dims) + (c * steps + i,))

    deflection, shear = (None, None)
    work = []
    for c in range(CHUNKS):
        operands = [x for pair in zip(strips[c], strips[0]) for x in pair]
        operands += [observed, noise_weight]
        specs = [WHOLE] * (2 * groups) + [columns_of(c, planes, 3, R), columns_of(c, planes, R)]
        aliases = {}
        if c > 0:
            aliases = {len(operands): 0, len(operands) + 1: 1}
            operands += [deflection, shear]
            specs += [kept, kept]
        deflection, shear, *held = pl.pallas_call(
            functools.partial(forward_kernel, groups, planes, c, length),
            grid=(steps,),
            out_shape=(
                shape(planes, 2, R, columns),
                shape(planes, 3, R, columns),
                shape(steps, 3 * planes, SUB, span),
                shape(steps, 4 * planes, SUB, span),
                shape(steps, 3 * planes, SUB, span),
                shape(steps, R, SUB, span),
            ),
            in_specs=specs,
            out_specs=(
                columns_of(c, planes, 2, R),
                columns_of(c, planes, 3, R),
                triple,
                quad,
                triple,
                state,
            ),
            input_output_aliases=aliases,
            compiler_params=params(),
            name="forward",
        )(*operands)
        work.append(held)

    cots = []
    for matrices, states, sources, b in work:
        incoming = lax.ppermute(b, "plane", down_route)
        for hop in range(groups - 2):
            outgoing = pl.pallas_call(
                functools.partial(carry_kernel, planes),
                grid=(steps,),
                out_shape=shape(steps, R, SUB, span),
                in_specs=[SCALARS, state, state, triple],
                out_specs=state,
                compiler_params=params(),
                name="carry",
            )(mixing, incoming, b, matrices)
            incoming = lax.ppermute(outgoing, "plane", down_route)
        cots.append(
            pl.pallas_call(
                functools.partial(cotangent_kernel, planes),
                grid=(steps,),
                out_shape=shape(steps, 3 * planes, SUB, span),
                in_specs=[SCALARS, SCALARS, state, triple, triple, quad],
                out_specs=triple,
                compiler_params=params(),
                name="cotangent",
            )(mixing, lens_weight, incoming, sources, matrices, states)
        )

    partial = pl.pallas_call(
        functools.partial(stencil_kernel, planes),
        out_shape=shape(slabs, planes, SUB, width),
        in_specs=[WHOLE] * CHUNKS,
        out_specs=WHOLE,
        compiler_params=params(),
        name="stencil",
    )(*cots)
    returned = lax.all_to_all(partial, "slab", split_axis=0, concat_axis=0, tiled=True)
    potential_grad = pl.pallas_call(
        combine_kernel,
        out_shape=shape(planes, rows, width),
        in_specs=[WHOLE],
        out_specs=WHOLE,
        compiler_params=params(),
        name="combine",
    )(returned)
    return (deflection, shear, potential_grad)


def solution(mesh):
    placed = (
        P("plane", None, "slab"),
        P("plane"),
        P("plane"),
        P("plane", None, "slab", None),
        P("plane", "slab", None),
    )
    return jax.shard_map(
        on_device,
        mesh=mesh,
        in_specs=placed,
        out_specs=(
            P("plane", None, "slab", None),
            P("plane", None, "slab", None),
            P("plane", None, "slab"),
        ),
        check_vma=False,
    )
```

```python
import functools

import jax
import jax.numpy as jnp
from jax import lax
from jax.experimental import pallas as pl
from jax.experimental.pallas import tpu as pltpu
from jax.sharding import PartitionSpec as P

R = 6
SUB = 8
EDGE = 128
F32 = jnp.float32
VMEM_LIMIT = 32 * 1024 * 1024
CHUNKS = 4
SPAN = 4
MIX_LANE = 64


def pack_kernel(weight_ref, p_ref, out_ref):
    planes, rows, width = p_ref.shape
    for k in range(planes):
        w = weight_ref[k]
        for s in range(out_ref.shape[0]):
            before = (R * s - 1) % rows
            after = (R * (s + 1)) % rows
            strip = w * jnp.concatenate(
                [
                    p_ref[k, R * s : R * (s + 1), :],
                    p_ref[k, after : after + 1, :],
                    p_ref[k, before : before + 1, :],
                ],
                axis=0,
            )
            for t in range(width // EDGE):
                out_ref[s, t, k] = strip[:, EDGE * t : EDGE * (t + 1)]


def split_kernel(mix_ref, in_ref, *outs):
    tiles, planes = in_ref.shape[0:2]
    length = tiles // len(outs)
    lane = lax.broadcasted_iota(jnp.int32, (SUB, EDGE), 1)
    for c, out_ref in enumerate(outs):
        out_ref[0:length] = in_ref[length * c : length * (c + 1)]
    for k in range(planes):
        edge = jnp.where(lane == MIX_LANE, mix_ref[k] - 1.0, 0.0)
        for c in range(len(outs)):
            after = in_ref[(length * (c + 1)) % tiles, k]
            before = in_ref[(length * c - 1) % tiles, k]
            edge = jnp.where(lane == 2 * c, pltpu.roll(after, 2 * c, 1), edge)
            edge = jnp.where(lane == (2 * c - 1) % EDGE, pltpu.roll(before, 2 * c, 1), edge)
        outs[0][length, k] = edge


def row_up(x):
    return pltpu.roll(x, SUB - 1, 0)


def row_down(x):
    return pltpu.roll(x, 1, 0)


def col_prev(x):
    return pltpu.roll(x, 1, 1)[:, EDGE:-EDGE]


def col_next(x):
    return pltpu.roll(x, x.shape[1] - 1, 1)[:, EDGE:-EDGE]


def transposed_step(m0, m1, off, p, q, keep):
    new_p = [
        m0 * p[0] + off * p[2] + q[0],
        m0 * p[1] + off * p[3] + q[1],
        off * p[0] + m1 * p[2] + q[2],
        off * p[1] + m1 * p[3] + q[3],
    ]
    return (new_p, [keep * x for x in p])


def pack_state(out_ref, fields):
    for j in range(R):
        out_ref[0, j] = jnp.concatenate(
            [fields[j], fields[6][j : j + 1], fields[7][j : j + 1]], axis=0
        )


def unpack_state(arrived):
    tiles = [sum(in_ref[0, j] for in_ref in arrived) for j in range(R)]
    fields = [t[0:R] for t in tiles]
    fields.append(jnp.concatenate([t[6:7] for t in tiles], axis=0))
    fields.append(jnp.concatenate([t[7:8] for t in tiles], axis=0))
    return fields


def forward_kernel(groups, planes, chunk, length, *refs):
    strips = refs[: 2 * groups]
    obs_ref, noise_ref = refs[2 * groups : 2 * groups + 2]
    map_ref, m_ref, a_ref, src_ref, b_ref = refs[-5:]
    step = pl.program_id(0)
    width = obs_ref.shape[-1]
    span = width // EDGE
    first = step * span
    at_start = first == 0
    at_end = first + span == length
    one = jnp.ones((SUB, width), F32)
    zero = jnp.zeros((SUB, width), F32)
    a = [one, zero, zero, one]
    a_before = a
    psi = jnp.zeros((SUB, width + 2 * EDGE), F32)
    psi_before = psi
    keeps = []
    for group in range(groups):
        strip_ref, edge_ref = strips[2 * group : 2 * group + 2]
        own = group == groups - 1
        for k in range(planes):
            edge = edge_ref[edge_ref.shape[0] - 1, k]
            excess = edge[:, MIX_LANE : MIX_LANE + 1]
            mix = 1.0 + excess
            beside = pltpu.roll(edge, (EDGE - 2 * chunk) % EDGE, 1)
            left = jnp.where(at_start, beside, strip_ref[jnp.maximum(first - 1, 0), k])
            right = jnp.where(at_end, beside, strip_ref[jnp.minimum(first + span, length - 1), k])
            tiles = [strip_ref[first + t, k] for t in range(span)]
            mid = jnp.concatenate(tiles, axis=1)
            ext = jnp.concatenate([left] + tiles + [right], axis=1)
            up = row_up(ext)
            down = row_down(ext)
            across = up - down
            twice = 2.0 * mid
            m0 = mix - ((up + down)[:, EDGE:-EDGE] - twice)
            m1 = mix - (col_next(ext) + col_prev(ext) - twice)
            off = 0.25 * (col_prev(across) - col_next(across))
            if own:
                m_ref[0, 3 * k] = m0
                m_ref[0, 3 * k + 1] = m1
                m_ref[0, 3 * k + 2] = off
                keeps.append(-excess[0:R])
                for j in range(4):
                    a_ref[0, 4 * k + j] = a[j]
            new_a = [
                m0 * a[0] + off * a[2] - excess * a_before[0],
                m0 * a[1] + off * a[3] - excess * a_before[1],
                off * a[0] + m1 * a[2] - excess * a_before[2],
                off * a[1] + m1 * a[3] - excess * a_before[3],
            ]
            a_before, a = (a, new_a)
            psi, psi_before = (mix * psi - excess * psi_before - ext, psi)
            if own:
                slope_rows = 0.5 * (row_up(psi) - row_down(psi))[:, EDGE:-EDGE]
                slope_cols = 0.5 * (col_next(psi) - col_prev(psi))
                shear = [
                    1.0 - 0.5 * (a[0] + a[3]),
                    0.5 * (a[3] - a[0]),
                    -0.5 * (a[1] + a[2]),
                ]
                for j, field in enumerate([slope_rows, slope_cols] + shear):
                    map_ref[0, 5 * k + j] = field
                noise = -0.5 * noise_ref[k]
                r = [noise * (shear[j][0:R] - obs_ref[k, j]) for j in range(3)]
                src_ref[0, 3 * k, 0:R] = r[0] + r[1]
                src_ref[0, 3 * k + 1, 0:R] = r[2]
                src_ref[0, 3 * k + 2, 0:R] = r[0] - r[1]
    none = jnp.zeros((R, width), F32)
    p = [none] * 4
    q = [none] * 4
    for k in reversed(range(planes)):
        s0, s1, s3 = (src_ref[0, 3 * k + j, 0:R] for j in range(3))
        p = [p[0] + s0, p[1] + s1, p[2] + s1, p[3] + s3]
        m0, m1, off = (m_ref[0, 3 * k + j, 0:R] for j in range(3))
        p, q = transposed_step(m0, m1, off, p, q, keeps[k])
    pack_state(b_ref, p + q)


def assemble_kernel(*refs):
    maps = refs[:-2]
    defl_ref, shear_ref = refs[-2:]
    steps, width = (maps[0].shape[0], maps[0].shape[-1])
    for c, map_ref in enumerate(maps):
        for i in range(steps):
            start = (c * steps + i) * width
            for k in range(defl_ref.shape[0]):
                for j in range(2):
                    defl_ref[k, j, :, start : start + width] = map_ref[i, 5 * k + j, 0:R]
                for j in range(3):
                    shear_ref[k, j, :, start : start + width] = map_ref[i, 5 * k + 2 + j, 0:R]


def carry_kernel(planes, mix_ref, in_ref, b_ref, m_ref, out_ref):
    fields = unpack_state([in_ref])
    p, q = (fields[0:4], fields[4:8])
    for k in reversed(range(planes)):
        m0, m1, off = (m_ref[0, 3 * k + j, 0:R] for j in range(3))
        p, q = transposed_step(m0, m1, off, p, q, 1.0 - mix_ref[k])
    pack_state(out_ref, p + q)
    out_ref[...] += b_ref[...]


def cotangent_kernel(planes, mix_ref, weight_ref, src_ref, m_ref, a_ref, *refs):
    arrived, cot_ref = (refs[:-1], refs[-1])
    width = cot_ref.shape[-1]
    fields = unpack_state(arrived)
    p, q = (fields[0:4], fields[4:8])
    blank = jnp.zeros((SUB - R, width), F32)
    for k in reversed(range(planes)):
        s0, s1, s3 = (src_ref[0, 3 * k + j, 0:R] for j in range(3))
        p = [p[0] + s0, p[1] + s1, p[2] + s1, p[3] + s3]
        a = [a_ref[0, 4 * k + j, 0:R] for j in range(4)]
        w = -weight_ref[k]
        cots = [
            w * (p[0] * a[0] + p[1] * a[1]),
            w * (p[2] * a[2] + p[3] * a[3]),
            (0.25 * w) * (p[0] * a[2] + p[1] * a[3] + p[2] * a[0] + p[3] * a[1]),
        ]
        for j in range(3):
            cot_ref[0, 3 * k + j] = jnp.concatenate([cots[j], blank], axis=0)
        m0, m1, off = (m_ref[0, 3 * k + j, 0:R] for j in range(3))
        p, q = transposed_step(m0, m1, off, p, q, 1.0 - mix_ref[k])


def stencil_kernel(planes, *refs):
    cots, out_ref = (refs[:-1], refs[-1])
    out = out_ref.shape[-1]
    steps, width = (cots[0].shape[0], cots[0].shape[-1])
    blocks = len(cots) * steps

    def cot(block, field):
        return cots[block // steps].at[block % steps, field]

    for c in range(blocks):
        before = (c - 1) % blocks
        after = (c + 1) % blocks

        def ext(field):
            return jnp.concatenate(
                [
                    cot(before, field)[:, width - EDGE :],
                    cot(c, field)[...],
                    cot(after, field)[:, 0:EDGE],
                ],
                axis=1,
            )

        for k in range(planes):
            cot_rows = cot(c, 3 * k)[...]
            cot_cols = ext(3 * k + 1)
            cot_mixed = ext(3 * k + 2)
            across = row_up(cot_mixed) - row_down(cot_mixed)
            rows_part = row_up(cot_rows) + row_down(cot_rows) - 2.0 * cot_rows
            cols_part = col_next(cot_cols) + col_prev(cot_cols) - 2.0 * cot_cols[:, EDGE:-EDGE]
            grad = rows_part + cols_part + (col_next(across) - col_prev(across))
            for part in range(max(1, width // out)):
                place = c * width + part * out
                size = min(out, width)
                start = place % out
                out_ref[place // out, k, :, start : start + size] = grad[
                    :, part * out : part * out + size
                ]


def combine_kernel(in_ref, out_ref):
    slabs, planes, _, width = in_ref.shape
    blank = jnp.zeros((R - 2, width), F32)
    for k in range(planes):
        for s in range(slabs):
            halo = jnp.concatenate(
                [in_ref[(s - 1) % slabs, k, 6:7], blank, in_ref[(s + 1) % slabs, k, 7:8]], axis=0
            )
            out_ref[k, R * s : R * (s + 1), :] = in_ref[s, k, 0:R] + halo


def shape(*dims):
    return jax.ShapeDtypeStruct(dims, F32)


def params():
    return pltpu.CompilerParams(vmem_limit_bytes=VMEM_LIMIT)


def block_of(*dims):
    return pl.BlockSpec((1,) + dims, lambda c: (c,) + (0,) * len(dims))


SCALARS = pl.BlockSpec(memory_space=pltpu.SMEM)
WHOLE = pl.BlockSpec(memory_space=pltpu.VMEM)


def on_device(potential, mixing, lens_weight, observed, noise_weight):
    groups = lax.axis_size("plane")
    slabs = lax.axis_size("slab")
    planes, rows, width = potential.shape
    assert rows == R * slabs and width % EDGE == 0
    columns = width * slabs
    tiles = width // EDGE
    length = tiles * slabs // CHUNKS
    span = SPAN * EDGE
    steps = length // SPAN

    def climb(x, hop):
        return lax.ppermute(x, "plane", [(i, i + 1) for i in range(hop, groups - 1)])

    def descend(x, hop):
        return lax.ppermute(x, "plane", [(groups - 1 - hop, groups - 2 - hop)])

    packed = pl.pallas_call(
        pack_kernel,
        out_shape=shape(slabs, tiles, planes, SUB, EDGE),
        in_specs=[SCALARS, WHOLE],
        out_specs=WHOLE,
        compiler_params=params(),
        name="pack",
    )(lens_weight, potential)
    own = lax.all_to_all(packed, "slab", split_axis=0, concat_axis=0, tiled=True)
    own = own.reshape(slabs * tiles, planes, SUB, EDGE)
    pieces = pl.pallas_call(
        split_kernel,
        out_shape=tuple(
            shape(length + (c == 0), planes, SUB, EDGE) for c in range(CHUNKS)
        ),
        in_specs=[SCALARS, WHOLE],
        out_specs=(WHOLE,) * CHUNKS,
        compiler_params=params(),
        name="split",
    )(mixing, own)
    strips = [[piece] for piece in pieces]
    for turn in range(CHUNKS + groups - 2):
        for c in range(CHUNKS):
            if 0 <= turn - c < groups - 1:
                strips[c].insert(0, climb(strips[c][0], turn - c))

    state = block_of(R, SUB, span)
    triple = block_of(3 * planes, SUB, span)
    quad = block_of(4 * planes, SUB, span)
    quint = block_of(5 * planes, SUB, span)
    maps = []
    work = []
    for c in range(CHUNKS):

        def columns_of(*dims, at=c * steps):
            return pl.BlockSpec(dims + (span,), lambda i: (0,) * len(dims) + (at + i,))

        map_piece, *held = pl.pallas_call(
            functools.partial(forward_kernel, groups, planes, c, length),
            grid=(steps,),
            out_shape=(
                shape(steps, 5 * planes, SUB, span),
                shape(steps, 3 * planes, SUB, span),
                shape(steps, 4 * planes, SUB, span),
                shape(steps, 3 * planes, SUB, span),
                shape(steps, R, SUB, span),
            ),
            in_specs=[WHOLE] * (2 * groups) + [columns_of(planes, 3, R), columns_of(planes, R)],
            out_specs=(quint, triple, quad, triple, state),
            compiler_params=params(),
            name="forward",
        )(*[x for pair in zip(strips[c], strips[0]) for x in pair], observed, noise_weight)
        maps.append(map_piece)
        work.append(held)

    cots = []
    for matrices, states, sources, b in work:
        arrived = [descend(b, 0)]
        for hop in range(1, groups - 1):
            outgoing = pl.pallas_call(
                functools.partial(carry_kernel, planes),
                grid=(steps,),
                out_shape=shape(steps, R, SUB, span),
                in_specs=[SCALARS, state, state, triple],
                out_specs=state,
                compiler_params=params(),
                name="carry",
            )(mixing, arrived[-1], b, matrices)
            arrived.append(descend(outgoing, hop))
        cots.append(
            pl.pallas_call(
                functools.partial(cotangent_kernel, planes),
                grid=(steps,),
                out_shape=shape(steps, 3 * planes, SUB, span),
                in_specs=[SCALARS, SCALARS, triple, triple, quad] + [state] * (groups - 1),
                out_specs=triple,
                compiler_params=params(),
                name="cotangent",
            )(mixing, lens_weight, sources, matrices, states, *arrived)
        )

    partial = pl.pallas_call(
        functools.partial(stencil_kernel, planes),
        out_shape=shape(slabs, planes, SUB, width),
        in_specs=[WHOLE] * CHUNKS,
        out_specs=WHOLE,
        compiler_params=params(),
        name="stencil",
    )(*cots)
    returned = lax.all_to_all(partial, "slab", split_axis=0, concat_axis=0, tiled=True)
    deflection, shear = pl.pallas_call(
        assemble_kernel,
        out_shape=(shape(planes, 2, R, columns), shape(planes, 3, R, columns)),
        in_specs=[WHOLE] * CHUNKS,
        out_specs=(WHOLE, WHOLE),
        compiler_params=params(),
        name="assemble",
    )(*maps)
    potential_grad = pl.pallas_call(
        combine_kernel,
        out_shape=shape(planes, rows, width),
        in_specs=[WHOLE],
        out_specs=WHOLE,
        compiler_params=params(),
        name="combine",
    )(returned)
    return (deflection, shear, potential_grad)


def solution(mesh):
    placed = (
        P("plane", None, "slab"),
        P("plane"),
        P("plane"),
        P("plane", None, "slab", None),
        P("plane", "slab", None),
    )
    return jax.shard_map(
        on_device,
        mesh=mesh,
        in_specs=placed,
        out_specs=(
            P("plane", None, "slab", None),
            P("plane", None, "slab", None),
            P("plane", None, "slab"),
        ),
        check_vma=False,
    )
```

```python
import functools

import jax
import jax.numpy as jnp
from jax import lax
from jax.experimental import pallas as pl
from jax.experimental.pallas import tpu as pltpu
from jax.sharding import PartitionSpec as P

R = 6
SUB = 8
EDGE = 128
F32 = jnp.float32
VMEM_LIMIT = 32 * 1024 * 1024
CHUNKS = 4
SPAN = 4
MIX_LANE = 64


def write_strips(column, k, out_ref):
    rows, width = column.shape
    for s in range(out_ref.shape[0]):
        before = (R * s - 1) % rows
        after = (R * (s + 1)) % rows
        strip = jnp.concatenate(
            [
                column[R * s : R * (s + 1)],
                column[after : after + 1],
                column[before : before + 1],
            ],
            axis=0,
        )
        for t in range(width // EDGE):
            out_ref[s, t, k] = strip[:, EDGE * t : EDGE * (t + 1)]


def pack_kernel(weight_ref, mix_ref, p_ref, out_ref, column_ref):
    planes, rows, width = p_ref.shape
    for k in range(planes):
        column = weight_ref[k] * p_ref[k]
        column_ref[k, 0:rows] = column
        column_ref[k, rows:] = jnp.full((SUB, width), mix_ref[k] - 1.0, F32)
        write_strips(column, k, out_ref)


def repack_kernel(column_ref, out_ref):
    for k in range(column_ref.shape[0]):
        write_strips(column_ref[k, 0 : column_ref.shape[1] - SUB], k, out_ref)


def split_kernel(column_ref, in_ref, *outs):
    tiles, planes = in_ref.shape[0:2]
    length = tiles // len(outs)
    lane = lax.broadcasted_iota(jnp.int32, (SUB, EDGE), 1)
    for c, out_ref in enumerate(outs):
        out_ref[0:length] = in_ref[length * c : length * (c + 1)]
    for k in range(planes):
        edge = jnp.where(lane == MIX_LANE, column_ref[k, column_ref.shape[1] - SUB :, 0:EDGE], 0.0)
        for c in range(len(outs)):
            after = in_ref[(length * (c + 1)) % tiles, k]
            before = in_ref[(length * c - 1) % tiles, k]
            edge = jnp.where(lane == 2 * c, pltpu.roll(after, 2 * c, 1), edge)
            edge = jnp.where(lane == (2 * c - 1) % EDGE, pltpu.roll(before, 2 * c, 1), edge)
        outs[0][length, k] = edge


def edges_kernel(*refs):
    strips = refs[:-2]
    beside_ref, excess_ref = refs[-2:]
    for group, strip_ref in enumerate(strips):
        planes = strip_ref.shape[1]
        for k in range(planes):
            edge = strip_ref[strip_ref.shape[0] - 1, k]
            at = group * planes + k
            excess_ref[at] = jnp.broadcast_to(edge[:, MIX_LANE : MIX_LANE + 1], edge.shape)
            for c in range(CHUNKS):
                beside_ref[c, at] = pltpu.roll(edge, (EDGE - 2 * c) % EDGE, 1)


def row_up(x):
    return pltpu.roll(x, SUB - 1, 0)


def row_down(x):
    return pltpu.roll(x, 1, 0)


def col_prev(x):
    return pltpu.roll(x, 1, 1)[:, EDGE:-EDGE]


def col_next(x):
    return pltpu.roll(x, x.shape[1] - 1, 1)[:, EDGE:-EDGE]


def transposed_step(m0, m1, off, p, q, keep):
    new_p = [
        m0 * p[0] + off * p[2] + q[0],
        m0 * p[1] + off * p[3] + q[1],
        off * p[0] + m1 * p[2] + q[2],
        off * p[1] + m1 * p[3] + q[3],
    ]
    return (new_p, [keep * x for x in p])


def pack_state(out_ref, fields):
    for j in range(R):
        out_ref[0, j] = jnp.concatenate(
            [fields[j], fields[6][j : j + 1], fields[7][j : j + 1]], axis=0
        )


def unpack_state(arrived):
    tiles = [sum(in_ref[0, j] for in_ref in arrived) for j in range(R)]
    fields = [t[0:R] for t in tiles]
    fields.append(jnp.concatenate([t[6:7] for t in tiles], axis=0))
    fields.append(jnp.concatenate([t[7:8] for t in tiles], axis=0))
    return fields


def forward_kernel(groups, planes, chunk, length, *refs):
    strips = refs[:groups]
    beside_ref, excess_ref, obs_ref, noise_ref = refs[groups : groups + 4]
    map_ref, m_ref, a_ref, src_ref, b_ref = refs[-5:]
    step = pl.program_id(0)
    width = obs_ref.shape[-1]
    span = width // EDGE
    first = step * span
    at_start = first == 0
    at_end = first + span == length
    one = jnp.ones((SUB, width), F32)
    zero = jnp.zeros((SUB, width), F32)
    a = [one, zero, zero, one]
    a_before = a
    psi = jnp.zeros((SUB, width + 2 * EDGE), F32)
    psi_before = psi
    keeps = []
    for group in range(groups):
        strip_ref = strips[group]
        own = group == groups - 1
        for k in range(planes):
            beside = beside_ref[chunk, group * planes + k]
            excess_tile = excess_ref[group * planes + k]
            excess_ext = jnp.concatenate([excess_tile] * (span + 2), axis=1)
            excess = excess_ext[:, EDGE:-EDGE]
            mix_ext = jnp.concatenate([1.0 + excess_tile] * (span + 2), axis=1)
            mix = mix_ext[:, EDGE:-EDGE]
            left = jnp.where(at_start, beside, strip_ref[jnp.maximum(first - 1, 0), k])
            right = jnp.where(at_end, beside, strip_ref[jnp.minimum(first + span, length - 1), k])
            tiles = [strip_ref[first + t, k] for t in range(span)]
            mid = jnp.concatenate(tiles, axis=1)
            ext = jnp.concatenate([left] + tiles + [right], axis=1)
            up = row_up(ext)
            down = row_down(ext)
            across = up - down
            twice = 2.0 * mid
            m0 = mix - ((up + down)[:, EDGE:-EDGE] - twice)
            m1 = mix - (col_next(ext) + col_prev(ext) - twice)
            off = 0.25 * (col_prev(across) - col_next(across))
            if own:
                m_ref[0, 3 * k] = m0
                m_ref[0, 3 * k + 1] = m1
                m_ref[0, 3 * k + 2] = off
                keeps.append(-excess[0:R])
                for j in range(4):
                    a_ref[0, 4 * k + j] = a[j]
            new_a = [
                m0 * a[0] + off * a[2] - excess * a_before[0],
                m0 * a[1] + off * a[3] - excess * a_before[1],
                off * a[0] + m1 * a[2] - excess * a_before[2],
                off * a[1] + m1 * a[3] - excess * a_before[3],
            ]
            a_before, a = (a, new_a)
            psi, psi_before = (mix_ext * psi - excess_ext * psi_before - ext, psi)
            if own:
                slope_rows = 0.5 * (row_up(psi) - row_down(psi))[:, EDGE:-EDGE]
                slope_cols = 0.5 * (col_next(psi) - col_prev(psi))
                shear = [
                    1.0 - 0.5 * (a[0] + a[3]),
                    0.5 * (a[3] - a[0]),
                    -0.5 * (a[1] + a[2]),
                ]
                for j, field in enumerate([slope_rows, slope_cols] + shear):
                    map_ref[0, 5 * k + j] = field
                noise = -0.5 * noise_ref[k]
                r = [noise * (shear[j][0:R] - obs_ref[k, j]) for j in range(3)]
                src_ref[0, 3 * k, 0:R] = r[0] + r[1]
                src_ref[0, 3 * k + 1, 0:R] = r[2]
                src_ref[0, 3 * k + 2, 0:R] = r[0] - r[1]
    none = jnp.zeros((R, width), F32)
    p = [none] * 4
    q = [none] * 4
    for k in reversed(range(planes)):
        s0, s1, s3 = (src_ref[0, 3 * k + j, 0:R] for j in range(3))
        p = [p[0] + s0, p[1] + s1, p[2] + s1, p[3] + s3]
        m0, m1, off = (m_ref[0, 3 * k + j, 0:R] for j in range(3))
        p, q = transposed_step(m0, m1, off, p, q, keeps[k])
    pack_state(b_ref, p + q)


def assemble_kernel(*refs):
    maps = refs[:-2]
    defl_ref, shear_ref = refs[-2:]
    steps, width = (maps[0].shape[0], maps[0].shape[-1])
    for c, map_ref in enumerate(maps):
        for i in range(steps):
            start = (c * steps + i) * width
            for k in range(defl_ref.shape[0]):
                for j in range(2):
                    defl_ref[k, j, :, start : start + width] = map_ref[i, 5 * k + j, 0:R]
                for j in range(3):
                    shear_ref[k, j, :, start : start + width] = map_ref[i, 5 * k + 2 + j, 0:R]


def carry_kernel(planes, mix_ref, in_ref, b_ref, m_ref, out_ref):
    fields = unpack_state([in_ref])
    p, q = (fields[0:4], fields[4:8])
    for k in reversed(range(planes)):
        m0, m1, off = (m_ref[0, 3 * k + j, 0:R] for j in range(3))
        p, q = transposed_step(m0, m1, off, p, q, 1.0 - mix_ref[k])
    pack_state(out_ref, p + q)
    out_ref[...] += b_ref[...]


def cotangent_kernel(planes, mix_ref, weight_ref, src_ref, m_ref, a_ref, *refs):
    arrived, cot_ref = (refs[:-1], refs[-1])
    width = cot_ref.shape[-1]
    fields = unpack_state(arrived)
    p, q = (fields[0:4], fields[4:8])
    blank = jnp.zeros((SUB - R, width), F32)
    for k in reversed(range(planes)):
        s0, s1, s3 = (src_ref[0, 3 * k + j, 0:R] for j in range(3))
        p = [p[0] + s0, p[1] + s1, p[2] + s1, p[3] + s3]
        a = [a_ref[0, 4 * k + j, 0:R] for j in range(4)]
        w = -weight_ref[k]
        cots = [
            w * (p[0] * a[0] + p[1] * a[1]),
            w * (p[2] * a[2] + p[3] * a[3]),
            (0.25 * w) * (p[0] * a[2] + p[1] * a[3] + p[2] * a[0] + p[3] * a[1]),
        ]
        for j in range(3):
            cot_ref[0, 3 * k + j] = jnp.concatenate([cots[j], blank], axis=0)
        m0, m1, off = (m_ref[0, 3 * k + j, 0:R] for j in range(3))
        p, q = transposed_step(m0, m1, off, p, q, 1.0 - mix_ref[k])


def stencil_kernel(planes, *refs):
    cots, out_ref = (refs[:-1], refs[-1])
    out = out_ref.shape[-1]
    steps, width = (cots[0].shape[0], cots[0].shape[-1])
    blocks = len(cots) * steps

    def cot(block, field):
        return cots[block // steps].at[block % steps, field]

    for c in range(blocks):
        before = (c - 1) % blocks
        after = (c + 1) % blocks

        def ext(field):
            return jnp.concatenate(
                [
                    cot(before, field)[:, width - EDGE :],
                    cot(c, field)[...],
                    cot(after, field)[:, 0:EDGE],
                ],
                axis=1,
            )

        for k in range(planes):
            cot_rows = cot(c, 3 * k)[...]
            cot_cols = ext(3 * k + 1)
            cot_mixed = ext(3 * k + 2)
            across = row_up(cot_mixed) - row_down(cot_mixed)
            rows_part = row_up(cot_rows) + row_down(cot_rows) - 2.0 * cot_rows
            cols_part = col_next(cot_cols) + col_prev(cot_cols) - 2.0 * cot_cols[:, EDGE:-EDGE]
            grad = rows_part + cols_part + (col_next(across) - col_prev(across))
            for part in range(max(1, width // out)):
                place = c * width + part * out
                size = min(out, width)
                start = place % out
                out_ref[place // out, k, :, start : start + size] = grad[
                    :, part * out : part * out + size
                ]


def combine_kernel(in_ref, out_ref):
    slabs, planes, _, width = in_ref.shape
    blank = jnp.zeros((R - 2, width), F32)
    for k in range(planes):
        for s in range(slabs):
            halo = jnp.concatenate(
                [in_ref[(s - 1) % slabs, k, 6:7], blank, in_ref[(s + 1) % slabs, k, 7:8]], axis=0
            )
            out_ref[k, R * s : R * (s + 1), :] = in_ref[s, k, 0:R] + halo


def shape(*dims):
    return jax.ShapeDtypeStruct(dims, F32)


def params():
    return pltpu.CompilerParams(vmem_limit_bytes=VMEM_LIMIT)


def block_of(*dims):
    return pl.BlockSpec((1,) + dims, lambda c: (c,) + (0,) * len(dims))


SCALARS = pl.BlockSpec(memory_space=pltpu.SMEM)
WHOLE = pl.BlockSpec(memory_space=pltpu.VMEM)


def on_device(potential, mixing, lens_weight, observed, noise_weight):
    groups = lax.axis_size("plane")
    slabs = lax.axis_size("slab")
    planes, rows, width = potential.shape
    assert rows == R * slabs and width % EDGE == 0
    columns = width * slabs
    tiles = width // EDGE
    length = tiles * slabs // CHUNKS
    span = SPAN * EDGE
    steps = length // SPAN

    def climb(x, hop):
        return lax.ppermute(x, "plane", [(i, i + 1) for i in range(hop, groups - 1)])

    def descend(x, hop):
        return lax.ppermute(x, "plane", [(groups - 1 - hop, groups - 2 - hop)])

    packed_shape = shape(slabs, tiles, planes, SUB, EDGE)
    packed, column = pl.pallas_call(
        pack_kernel,
        out_shape=(packed_shape, shape(planes, rows + SUB, width)),
        in_specs=[SCALARS, SCALARS, WHOLE],
        out_specs=(WHOLE, WHOLE),
        compiler_params=params(),
        name="pack",
    )(lens_weight, mixing, potential)

    def to_rows(packed, column):
        strip = lax.all_to_all(packed, "slab", split_axis=0, concat_axis=0, tiled=True)
        return pl.pallas_call(
            split_kernel,
            out_shape=tuple(
                shape(length + (c == 0), planes, SUB, EDGE) for c in range(CHUNKS)
            ),
            in_specs=[WHOLE, WHOLE],
            out_specs=(WHOLE,) * CHUNKS,
            compiler_params=params(),
            name="split",
        )(column, strip.reshape(slabs * tiles, planes, SUB, EDGE))

    column_before = climb(column, 0)
    pieces = to_rows(packed, column)
    two_up = [(i, i + 2) for i in range(groups - 2)]
    further = [[lax.ppermute(piece, "plane", two_up)] for piece in pieces]
    packed_before = pl.pallas_call(
        repack_kernel,
        out_shape=packed_shape,
        in_specs=[WHOLE],
        out_specs=WHOLE,
        compiler_params=params(),
        name="repack",
    )(column_before)
    pieces_before = to_rows(packed_before, column_before)
    for c in range(CHUNKS):
        further[c][0] = lax.optimization_barrier((further[c][0], pieces_before[c]))[0]
    for hop in range(2, groups - 1):
        for c in range(CHUNKS):
            further[c].insert(0, climb(further[c][0], hop))
    strips = [further[c] + [pieces_before[c], pieces[c]] for c in range(CHUNKS)]
    beside, excess = pl.pallas_call(
        edges_kernel,
        out_shape=(
            shape(CHUNKS, groups * planes, SUB, EDGE),
            shape(groups * planes, SUB, EDGE),
        ),
        in_specs=[WHOLE] * groups,
        out_specs=(WHOLE, WHOLE),
        compiler_params=params(),
        name="edges",
    )(*strips[0])

    state = block_of(R, SUB, span)
    triple = block_of(3 * planes, SUB, span)
    quad = block_of(4 * planes, SUB, span)
    quint = block_of(5 * planes, SUB, span)
    maps = []
    work = []
    for c in range(CHUNKS):

        def columns_of(*dims, at=c * steps):
            return pl.BlockSpec(dims + (span,), lambda i: (0,) * len(dims) + (at + i,))

        map_piece, *held = pl.pallas_call(
            functools.partial(forward_kernel, groups, planes, c, length),
            grid=(steps,),
            out_shape=(
                shape(steps, 5 * planes, SUB, span),
                shape(steps, 3 * planes, SUB, span),
                shape(steps, 4 * planes, SUB, span),
                shape(steps, 3 * planes, SUB, span),
                shape(steps, R, SUB, span),
            ),
            in_specs=[WHOLE] * (groups + 2) + [columns_of(planes, 3, R), columns_of(planes, R)],
            out_specs=(quint, triple, quad, triple, state),
            compiler_params=params(),
            name="forward",
        )(*strips[c], beside, excess, observed, noise_weight)
        maps.append(map_piece)
        work.append(held)

    cots = []
    for matrices, states, sources, b in work:
        arrived = [descend(b, 0)]
        for hop in range(1, groups - 1):
            outgoing = pl.pallas_call(
                functools.partial(carry_kernel, planes),
                grid=(steps,),
                out_shape=shape(steps, R, SUB, span),
                in_specs=[SCALARS, state, state, triple],
                out_specs=state,
                compiler_params=params(),
                name="carry",
            )(mixing, arrived[-1], b, matrices)
            arrived.append(descend(outgoing, hop))
        cots.append(
            pl.pallas_call(
                functools.partial(cotangent_kernel, planes),
                grid=(steps,),
                out_shape=shape(steps, 3 * planes, SUB, span),
                in_specs=[SCALARS, SCALARS, triple, triple, quad] + [state] * (groups - 1),
                out_specs=triple,
                compiler_params=params(),
                name="cotangent",
            )(mixing, lens_weight, sources, matrices, states, *arrived)
        )

    partial = pl.pallas_call(
        functools.partial(stencil_kernel, planes),
        out_shape=shape(slabs, planes, SUB, width),
        in_specs=[WHOLE] * CHUNKS,
        out_specs=WHOLE,
        compiler_params=params(),
        name="stencil",
    )(*cots)
    returned = lax.all_to_all(partial, "slab", split_axis=0, concat_axis=0, tiled=True)
    deflection, shear = pl.pallas_call(
        assemble_kernel,
        out_shape=(shape(planes, 2, R, columns), shape(planes, 3, R, columns)),
        in_specs=[WHOLE] * CHUNKS,
        out_specs=(WHOLE, WHOLE),
        compiler_params=params(),
        name="assemble",
    )(*maps)
    potential_grad = pl.pallas_call(
        combine_kernel,
        out_shape=shape(planes, rows, width),
        in_specs=[WHOLE],
        out_specs=WHOLE,
        compiler_params=params(),
        name="combine",
    )(returned)
    return (deflection, shear, potential_grad)


def solution(mesh):
    placed = (
        P("plane", None, "slab"),
        P("plane"),
        P("plane"),
        P("plane", None, "slab", None),
        P("plane", "slab", None),
    )
    return jax.shard_map(
        on_device,
        mesh=mesh,
        in_specs=placed,
        out_specs=(
            P("plane", None, "slab", None),
            P("plane", None, "slab", None),
            P("plane", None, "slab"),
        ),
        check_vma=False,
    )
```

```python
import functools

import jax
import jax.numpy as jnp
from jax import lax
from jax.experimental import pallas as pl
from jax.experimental.pallas import tpu as pltpu
from jax.sharding import PartitionSpec as P

R = 6
SUB = 8
EDGE = 128
F32 = jnp.float32
VMEM_LIMIT = 16 * 1024 * 1024
CHUNKS = 4
SPAN = 4
MIX_LANE = 64


def pack_kernel(weight_ref, p_ref, out_ref):
    planes, rows, width = p_ref.shape
    for k in range(planes):
        w = weight_ref[k]
        for s in range(out_ref.shape[0]):
            before = (R * s - 1) % rows
            after = (R * (s + 1)) % rows
            strip = w * jnp.concatenate(
                [
                    p_ref[k, R * s : R * (s + 1), :],
                    p_ref[k, after : after + 1, :],
                    p_ref[k, before : before + 1, :],
                ],
                axis=0,
            )
            for t in range(width // EDGE):
                out_ref[s, t, k] = strip[:, EDGE * t : EDGE * (t + 1)]


def split_kernel(mix_ref, in_ref, *outs):
    tiles, planes = in_ref.shape[0:2]
    length = tiles // len(outs)
    lane = lax.broadcasted_iota(jnp.int32, (SUB, EDGE), 1)
    for c, out_ref in enumerate(outs):
        out_ref[0:length] = in_ref[length * c : length * (c + 1)]
    for k in range(planes):
        edge = jnp.where(lane == MIX_LANE, mix_ref[k] - 1.0, 0.0)
        for c in range(len(outs)):
            after = in_ref[(length * (c + 1)) % tiles, k]
            before = in_ref[(length * c - 1) % tiles, k]
            edge = jnp.where(lane == 2 * c, pltpu.roll(after, 2 * c, 1), edge)
            edge = jnp.where(lane == (2 * c - 1) % EDGE, pltpu.roll(before, 2 * c, 1), edge)
        outs[0][length, k] = edge


def edges_kernel(*refs):
    strips = refs[:-2]
    beside_ref, excess_ref = refs[-2:]
    for group, strip_ref in enumerate(strips):
        planes = strip_ref.shape[1]
        for k in range(planes):
            edge = strip_ref[strip_ref.shape[0] - 1, k]
            at = group * planes + k
            excess_ref[at] = jnp.broadcast_to(edge[:, MIX_LANE : MIX_LANE + 1], edge.shape)
            for c in range(CHUNKS):
                beside_ref[c, at] = pltpu.roll(edge, (EDGE - 2 * c) % EDGE, 1)


def row_up(x):
    return pltpu.roll(x, SUB - 1, 0)


def row_down(x):
    return pltpu.roll(x, 1, 0)


def col_prev(x):
    return pltpu.roll(x, 1, 1)[:, EDGE:-EDGE]


def col_next(x):
    return pltpu.roll(x, x.shape[1] - 1, 1)[:, EDGE:-EDGE]


def transposed_step(m0, m1, off, p, q, keep):
    new_p = [
        m0 * p[0] + off * p[2] + q[0],
        m0 * p[1] + off * p[3] + q[1],
        off * p[0] + m1 * p[2] + q[2],
        off * p[1] + m1 * p[3] + q[3],
    ]
    return (new_p, [keep * x for x in p])


def pack_state(out_ref, fields):
    for j in range(R):
        out_ref[0, j] = jnp.concatenate(
            [fields[j], fields[6][j : j + 1], fields[7][j : j + 1]], axis=0
        )


def unpack_state(arrived):
    tiles = [sum(in_ref[0, j] for in_ref in arrived) for j in range(R)]
    fields = [t[0:R] for t in tiles]
    fields.append(jnp.concatenate([t[6:7] for t in tiles], axis=0))
    fields.append(jnp.concatenate([t[7:8] for t in tiles], axis=0))
    return fields


def forward_kernel(groups, planes, chunk, length, *refs):
    strips = refs[:groups]
    beside_ref, excess_ref, obs_ref, noise_ref = refs[groups : groups + 4]
    map_ref, m_ref, a_ref, src_ref, b_ref = refs[-5:]
    step = pl.program_id(0)
    width = obs_ref.shape[-1]
    span = width // EDGE
    first = step * span
    at_start = first == 0
    at_end = first + span == length
    one = jnp.ones((SUB, width), F32)
    zero = jnp.zeros((SUB, width), F32)
    a = [one, zero, zero, one]
    a_before = a
    psi = jnp.zeros((SUB, width + 2 * EDGE), F32)
    psi_before = psi
    keeps = []
    for group in range(groups):
        strip_ref = strips[group]
        own = group == groups - 1
        for k in range(planes):
            beside = beside_ref[chunk, group * planes + k]
            excess_tile = excess_ref[group * planes + k]
            excess_ext = jnp.concatenate([excess_tile] * (span + 2), axis=1)
            excess = excess_ext[:, EDGE:-EDGE]
            mix_ext = jnp.concatenate([1.0 + excess_tile] * (span + 2), axis=1)
            mix = mix_ext[:, EDGE:-EDGE]
            left = jnp.where(at_start, beside, strip_ref[jnp.maximum(first - 1, 0), k])
            right = jnp.where(at_end, beside, strip_ref[jnp.minimum(first + span, length - 1), k])
            tiles = [strip_ref[first + t, k] for t in range(span)]
            mid = jnp.concatenate(tiles, axis=1)
            ext = jnp.concatenate([left] + tiles + [right], axis=1)
            up = row_up(ext)
            down = row_down(ext)
            across = up - down
            twice = 2.0 * mid
            m0 = mix - ((up + down)[:, EDGE:-EDGE] - twice)
            m1 = mix - (col_next(ext) + col_prev(ext) - twice)
            off = 0.25 * (col_prev(across) - col_next(across))
            if own:
                m_ref[0, 3 * k] = m0
                m_ref[0, 3 * k + 1] = m1
                m_ref[0, 3 * k + 2] = off
                keeps.append(-excess[0:R])
                for j in range(4):
                    a_ref[0, 4 * k + j] = a[j]
            new_a = [
                m0 * a[0] + off * a[2] - excess * a_before[0],
                m0 * a[1] + off * a[3] - excess * a_before[1],
                off * a[0] + m1 * a[2] - excess * a_before[2],
                off * a[1] + m1 * a[3] - excess * a_before[3],
            ]
            a_before, a = (a, new_a)
            psi, psi_before = (mix_ext * psi - excess_ext * psi_before - ext, psi)
            if own:
                slope_rows = 0.5 * (row_up(psi) - row_down(psi))[:, EDGE:-EDGE]
                slope_cols = 0.5 * (col_next(psi) - col_prev(psi))
                shear = [
                    1.0 - 0.5 * (a[0] + a[3]),
                    0.5 * (a[3] - a[0]),
                    -0.5 * (a[1] + a[2]),
                ]
                for j, field in enumerate([slope_rows, slope_cols] + shear):
                    map_ref[0, 5 * k + j] = field
                noise = -0.5 * noise_ref[k]
                r = [noise * (shear[j][0:R] - obs_ref[k, j]) for j in range(3)]
                src_ref[0, 3 * k, 0:R] = r[0] + r[1]
                src_ref[0, 3 * k + 1, 0:R] = r[2]
                src_ref[0, 3 * k + 2, 0:R] = r[0] - r[1]
    none = jnp.zeros((R, width), F32)
    p = [none] * 4
    q = [none] * 4
    for k in reversed(range(planes)):
        s0, s1, s3 = (src_ref[0, 3 * k + j, 0:R] for j in range(3))
        p = [p[0] + s0, p[1] + s1, p[2] + s1, p[3] + s3]
        m0, m1, off = (m_ref[0, 3 * k + j, 0:R] for j in range(3))
        p, q = transposed_step(m0, m1, off, p, q, keeps[k])
    pack_state(b_ref, p + q)


def assemble_kernel(*refs):
    maps = refs[:-2]
    defl_ref, shear_ref = refs[-2:]
    steps, width = (maps[0].shape[0], maps[0].shape[-1])
    for c, map_ref in enumerate(maps):
        for i in range(steps):
            start = (c * steps + i) * width
            for k in range(defl_ref.shape[0]):
                for j in range(2):
                    defl_ref[k, j, :, start : start + width] = map_ref[i, 5 * k + j, 0:R]
                for j in range(3):
                    shear_ref[k, j, :, start : start + width] = map_ref[i, 5 * k + 2 + j, 0:R]


def carry_kernel(planes, mix_ref, in_ref, b_ref, m_ref, out_ref):
    fields = unpack_state([in_ref])
    p, q = (fields[0:4], fields[4:8])
    for k in reversed(range(planes)):
        m0, m1, off = (m_ref[0, 3 * k + j, 0:R] for j in range(3))
        p, q = transposed_step(m0, m1, off, p, q, 1.0 - mix_ref[k])
    pack_state(out_ref, p + q)
    out_ref[...] += b_ref[...]


def cotangent_kernel(planes, mix_ref, weight_ref, src_ref, m_ref, a_ref, *refs):
    arrived, cot_ref = (refs[:-1], refs[-1])
    width = cot_ref.shape[-1]
    fields = unpack_state(arrived)
    p, q = (fields[0:4], fields[4:8])
    blank = jnp.zeros((SUB - R, width), F32)
    for k in reversed(range(planes)):
        s0, s1, s3 = (src_ref[0, 3 * k + j, 0:R] for j in range(3))
        p = [p[0] + s0, p[1] + s1, p[2] + s1, p[3] + s3]
        a = [a_ref[0, 4 * k + j, 0:R] for j in range(4)]
        w = -weight_ref[k]
        cots = [
            w * (p[0] * a[0] + p[1] * a[1]),
            w * (p[2] * a[2] + p[3] * a[3]),
            (0.25 * w) * (p[0] * a[2] + p[1] * a[3] + p[2] * a[0] + p[3] * a[1]),
        ]
        for j in range(3):
            cot_ref[0, 3 * k + j] = jnp.concatenate([cots[j], blank], axis=0)
        m0, m1, off = (m_ref[0, 3 * k + j, 0:R] for j in range(3))
        p, q = transposed_step(m0, m1, off, p, q, 1.0 - mix_ref[k])


def stencil_kernel(planes, *refs):
    cots, out_ref = (refs[:-1], refs[-1])
    out = out_ref.shape[-1]
    steps, width = (cots[0].shape[0], cots[0].shape[-1])
    blocks = len(cots) * steps

    def cot(block, field):
        return cots[block // steps].at[block % steps, field]

    for c in range(blocks):
        before = (c - 1) % blocks
        after = (c + 1) % blocks

        def ext(field):
            return jnp.concatenate(
                [
                    cot(before, field)[:, width - EDGE :],
                    cot(c, field)[...],
                    cot(after, field)[:, 0:EDGE],
                ],
                axis=1,
            )

        for k in range(planes):
            cot_rows = cot(c, 3 * k)[...]
            cot_cols = ext(3 * k + 1)
            cot_mixed = ext(3 * k + 2)
            across = row_up(cot_mixed) - row_down(cot_mixed)
            rows_part = row_up(cot_rows) + row_down(cot_rows) - 2.0 * cot_rows
            cols_part = col_next(cot_cols) + col_prev(cot_cols) - 2.0 * cot_cols[:, EDGE:-EDGE]
            grad = rows_part + cols_part + (col_next(across) - col_prev(across))
            for part in range(max(1, width // out)):
                place = c * width + part * out
                size = min(out, width)
                start = place % out
                out_ref[place // out, k, :, start : start + size] = grad[
                    :, part * out : part * out + size
                ]


def combine_kernel(in_ref, out_ref):
    slabs, planes, _, width = in_ref.shape
    blank = jnp.zeros((R - 2, width), F32)
    for k in range(planes):
        for s in range(slabs):
            halo = jnp.concatenate(
                [in_ref[(s - 1) % slabs, k, 6:7], blank, in_ref[(s + 1) % slabs, k, 7:8]], axis=0
            )
            out_ref[k, R * s : R * (s + 1), :] = in_ref[s, k, 0:R] + halo


def shape(*dims):
    return jax.ShapeDtypeStruct(dims, F32)


def params():
    return pltpu.CompilerParams(vmem_limit_bytes=VMEM_LIMIT)


def block_of(*dims):
    return pl.BlockSpec((1,) + dims, lambda c: (c,) + (0,) * len(dims))


SCALARS = pl.BlockSpec(memory_space=pltpu.SMEM)
WHOLE = pl.BlockSpec(memory_space=pltpu.VMEM)


def on_device(potential, mixing, lens_weight, observed, noise_weight):
    groups = lax.axis_size("plane")
    slabs = lax.axis_size("slab")
    planes, rows, width = potential.shape
    assert rows == R * slabs and width % EDGE == 0
    columns = width * slabs
    tiles = width // EDGE
    length = tiles * slabs // CHUNKS
    span = SPAN * EDGE
    steps = length // SPAN

    def climb(x, hop):
        return lax.ppermute(x, "plane", [(i, i + 1) for i in range(hop, groups - 1)])

    def descend(x, hop):
        return lax.ppermute(x, "plane", [(groups - 1 - hop, groups - 2 - hop)])

    packed = pl.pallas_call(
        pack_kernel,
        out_shape=shape(slabs, tiles, planes, SUB, EDGE),
        in_specs=[SCALARS, WHOLE],
        out_specs=WHOLE,
        compiler_params=params(),
        name="pack",
    )(lens_weight, potential)
    own = lax.all_to_all(packed, "slab", split_axis=0, concat_axis=0, tiled=True)
    own = own.reshape(slabs * tiles, planes, SUB, EDGE)
    pieces = pl.pallas_call(
        split_kernel,
        out_shape=tuple(
            shape(length + (c == 0), planes, SUB, EDGE) for c in range(CHUNKS)
        ),
        in_specs=[SCALARS, WHOLE],
        out_specs=(WHOLE,) * CHUNKS,
        compiler_params=params(),
        name="split",
    )(mixing, own)
    strips = [[piece] for piece in pieces]
    for turn in range(CHUNKS + groups - 2):
        for c in range(CHUNKS):
            if 0 <= turn - c < groups - 1:
                strips[c].insert(0, climb(strips[c][0], turn - c))

    beside, excess = pl.pallas_call(
        edges_kernel,
        out_shape=(
            shape(CHUNKS, groups * planes, SUB, EDGE),
            shape(groups * planes, SUB, EDGE),
        ),
        in_specs=[WHOLE] * groups,
        out_specs=(WHOLE, WHOLE),
        compiler_params=params(),
        name="edges",
    )(*strips[0])

    state = block_of(R, SUB, span)
    triple = block_of(3 * planes, SUB, span)
    quad = block_of(4 * planes, SUB, span)
    quint = block_of(5 * planes, SUB, span)
    maps = []
    work = []
    for c in range(CHUNKS):

        def columns_of(*dims, at=c * steps):
            return pl.BlockSpec(dims + (span,), lambda i: (0,) * len(dims) + (at + i,))

        map_piece, *held = pl.pallas_call(
            functools.partial(forward_kernel, groups, planes, c, length),
            grid=(steps,),
            out_shape=(
                shape(steps, 5 * planes, SUB, span),
                shape(steps, 3 * planes, SUB, span),
                shape(steps, 4 * planes, SUB, span),
                shape(steps, 3 * planes, SUB, span),
                shape(steps, R, SUB, span),
            ),
            in_specs=[WHOLE] * (groups + 2) + [columns_of(planes, 3, R), columns_of(planes, R)],
            out_specs=(quint, triple, quad, triple, state),
            compiler_params=params(),
            name="forward",
        )(*strips[c], beside, excess, observed, noise_weight)
        maps.append(map_piece)
        work.append(held)

    cots = []
    for matrices, states, sources, b in work:
        arrived = [descend(b, 0)]
        for hop in range(1, groups - 1):
            outgoing = pl.pallas_call(
                functools.partial(carry_kernel, planes),
                grid=(steps,),
                out_shape=shape(steps, R, SUB, span),
                in_specs=[SCALARS, state, state, triple],
                out_specs=state,
                compiler_params=params(),
                name="carry",
            )(mixing, arrived[-1], b, matrices)
            arrived.append(descend(outgoing, hop))
        cots.append(
            pl.pallas_call(
                functools.partial(cotangent_kernel, planes),
                grid=(steps,),
                out_shape=shape(steps, 3 * planes, SUB, span),
                in_specs=[SCALARS, SCALARS, triple, triple, quad] + [state] * (groups - 1),
                out_specs=triple,
                compiler_params=params(),
                name="cotangent",
            )(mixing, lens_weight, sources, matrices, states, *arrived)
        )

    partial = pl.pallas_call(
        functools.partial(stencil_kernel, planes),
        out_shape=shape(slabs, planes, SUB, width),
        in_specs=[WHOLE] * CHUNKS,
        out_specs=WHOLE,
        compiler_params=params(),
        name="stencil",
    )(*cots)
    returned = lax.all_to_all(partial, "slab", split_axis=0, concat_axis=0, tiled=True)
    deflection, shear = pl.pallas_call(
        assemble_kernel,
        out_shape=(shape(planes, 2, R, columns), shape(planes, 3, R, columns)),
        in_specs=[WHOLE] * CHUNKS,
        out_specs=(WHOLE, WHOLE),
        compiler_params=params(),
        name="assemble",
    )(*maps)
    potential_grad = pl.pallas_call(
        combine_kernel,
        out_shape=shape(planes, rows, width),
        in_specs=[WHOLE],
        out_specs=WHOLE,
        compiler_params=params(),
        name="combine",
    )(returned)
    return (deflection, shear, potential_grad)


def solution(mesh):
    placed = (
        P("plane", None, "slab"),
        P("plane"),
        P("plane"),
        P("plane", None, "slab", None),
        P("plane", "slab", None),
    )
    return jax.shard_map(
        on_device,
        mesh=mesh,
        in_specs=placed,
        out_specs=(
            P("plane", None, "slab", None),
            P("plane", None, "slab", None),
            P("plane", None, "slab"),
        ),
        check_vma=False,
    )
```

```python
import functools

import jax
import jax.numpy as jnp
from jax import lax
from jax.experimental import pallas as pl
from jax.experimental.pallas import tpu as pltpu
from jax.sharding import PartitionSpec as P

R = 6
SUB = 8
EDGE = 128
F32 = jnp.float32
VMEM_LIMIT = 16 * 1024 * 1024
CHUNKS = 4
SPAN = 4
MIX_LANE = 64


def pack_kernel(coef_ref, p_ref, out_ref):
    planes, rows, width = p_ref.shape
    for k in range(planes):
        w = coef_ref[0, k]
        for s in range(out_ref.shape[0]):
            before = (R * s - 1) % rows
            after = (R * (s + 1)) % rows
            strip = w * jnp.concatenate(
                [
                    p_ref[k, R * s : R * (s + 1), :],
                    p_ref[k, after : after + 1, :],
                    p_ref[k, before : before + 1, :],
                ],
                axis=0,
            )
            for t in range(width // EDGE):
                out_ref[s, t, k] = strip[:, EDGE * t : EDGE * (t + 1)]


def split_kernel(coef_ref, in_ref, *outs):
    tiles, planes = in_ref.shape[0:2]
    length = tiles // len(outs)
    lane = lax.broadcasted_iota(jnp.int32, (SUB, EDGE), 1)
    for c, out_ref in enumerate(outs):
        out_ref[0:length] = in_ref[length * c : length * (c + 1)]
    for k in range(planes):
        edge = jnp.where(lane == MIX_LANE, coef_ref[1, k] - 1.0, 0.0)
        for c in range(len(outs)):
            after = in_ref[(length * (c + 1)) % tiles, k]
            before = in_ref[(length * c - 1) % tiles, k]
            edge = jnp.where(lane == 2 * c, pltpu.roll(after, 2 * c, 1), edge)
            edge = jnp.where(lane == (2 * c - 1) % EDGE, pltpu.roll(before, 2 * c, 1), edge)
        outs[0][length, k] = edge


def edges_kernel(*refs):
    strips = refs[:-2]
    beside_ref, excess_ref = refs[-2:]
    for group, strip_ref in enumerate(strips):
        planes = strip_ref.shape[1]
        for k in range(planes):
            edge = strip_ref[strip_ref.shape[0] - 1, k]
            at = group * planes + k
            excess_ref[at] = jnp.broadcast_to(edge[:, MIX_LANE : MIX_LANE + 1], edge.shape)
            for c in range(CHUNKS):
                beside_ref[c, at] = pltpu.roll(edge, (EDGE - 2 * c) % EDGE, 1)


def row_up(x):
    return pltpu.roll(x, SUB - 1, 0)


def row_down(x):
    return pltpu.roll(x, 1, 0)


def col_prev(x):
    return pltpu.roll(x, 1, 1)[:, EDGE:-EDGE]


def col_next(x):
    return pltpu.roll(x, x.shape[1] - 1, 1)[:, EDGE:-EDGE]


def transposed_step(m0, m1, off, p, q, keep):
    new_p = [
        m0 * p[0] + off * p[2] + q[0],
        m0 * p[1] + off * p[3] + q[1],
        off * p[0] + m1 * p[2] + q[2],
        off * p[1] + m1 * p[3] + q[3],
    ]
    return (new_p, [keep * x for x in p])


def pack_state(out_ref, step, fields, extra_ref=None):
    for j in range(R):
        tile = jnp.concatenate(
            [fields[j], fields[6][j : j + 1], fields[7][j : j + 1]], axis=0
        )
        out_ref[step, j] = tile if extra_ref is None else tile + extra_ref[step, j]


def unpack_state(arrived, step):
    tiles = [sum(in_ref[step, j] for in_ref in arrived) for j in range(R)]
    fields = [t[0:R] for t in tiles]
    fields.append(jnp.concatenate([t[6:7] for t in tiles], axis=0))
    fields.append(jnp.concatenate([t[7:8] for t in tiles], axis=0))
    return fields


def forward_block(groups, planes, chunk, length, step, *refs):
    strips = refs[:groups]
    beside_ref, excess_ref, obs_ref, noise_ref = refs[groups : groups + 4]
    map_ref, m_ref, a_ref, src_ref, b_ref = refs[-5:]
    width = m_ref.shape[-1]
    span = width // EDGE
    first = step * span
    start = EDGE * (chunk * length + first)
    one = jnp.ones((SUB, width), F32)
    zero = jnp.zeros((SUB, width), F32)
    a = [one, zero, zero, one]
    a_before = a
    psi = jnp.zeros((SUB, width + 2 * EDGE), F32)
    psi_before = psi
    keeps = []
    for group in range(groups):
        strip_ref = strips[group]
        own = group == groups - 1
        for k in range(planes):
            beside = beside_ref[chunk, group * planes + k]
            excess_tile = excess_ref[group * planes + k]
            excess_ext = jnp.concatenate([excess_tile] * (span + 2), axis=1)
            excess = excess_ext[:, EDGE:-EDGE]
            mix_ext = jnp.concatenate([1.0 + excess_tile] * (span + 2), axis=1)
            mix = mix_ext[:, EDGE:-EDGE]
            left = strip_ref[first - 1, k] if first > 0 else beside
            right = strip_ref[first + span, k] if first + span < length else beside
            tiles = [strip_ref[first + t, k] for t in range(span)]
            mid = jnp.concatenate(tiles, axis=1)
            ext = jnp.concatenate([left] + tiles + [right], axis=1)
            up = row_up(ext)
            down = row_down(ext)
            across = up - down
            twice = 2.0 * mid
            m0 = mix - ((up + down)[:, EDGE:-EDGE] - twice)
            m1 = mix - (col_next(ext) + col_prev(ext) - twice)
            off = 0.25 * (col_prev(across) - col_next(across))
            if own:
                m_ref[step, 3 * k] = m0
                m_ref[step, 3 * k + 1] = m1
                m_ref[step, 3 * k + 2] = off
                keeps.append(-excess[0:R])
                for j in range(4):
                    a_ref[step, 4 * k + j] = a[j]
            new_a = [
                m0 * a[0] + off * a[2] - excess * a_before[0],
                m0 * a[1] + off * a[3] - excess * a_before[1],
                off * a[0] + m1 * a[2] - excess * a_before[2],
                off * a[1] + m1 * a[3] - excess * a_before[3],
            ]
            a_before, a = (a, new_a)
            psi, psi_before = (mix_ext * psi - excess_ext * psi_before - ext, psi)
            if own:
                slope_rows = 0.5 * (row_up(psi) - row_down(psi))[:, EDGE:-EDGE]
                slope_cols = 0.5 * (col_next(psi) - col_prev(psi))
                shear = [
                    1.0 - 0.5 * (a[0] + a[3]),
                    0.5 * (a[3] - a[0]),
                    -0.5 * (a[1] + a[2]),
                ]
                for j, field in enumerate([slope_rows, slope_cols] + shear):
                    map_ref[step, 5 * k + j] = field
                noise = -0.5 * noise_ref[k, :, start : start + width]
                r = [
                    noise * (shear[j][0:R] - obs_ref[k, j, :, start : start + width])
                    for j in range(3)
                ]
                src_ref[step, 3 * k, 0:R] = r[0] + r[1]
                src_ref[step, 3 * k + 1, 0:R] = r[2]
                src_ref[step, 3 * k + 2, 0:R] = r[0] - r[1]
    none = jnp.zeros((R, width), F32)
    p = [none] * 4
    q = [none] * 4
    for k in reversed(range(planes)):
        s0, s1, s3 = (src_ref[step, 3 * k + j, 0:R] for j in range(3))
        p = [p[0] + s0, p[1] + s1, p[2] + s1, p[3] + s3]
        m0, m1, off = (m_ref[step, 3 * k + j, 0:R] for j in range(3))
        p, q = transposed_step(m0, m1, off, p, q, keeps[k])
    pack_state(b_ref, step, p + q)


def forward_kernel(groups, planes, chunk, length, *refs):
    for step in range(refs[-1].shape[0]):
        forward_block(groups, planes, chunk, length, step, *refs)


def assemble_kernel(*refs):
    maps = refs[:-2]
    defl_ref, shear_ref = refs[-2:]
    steps, width = (maps[0].shape[0], maps[0].shape[-1])
    for c, map_ref in enumerate(maps):
        for i in range(steps):
            start = (c * steps + i) * width
            for k in range(defl_ref.shape[0]):
                for j in range(2):
                    defl_ref[k, j, :, start : start + width] = map_ref[i, 5 * k + j, 0:R]
                for j in range(3):
                    shear_ref[k, j, :, start : start + width] = map_ref[i, 5 * k + 2 + j, 0:R]


def carry_kernel(planes, sender, coef_ref, in_ref, b_ref, m_ref, out_ref):
    @pl.when(lax.axis_index("plane") == sender)
    def _():
        for step in range(out_ref.shape[0]):
            fields = unpack_state([in_ref], step)
            p, q = (fields[0:4], fields[4:8])
            for k in reversed(range(planes)):
                m0, m1, off = (m_ref[step, 3 * k + j, 0:R] for j in range(3))
                p, q = transposed_step(m0, m1, off, p, q, 1.0 - coef_ref[1, k])
            pack_state(out_ref, step, p + q, b_ref)


def cotangent_kernel(planes, coef_ref, src_ref, m_ref, a_ref, *refs):
    arrived, cot_ref = (refs[:-1], refs[-1])
    blank = jnp.zeros((SUB - R, cot_ref.shape[-1]), F32)
    for step in range(cot_ref.shape[0]):
        fields = unpack_state(arrived, step)
        p, q = (fields[0:4], fields[4:8])
        for k in reversed(range(planes)):
            s0, s1, s3 = (src_ref[step, 3 * k + j, 0:R] for j in range(3))
            p = [p[0] + s0, p[1] + s1, p[2] + s1, p[3] + s3]
            a = [a_ref[step, 4 * k + j, 0:R] for j in range(4)]
            w = -coef_ref[0, k]
            cots = [
                w * (p[0] * a[0] + p[1] * a[1]),
                w * (p[2] * a[2] + p[3] * a[3]),
                (0.25 * w) * (p[0] * a[2] + p[1] * a[3] + p[2] * a[0] + p[3] * a[1]),
            ]
            for j in range(3):
                cot_ref[step, 3 * k + j] = jnp.concatenate([cots[j], blank], axis=0)
            m0, m1, off = (m_ref[step, 3 * k + j, 0:R] for j in range(3))
            p, q = transposed_step(m0, m1, off, p, q, 1.0 - coef_ref[1, k])


def stencil_kernel(planes, *refs):
    cots, out_ref = (refs[:-1], refs[-1])
    out = out_ref.shape[-1]
    steps, width = (cots[0].shape[0], cots[0].shape[-1])
    blocks = len(cots) * steps

    def cot(block, field):
        return cots[block // steps].at[block % steps, field]

    for c in range(blocks):
        before = (c - 1) % blocks
        after = (c + 1) % blocks

        def ext(field):
            return jnp.concatenate(
                [
                    cot(before, field)[:, width - EDGE :],
                    cot(c, field)[...],
                    cot(after, field)[:, 0:EDGE],
                ],
                axis=1,
            )

        for k in range(planes):
            cot_rows = cot(c, 3 * k)[...]
            cot_cols = ext(3 * k + 1)
            cot_mixed = ext(3 * k + 2)
            across = row_up(cot_mixed) - row_down(cot_mixed)
            rows_part = row_up(cot_rows) + row_down(cot_rows) - 2.0 * cot_rows
            cols_part = col_next(cot_cols) + col_prev(cot_cols) - 2.0 * cot_cols[:, EDGE:-EDGE]
            grad = rows_part + cols_part + (col_next(across) - col_prev(across))
            for part in range(max(1, width // out)):
                place = c * width + part * out
                size = min(out, width)
                start = place % out
                out_ref[place // out, k, :, start : start + size] = grad[
                    :, part * out : part * out + size
                ]


def combine_kernel(in_ref, out_ref):
    slabs, planes, _, width = in_ref.shape
    blank = jnp.zeros((R - 2, width), F32)
    for k in range(planes):
        for s in range(slabs):
            halo = jnp.concatenate(
                [in_ref[(s - 1) % slabs, k, 6:7], blank, in_ref[(s + 1) % slabs, k, 7:8]], axis=0
            )
            out_ref[k, R * s : R * (s + 1), :] = in_ref[s, k, 0:R] + halo


def shape(*dims):
    return jax.ShapeDtypeStruct(dims, F32)


def params():
    return pltpu.CompilerParams(vmem_limit_bytes=VMEM_LIMIT)


SCALARS = pl.BlockSpec(memory_space=pltpu.SMEM)
WHOLE = pl.BlockSpec(memory_space=pltpu.VMEM)


def on_device(potential, mixing, lens_weight, observed, noise_weight):
    groups = lax.axis_size("plane")
    slabs = lax.axis_size("slab")
    planes, rows, width = potential.shape
    assert rows == R * slabs and width % EDGE == 0
    columns = width * slabs
    tiles = width // EDGE
    length = tiles * slabs // CHUNKS
    span = SPAN * EDGE
    steps = length // SPAN

    def climb(x, hop):
        return lax.ppermute(x, "plane", [(i, i + 1) for i in range(hop, groups - 1)])

    def descend(x, hop):
        return lax.ppermute(x, "plane", [(groups - 1 - hop, groups - 2 - hop)])

    coef = jnp.stack([lens_weight, mixing])
    packed = pl.pallas_call(
        pack_kernel,
        out_shape=shape(slabs, tiles, planes, SUB, EDGE),
        in_specs=[SCALARS, WHOLE],
        out_specs=WHOLE,
        compiler_params=params(),
        name="pack",
    )(coef, potential)
    own = lax.all_to_all(packed, "slab", split_axis=0, concat_axis=0, tiled=True)
    own = own.reshape(slabs * tiles, planes, SUB, EDGE)
    pieces = pl.pallas_call(
        split_kernel,
        out_shape=tuple(
            shape(length + (c == 0), planes, SUB, EDGE) for c in range(CHUNKS)
        ),
        in_specs=[SCALARS, WHOLE],
        out_specs=(WHOLE,) * CHUNKS,
        compiler_params=params(),
        name="split",
    )(coef, own)
    strips = [[piece] for piece in pieces]
    for turn in range(CHUNKS + groups - 2):
        for c in range(CHUNKS):
            if 0 <= turn - c < groups - 1:
                strips[c].insert(0, climb(strips[c][0], turn - c))

    beside, excess = pl.pallas_call(
        edges_kernel,
        out_shape=(
            shape(CHUNKS, groups * planes, SUB, EDGE),
            shape(groups * planes, SUB, EDGE),
        ),
        in_specs=[WHOLE] * groups,
        out_specs=(WHOLE, WHOLE),
        compiler_params=params(),
        name="edges",
    )(*strips[0])

    maps = []
    work = []
    for c in range(CHUNKS):
        map_piece, *held = pl.pallas_call(
            functools.partial(forward_kernel, groups, planes, c, length),
            out_shape=(
                shape(steps, 5 * planes, SUB, span),
                shape(steps, 3 * planes, SUB, span),
                shape(steps, 4 * planes, SUB, span),
                shape(steps, 3 * planes, SUB, span),
                shape(steps, R, SUB, span),
            ),
            in_specs=[WHOLE] * (groups + 4),
            out_specs=(WHOLE,) * 5,
            compiler_params=params(),
            name="forward",
        )(*strips[c], beside, excess, observed, noise_weight)
        maps.append(map_piece)
        work.append(held)

    cots = []
    for matrices, states, sources, b in work:
        arrived = [descend(b, 0)]
        for hop in range(1, groups - 1):
            outgoing = pl.pallas_call(
                functools.partial(carry_kernel, planes, groups - 1 - hop),
                out_shape=shape(steps, R, SUB, span),
                in_specs=[SCALARS] + [WHOLE] * 3,
                out_specs=WHOLE,
                compiler_params=params(),
                name="carry",
            )(coef, arrived[-1], b, matrices)
            arrived.append(descend(outgoing, hop))
        cots.append(
            pl.pallas_call(
                functools.partial(cotangent_kernel, planes),
                out_shape=shape(steps, 3 * planes, SUB, span),
                in_specs=[SCALARS] + [WHOLE] * (groups + 2),
                out_specs=WHOLE,
                compiler_params=params(),
                name="cotangent",
            )(coef, sources, matrices, states, *arrived)
        )

    partial = pl.pallas_call(
        functools.partial(stencil_kernel, planes),
        out_shape=shape(slabs, planes, SUB, width),
        in_specs=[WHOLE] * CHUNKS,
        out_specs=WHOLE,
        compiler_params=params(),
        name="stencil",
    )(*cots)
    returned = lax.all_to_all(partial, "slab", split_axis=0, concat_axis=0, tiled=True)
    deflection, shear = pl.pallas_call(
        assemble_kernel,
        out_shape=(shape(planes, 2, R, columns), shape(planes, 3, R, columns)),
        in_specs=[WHOLE] * CHUNKS,
        out_specs=(WHOLE, WHOLE),
        compiler_params=params(),
        name="assemble",
    )(*maps)
    potential_grad = pl.pallas_call(
        combine_kernel,
        out_shape=shape(planes, rows, width),
        in_specs=[WHOLE],
        out_specs=WHOLE,
        compiler_params=params(),
        name="combine",
    )(returned)
    return (deflection, shear, potential_grad)


def solution(mesh):
    placed = (
        P("plane", None, "slab"),
        P("plane"),
        P("plane"),
        P("plane", None, "slab", None),
        P("plane", "slab", None),
    )
    return jax.shard_map(
        on_device,
        mesh=mesh,
        in_specs=placed,
        out_specs=(
            P("plane", None, "slab", None),
            P("plane", None, "slab", None),
            P("plane", None, "slab"),
        ),
        check_vma=False,
    )
```

```python
import functools

import jax
import jax.numpy as jnp
from jax import lax
from jax.experimental import pallas as pl
from jax.experimental.pallas import tpu as pltpu
from jax.sharding import PartitionSpec as P

R = 6
SUB = 8
EDGE = 128
F32 = jnp.float32
VMEM_LIMIT = 16 * 1024 * 1024
CHUNKS = 4
WAVE = 2
SPAN = 4
MIX_LANE = 64


def pack_kernel(coef_ref, p_ref, out_ref, weight_ref):
    planes, rows, width = p_ref.shape
    for k in range(planes):
        w = coef_ref[0, k]
        weight_ref[k] = jnp.full((SUB, EDGE), w, F32)
        for s in range(out_ref.shape[0]):
            before = (R * s - 1) % rows
            after = (R * (s + 1)) % rows
            strip = w * jnp.concatenate(
                [
                    p_ref[k, R * s : R * (s + 1), :],
                    p_ref[k, after : after + 1, :],
                    p_ref[k, before : before + 1, :],
                ],
                axis=0,
            )
            for t in range(width // EDGE):
                out_ref[s, t, k] = strip[:, EDGE * t : EDGE * (t + 1)]


def split_kernel(coef_ref, in_ref, *outs):
    tiles, planes = in_ref.shape[0:2]
    length = tiles // len(outs)
    lane = lax.broadcasted_iota(jnp.int32, (SUB, EDGE), 1)
    for c, out_ref in enumerate(outs):
        out_ref[0:length] = in_ref[length * c : length * (c + 1)]
    for k in range(planes):
        edge = jnp.where(lane == MIX_LANE, coef_ref[1, k] - 1.0, 0.0)
        for c in range(len(outs)):
            after = in_ref[(length * (c + 1)) % tiles, k]
            before = in_ref[(length * c - 1) % tiles, k]
            edge = jnp.where(lane == 2 * c, pltpu.roll(after, 2 * c, 1), edge)
            edge = jnp.where(lane == (2 * c - 1) % EDGE, pltpu.roll(before, 2 * c, 1), edge)
        outs[0][length, k] = edge


def edges_kernel(*refs):
    strips = refs[:-2]
    beside_ref, excess_ref = refs[-2:]
    for group, strip_ref in enumerate(strips):
        planes = strip_ref.shape[1]
        for k in range(planes):
            edge = strip_ref[strip_ref.shape[0] - 1, k]
            at = group * planes + k
            excess_ref[at] = jnp.broadcast_to(edge[:, MIX_LANE : MIX_LANE + 1], edge.shape)
            for c in range(CHUNKS):
                beside_ref[c, at] = pltpu.roll(edge, (EDGE - 2 * c) % EDGE, 1)


def row_up(x):
    return pltpu.roll(x, SUB - 1, 0)


def row_down(x):
    return pltpu.roll(x, 1, 0)


def col_prev(x):
    return pltpu.roll(x, 1, 1)[:, EDGE:-EDGE]


def col_next(x):
    return pltpu.roll(x, x.shape[1] - 1, 1)[:, EDGE:-EDGE]


def transposed_step(m0, m1, off, p, q, keep):
    new_p = [
        m0 * p[0] + off * p[2] + q[0],
        m0 * p[1] + off * p[3] + q[1],
        off * p[0] + m1 * p[2] + q[2],
        off * p[1] + m1 * p[3] + q[3],
    ]
    return (new_p, [keep * x for x in p])


def pack_state(out_ref, step, fields, extra_ref=None):
    for j in range(R):
        tile = jnp.concatenate(
            [fields[j], fields[6][j : j + 1], fields[7][j : j + 1]], axis=0
        )
        out_ref[step, j] = tile if extra_ref is None else tile + extra_ref[step, j]


def unpack_state(arrived, step):
    tiles = [sum(in_ref[step, j] for in_ref in arrived) for j in range(R)]
    fields = [t[0:R] for t in tiles]
    fields.append(jnp.concatenate([t[6:7] for t in tiles], axis=0))
    fields.append(jnp.concatenate([t[7:8] for t in tiles], axis=0))
    return fields


def forward_block(groups, planes, chunk, length, step, *refs):
    strips = refs[:groups]
    beside_ref, excess_ref, obs_ref, noise_ref = refs[groups : groups + 4]
    map_ref, m_ref, a_ref, src_ref, b_ref = refs[-5:]
    width = m_ref.shape[-1]
    span = width // EDGE
    first = step * span
    start = EDGE * (chunk * length + first)
    one = jnp.ones((SUB, width), F32)
    zero = jnp.zeros((SUB, width), F32)
    a = [one, zero, zero, one]
    a_before = a
    psi = jnp.zeros((SUB, width + 2 * EDGE), F32)
    psi_before = psi
    keeps = []
    for group in range(groups):
        strip_ref = strips[group]
        own = group == groups - 1
        for k in range(planes):
            beside = beside_ref[chunk, group * planes + k]
            excess_tile = excess_ref[group * planes + k]
            excess_ext = jnp.concatenate([excess_tile] * (span + 2), axis=1)
            excess = excess_ext[:, EDGE:-EDGE]
            mix_ext = jnp.concatenate([1.0 + excess_tile] * (span + 2), axis=1)
            mix = mix_ext[:, EDGE:-EDGE]
            left = strip_ref[first - 1, k] if first > 0 else beside
            right = strip_ref[first + span, k] if first + span < length else beside
            tiles = [strip_ref[first + t, k] for t in range(span)]
            mid = jnp.concatenate(tiles, axis=1)
            ext = jnp.concatenate([left] + tiles + [right], axis=1)
            up = row_up(ext)
            down = row_down(ext)
            across = up - down
            twice = 2.0 * mid
            m0 = mix - ((up + down)[:, EDGE:-EDGE] - twice)
            m1 = mix - (col_next(ext) + col_prev(ext) - twice)
            off = 0.25 * (col_prev(across) - col_next(across))
            if own:
                m_ref[step, 3 * k] = m0
                m_ref[step, 3 * k + 1] = m1
                m_ref[step, 3 * k + 2] = off
                keeps.append(-excess[0:R])
                for j in range(4):
                    a_ref[step, 4 * k + j] = a[j]
            new_a = [
                m0 * a[0] + off * a[2] - excess * a_before[0],
                m0 * a[1] + off * a[3] - excess * a_before[1],
                off * a[0] + m1 * a[2] - excess * a_before[2],
                off * a[1] + m1 * a[3] - excess * a_before[3],
            ]
            a_before, a = (a, new_a)
            psi, psi_before = (mix_ext * psi - excess_ext * psi_before - ext, psi)
            if own:
                slope_rows = 0.5 * (row_up(psi) - row_down(psi))[:, EDGE:-EDGE]
                slope_cols = 0.5 * (col_next(psi) - col_prev(psi))
                shear = [
                    1.0 - 0.5 * (a[0] + a[3]),
                    0.5 * (a[3] - a[0]),
                    -0.5 * (a[1] + a[2]),
                ]
                for j, field in enumerate([slope_rows, slope_cols] + shear):
                    map_ref[step, 5 * k + j] = field
                noise = -0.5 * noise_ref[k, :, start : start + width]
                r = [
                    noise * (shear[j][0:R] - obs_ref[k, j, :, start : start + width])
                    for j in range(3)
                ]
                src_ref[step, 3 * k, 0:R] = r[0] + r[1]
                src_ref[step, 3 * k + 1, 0:R] = r[2]
                src_ref[step, 3 * k + 2, 0:R] = r[0] - r[1]
    none = jnp.zeros((R, width), F32)
    p = [none] * 4
    q = [none] * 4
    for k in reversed(range(planes)):
        s0, s1, s3 = (src_ref[step, 3 * k + j, 0:R] for j in range(3))
        p = [p[0] + s0, p[1] + s1, p[2] + s1, p[3] + s3]
        m0, m1, off = (m_ref[step, 3 * k + j, 0:R] for j in range(3))
        p, q = transposed_step(m0, m1, off, p, q, keeps[k])
    pack_state(b_ref, step, p + q)


def forward_kernel(groups, planes, chunk, length, *refs):
    for step in range(refs[-1].shape[0]):
        forward_block(groups, planes, chunk, length, step, *refs)


def assemble_kernel(*refs):
    maps = refs[:-2]
    defl_ref, shear_ref = refs[-2:]
    steps, width = (maps[0].shape[0], maps[0].shape[-1])
    for c, map_ref in enumerate(maps):
        for i in range(steps):
            start = (c * steps + i) * width
            for k in range(defl_ref.shape[0]):
                for j in range(2):
                    defl_ref[k, j, :, start : start + width] = map_ref[i, 5 * k + j, 0:R]
                for j in range(3):
                    shear_ref[k, j, :, start : start + width] = map_ref[i, 5 * k + 2 + j, 0:R]


def own_tile(ref, k, planes, like):
    tile = ref[ref.shape[0] - planes + k, 0:R]
    return jnp.concatenate([tile] * (like.shape[1] // EDGE), axis=1)


def carry_kernel(planes, sender, in_ref, excess_ref, b_ref, m_ref, out_ref):
    @pl.when(lax.axis_index("plane") == sender)
    def _():
        for step in range(out_ref.shape[0]):
            fields = unpack_state([in_ref], step)
            p, q = (fields[0:4], fields[4:8])
            for k in reversed(range(planes)):
                m0, m1, off = (m_ref[step, 3 * k + j, 0:R] for j in range(3))
                p, q = transposed_step(m0, m1, off, p, q, -own_tile(excess_ref, k, planes, m0))
            pack_state(out_ref, step, p + q, b_ref)


def cotangent_kernel(planes, excess_ref, weight_ref, src_ref, m_ref, a_ref, *refs):
    arrived, cot_ref = (refs[:-1], refs[-1])
    blank = jnp.zeros((SUB - R, cot_ref.shape[-1]), F32)
    for step in range(cot_ref.shape[0]):
        fields = unpack_state(arrived, step)
        p, q = (fields[0:4], fields[4:8])
        for k in reversed(range(planes)):
            s0, s1, s3 = (src_ref[step, 3 * k + j, 0:R] for j in range(3))
            p = [p[0] + s0, p[1] + s1, p[2] + s1, p[3] + s3]
            a = [a_ref[step, 4 * k + j, 0:R] for j in range(4)]
            w = -own_tile(weight_ref, k, planes, s0)
            cots = [
                w * (p[0] * a[0] + p[1] * a[1]),
                w * (p[2] * a[2] + p[3] * a[3]),
                (0.25 * w) * (p[0] * a[2] + p[1] * a[3] + p[2] * a[0] + p[3] * a[1]),
            ]
            for j in range(3):
                cot_ref[step, 3 * k + j] = jnp.concatenate([cots[j], blank], axis=0)
            m0, m1, off = (m_ref[step, 3 * k + j, 0:R] for j in range(3))
            p, q = transposed_step(m0, m1, off, p, q, -own_tile(excess_ref, k, planes, m0))


def stencil_kernel(planes, *refs):
    cots, out_ref = (refs[:-1], refs[-1])
    out = out_ref.shape[-1]
    steps, width = (cots[0].shape[0], cots[0].shape[-1])
    blocks = len(cots) * steps

    def cot(block, field):
        return cots[block // steps].at[block % steps, field]

    for c in range(blocks):
        before = (c - 1) % blocks
        after = (c + 1) % blocks

        def ext(field):
            return jnp.concatenate(
                [
                    cot(before, field)[:, width - EDGE :],
                    cot(c, field)[...],
                    cot(after, field)[:, 0:EDGE],
                ],
                axis=1,
            )

        for k in range(planes):
            cot_rows = cot(c, 3 * k)[...]
            cot_cols = ext(3 * k + 1)
            cot_mixed = ext(3 * k + 2)
            across = row_up(cot_mixed) - row_down(cot_mixed)
            rows_part = row_up(cot_rows) + row_down(cot_rows) - 2.0 * cot_rows
            cols_part = col_next(cot_cols) + col_prev(cot_cols) - 2.0 * cot_cols[:, EDGE:-EDGE]
            grad = rows_part + cols_part + (col_next(across) - col_prev(across))
            for part in range(max(1, width // out)):
                place = c * width + part * out
                size = min(out, width)
                start = place % out
                out_ref[place // out, k, :, start : start + size] = grad[
                    :, part * out : part * out + size
                ]


def combine_kernel(in_ref, out_ref):
    slabs, planes, _, width = in_ref.shape
    blank = jnp.zeros((R - 2, width), F32)
    for k in range(planes):
        for s in range(slabs):
            halo = jnp.concatenate(
                [in_ref[(s - 1) % slabs, k, 6:7], blank, in_ref[(s + 1) % slabs, k, 7:8]], axis=0
            )
            out_ref[k, R * s : R * (s + 1), :] = in_ref[s, k, 0:R] + halo


def shape(*dims):
    return jax.ShapeDtypeStruct(dims, F32)


def params():
    return pltpu.CompilerParams(vmem_limit_bytes=VMEM_LIMIT)


SCALARS = pl.BlockSpec(memory_space=pltpu.SMEM)
WHOLE = pl.BlockSpec(memory_space=pltpu.VMEM)


def on_device(potential, mixing, lens_weight, observed, noise_weight):
    groups = lax.axis_size("plane")
    slabs = lax.axis_size("slab")
    planes, rows, width = potential.shape
    assert rows == R * slabs and width % EDGE == 0
    columns = width * slabs
    tiles = width // EDGE
    length = tiles * slabs // CHUNKS
    span = SPAN * EDGE
    steps = length // SPAN

    def climb(x, hop):
        return lax.ppermute(x, "plane", [(i, i + 1) for i in range(hop, groups - 1)])

    def descend(x, hop):
        return lax.ppermute(x, "plane", [(groups - 1 - hop, groups - 2 - hop)])

    coef = jnp.stack([lens_weight, mixing])
    packed, weights = pl.pallas_call(
        pack_kernel,
        out_shape=(shape(slabs, tiles, planes, SUB, EDGE), shape(planes, SUB, EDGE)),
        in_specs=[SCALARS, WHOLE],
        out_specs=(WHOLE, WHOLE),
        compiler_params=params(),
        name="pack",
    )(coef, potential)
    own = lax.all_to_all(packed, "slab", split_axis=0, concat_axis=0, tiled=True)
    own = own.reshape(slabs * tiles, planes, SUB, EDGE)
    pieces = pl.pallas_call(
        split_kernel,
        out_shape=tuple(
            shape(length + (c == 0), planes, SUB, EDGE) for c in range(CHUNKS)
        ),
        in_specs=[SCALARS, WHOLE],
        out_specs=(WHOLE,) * CHUNKS,
        compiler_params=params(),
        name="split",
    )(coef, own)
    events = [[] for c in range(CHUNKS)]

    def ordered(c, x):
        place = len(events[c]) + 1
        if c < WAVE or place >= len(events[c - WAVE]):
            return x
        return lax.optimization_barrier((x, events[c - WAVE][place]))[0]

    strips = []
    maps = []
    cots = []
    beside, excess = (None, None)
    for c in range(CHUNKS):
        line = [pieces[c]]
        for hop in range(groups - 1):
            line.insert(0, climb(ordered(c, line[0]), hop))
            events[c].append(line[0])
        strips.append(line)
        if c == 0:
            beside, excess = pl.pallas_call(
                edges_kernel,
                out_shape=(
                    shape(CHUNKS, groups * planes, SUB, EDGE),
                    shape(groups * planes, SUB, EDGE),
                ),
                in_specs=[WHOLE] * groups,
                out_specs=(WHOLE, WHOLE),
                compiler_params=params(),
                name="edges",
            )(*line)
        line = [ordered(c, line[0])] + line[1:]
        map_piece, matrices, states, sources, b = pl.pallas_call(
            functools.partial(forward_kernel, groups, planes, c, length),
            out_shape=(
                shape(steps, 5 * planes, SUB, span),
                shape(steps, 3 * planes, SUB, span),
                shape(steps, 4 * planes, SUB, span),
                shape(steps, 3 * planes, SUB, span),
                shape(steps, R, SUB, span),
            ),
            in_specs=[WHOLE] * (groups + 4),
            out_specs=(WHOLE,) * 5,
            compiler_params=params(),
            name="forward",
        )(*line, beside, excess, observed, noise_weight)
        maps.append(map_piece)
        events[c].append(b)
        arrived = [descend(b, 0)]
        for hop in range(1, groups - 1):
            outgoing = pl.pallas_call(
                functools.partial(carry_kernel, planes, groups - 1 - hop),
                out_shape=shape(steps, R, SUB, span),
                in_specs=[WHOLE] * 4,
                out_specs=WHOLE,
                compiler_params=params(),
                name="carry",
            )(ordered(c, arrived[-1]), excess, b, matrices)
            events[c].append(outgoing)
            arrived.append(descend(outgoing, hop))
        cots.append(
            pl.pallas_call(
                functools.partial(cotangent_kernel, planes),
                out_shape=shape(steps, 3 * planes, SUB, span),
                in_specs=[WHOLE] * (groups + 4),
                out_specs=WHOLE,
                compiler_params=params(),
                name="cotangent",
            )(excess, weights, sources, matrices, states, *arrived)
        )
        events[c].append(cots[-1])

    partial = pl.pallas_call(
        functools.partial(stencil_kernel, planes),
        out_shape=shape(slabs, planes, SUB, width),
        in_specs=[WHOLE] * CHUNKS,
        out_specs=WHOLE,
        compiler_params=params(),
        name="stencil",
    )(*cots)
    returned = lax.all_to_all(partial, "slab", split_axis=0, concat_axis=0, tiled=True)
    deflection, shear = pl.pallas_call(
        assemble_kernel,
        out_shape=(shape(planes, 2, R, columns), shape(planes, 3, R, columns)),
        in_specs=[WHOLE] * CHUNKS,
        out_specs=(WHOLE, WHOLE),
        compiler_params=params(),
        name="assemble",
    )(*maps)
    potential_grad = pl.pallas_call(
        combine_kernel,
        out_shape=shape(planes, rows, width),
        in_specs=[WHOLE],
        out_specs=WHOLE,
        compiler_params=params(),
        name="combine",
    )(returned)
    return (deflection, shear, potential_grad)


def solution(mesh):
    placed = (
        P("plane", None, "slab"),
        P("plane"),
        P("plane"),
        P("plane", None, "slab", None),
        P("plane", "slab", None),
    )
    return jax.shard_map(
        on_device,
        mesh=mesh,
        in_specs=placed,
        out_specs=(
            P("plane", None, "slab", None),
            P("plane", None, "slab", None),
            P("plane", None, "slab"),
        ),
        check_vma=False,
    )
```

```python
import functools

import jax
import jax.numpy as jnp
from jax import lax
from jax.experimental import pallas as pl
from jax.experimental.pallas import tpu as pltpu
from jax.sharding import PartitionSpec as P

R = 6
SUB = 8
EDGE = 128
F32 = jnp.float32
VMEM_LIMIT = 16 * 1024 * 1024
CHUNKS = 4
WAVE = 2
SPAN = 4
MIX_LANE = 64


def pack_kernel(coef_ref, p_ref, out_ref, weight_ref):
    planes, rows, width = p_ref.shape
    for k in range(planes):
        w = coef_ref[0, k]
        weight_ref[k] = jnp.full((SUB, EDGE), w, F32)
        for s in range(out_ref.shape[0]):
            before = (R * s - 1) % rows
            after = (R * (s + 1)) % rows
            strip = w * jnp.concatenate(
                [
                    p_ref[k, R * s : R * (s + 1), :],
                    p_ref[k, after : after + 1, :],
                    p_ref[k, before : before + 1, :],
                ],
                axis=0,
            )
            for t in range(width // EDGE):
                out_ref[s, t, k] = strip[:, EDGE * t : EDGE * (t + 1)]


def split_kernel(coef_ref, in_ref, *outs):
    tiles, planes = in_ref.shape[0:2]
    length = tiles // len(outs)
    lane = lax.broadcasted_iota(jnp.int32, (SUB, EDGE), 1)
    for c, out_ref in enumerate(outs):
        out_ref[0:length] = in_ref[length * c : length * (c + 1)]
    for k in range(planes):
        edge = jnp.where(lane == MIX_LANE, coef_ref[1, k] - 1.0, 0.0)
        for c in range(len(outs)):
            after = in_ref[(length * (c + 1)) % tiles, k]
            before = in_ref[(length * c - 1) % tiles, k]
            edge = jnp.where(lane == 2 * c, pltpu.roll(after, 2 * c, 1), edge)
            edge = jnp.where(lane == (2 * c - 1) % EDGE, pltpu.roll(before, 2 * c, 1), edge)
        outs[0][length, k] = edge


def edges_kernel(*refs):
    strips = refs[:-2]
    beside_ref, excess_ref = refs[-2:]
    for group, strip_ref in enumerate(strips):
        planes = strip_ref.shape[1]
        for k in range(planes):
            edge = strip_ref[strip_ref.shape[0] - 1, k]
            at = group * planes + k
            excess_ref[at] = jnp.broadcast_to(edge[:, MIX_LANE : MIX_LANE + 1], edge.shape)
            for c in range(CHUNKS):
                beside_ref[c, at] = pltpu.roll(edge, (EDGE - 2 * c) % EDGE, 1)


def row_up(x):
    return pltpu.roll(x, SUB - 1, 0)


def row_down(x):
    return pltpu.roll(x, 1, 0)


def col_prev(x):
    return pltpu.roll(x, 1, 1)[:, EDGE:-EDGE]


def col_next(x):
    return pltpu.roll(x, x.shape[1] - 1, 1)[:, EDGE:-EDGE]


def transposed_step(m0, m1, off, p, q, keep):
    new_p = [
        m0 * p[0] + off * p[2] + q[0],
        m0 * p[1] + off * p[3] + q[1],
        off * p[0] + m1 * p[2] + q[2],
        off * p[1] + m1 * p[3] + q[3],
    ]
    return (new_p, [keep * x for x in p])


def pack_state(out_ref, step, fields, extra_ref=None):
    for j in range(R):
        tile = jnp.concatenate(
            [fields[j], fields[6][j : j + 1], fields[7][j : j + 1]], axis=0
        )
        out_ref[step, j] = tile if extra_ref is None else tile + extra_ref[step, j]


def unpack_state(arrived, step):
    tiles = [sum(in_ref[step, j] for in_ref in arrived) for j in range(R)]
    fields = [t[0:R] for t in tiles]
    fields.append(jnp.concatenate([t[6:7] for t in tiles], axis=0))
    fields.append(jnp.concatenate([t[7:8] for t in tiles], axis=0))
    return fields


def forward_block(groups, planes, chunk, length, step, *refs):
    strips = refs[:groups]
    beside_ref, excess_ref, obs_ref, noise_ref = refs[groups : groups + 4]
    map_ref, m_ref, a_ref, src_ref, b_ref = refs[-5:]
    width = m_ref.shape[-1]
    span = width // EDGE
    first = step * span
    start = EDGE * (chunk * length + first)
    one = jnp.ones((SUB, width), F32)
    zero = jnp.zeros((SUB, width), F32)
    a = [one, zero, zero, one]
    a_before = a
    psi = jnp.zeros((SUB, width + 2 * EDGE), F32)
    psi_before = psi
    keeps = []
    for group in range(groups):
        strip_ref = strips[group]
        own = group == groups - 1
        for k in range(planes):
            beside = beside_ref[chunk, group * planes + k]
            excess_tile = excess_ref[group * planes + k]
            excess_ext = jnp.concatenate([excess_tile] * (span + 2), axis=1)
            excess = excess_ext[:, EDGE:-EDGE]
            mix_ext = jnp.concatenate([1.0 + excess_tile] * (span + 2), axis=1)
            mix = mix_ext[:, EDGE:-EDGE]
            left = strip_ref[first - 1, k] if first > 0 else beside
            right = strip_ref[first + span, k] if first + span < length else beside
            tiles = [strip_ref[first + t, k] for t in range(span)]
            mid = jnp.concatenate(tiles, axis=1)
            ext = jnp.concatenate([left] + tiles + [right], axis=1)
            up = row_up(ext)
            down = row_down(ext)
            across = up - down
            twice = 2.0 * mid
            m0 = mix - ((up + down)[:, EDGE:-EDGE] - twice)
            m1 = mix - (col_next(ext) + col_prev(ext) - twice)
            off = 0.25 * (col_prev(across) - col_next(across))
            if own:
                m_ref[step, 3 * k] = m0
                m_ref[step, 3 * k + 1] = m1
                m_ref[step, 3 * k + 2] = off
                keeps.append(-excess[0:R])
                for j in range(4):
                    a_ref[step, 4 * k + j] = a[j]
            new_a = [
                m0 * a[0] + off * a[2] - excess * a_before[0],
                m0 * a[1] + off * a[3] - excess * a_before[1],
                off * a[0] + m1 * a[2] - excess * a_before[2],
                off * a[1] + m1 * a[3] - excess * a_before[3],
            ]
            a_before, a = (a, new_a)
            psi, psi_before = (mix_ext * psi - excess_ext * psi_before - ext, psi)
            if own:
                slope_rows = 0.5 * (row_up(psi) - row_down(psi))[:, EDGE:-EDGE]
                slope_cols = 0.5 * (col_next(psi) - col_prev(psi))
                shear = [
                    1.0 - 0.5 * (a[0] + a[3]),
                    0.5 * (a[3] - a[0]),
                    -0.5 * (a[1] + a[2]),
                ]
                for j, field in enumerate([slope_rows, slope_cols] + shear):
                    map_ref[step, 5 * k + j] = field
                noise = -0.5 * noise_ref[k, :, start : start + width]
                r = [
                    noise * (shear[j][0:R] - obs_ref[k, j, :, start : start + width])
                    for j in range(3)
                ]
                src_ref[step, 3 * k, 0:R] = r[0] + r[1]
                src_ref[step, 3 * k + 1, 0:R] = r[2]
                src_ref[step, 3 * k + 2, 0:R] = r[0] - r[1]
    none = jnp.zeros((R, width), F32)
    p = [none] * 4
    q = [none] * 4
    for k in reversed(range(planes)):
        s0, s1, s3 = (src_ref[step, 3 * k + j, 0:R] for j in range(3))
        p = [p[0] + s0, p[1] + s1, p[2] + s1, p[3] + s3]
        m0, m1, off = (m_ref[step, 3 * k + j, 0:R] for j in range(3))
        p, q = transposed_step(m0, m1, off, p, q, keeps[k])
    pack_state(b_ref, step, p + q)


def forward_kernel(groups, planes, chunk, length, *refs):
    for step in range(refs[-1].shape[0]):
        forward_block(groups, planes, chunk, length, step, *refs)


def assemble_kernel(*refs):
    maps = refs[:-2]
    defl_ref, shear_ref = refs[-2:]
    steps, width = (maps[0].shape[0], maps[0].shape[-1])
    for c, map_ref in enumerate(maps):
        for i in range(steps):
            start = (c * steps + i) * width
            for k in range(defl_ref.shape[0]):
                for j in range(2):
                    defl_ref[k, j, :, start : start + width] = map_ref[i, 5 * k + j, 0:R]
                for j in range(3):
                    shear_ref[k, j, :, start : start + width] = map_ref[i, 5 * k + 2 + j, 0:R]


def own_tile(ref, k, planes, like):
    tile = ref[ref.shape[0] - planes + k, 0:R]
    return jnp.concatenate([tile] * (like.shape[1] // EDGE), axis=1)


def carry_kernel(planes, sender, in_ref, excess_ref, b_ref, m_ref, out_ref):
    @pl.when(lax.axis_index("plane") == sender)
    def _():
        for step in range(out_ref.shape[0]):
            fields = unpack_state([in_ref], step)
            p, q = (fields[0:4], fields[4:8])
            for k in reversed(range(planes)):
                m0, m1, off = (m_ref[step, 3 * k + j, 0:R] for j in range(3))
                p, q = transposed_step(m0, m1, off, p, q, -own_tile(excess_ref, k, planes, m0))
            pack_state(out_ref, step, p + q, b_ref)


def cotangent_kernel(planes, excess_ref, weight_ref, src_ref, m_ref, a_ref, *refs):
    arrived, cot_ref = (refs[:-1], refs[-1])
    blank = jnp.zeros((SUB - R, cot_ref.shape[-1]), F32)
    for step in range(cot_ref.shape[0]):
        fields = unpack_state(arrived, step)
        p, q = (fields[0:4], fields[4:8])
        for k in reversed(range(planes)):
            s0, s1, s3 = (src_ref[step, 3 * k + j, 0:R] for j in range(3))
            p = [p[0] + s0, p[1] + s1, p[2] + s1, p[3] + s3]
            a = [a_ref[step, 4 * k + j, 0:R] for j in range(4)]
            w = -own_tile(weight_ref, k, planes, s0)
            cots = [
                w * (p[0] * a[0] + p[1] * a[1]),
                w * (p[2] * a[2] + p[3] * a[3]),
                (0.25 * w) * (p[0] * a[2] + p[1] * a[3] + p[2] * a[0] + p[3] * a[1]),
            ]
            for j in range(3):
                cot_ref[step, 3 * k + j] = jnp.concatenate([cots[j], blank], axis=0)
            m0, m1, off = (m_ref[step, 3 * k + j, 0:R] for j in range(3))
            p, q = transposed_step(m0, m1, off, p, q, -own_tile(excess_ref, k, planes, m0))


def stencil_kernel(planes, *refs):
    cots, out_ref = (refs[:-1], refs[-1])
    out = out_ref.shape[-1]
    steps, width = (cots[0].shape[0], cots[0].shape[-1])
    blocks = len(cots) * steps

    def cot(block, field):
        return cots[block // steps].at[block % steps, field]

    for c in range(blocks):
        before = (c - 1) % blocks
        after = (c + 1) % blocks

        def ext(field):
            return jnp.concatenate(
                [
                    cot(before, field)[:, width - EDGE :],
                    cot(c, field)[...],
                    cot(after, field)[:, 0:EDGE],
                ],
                axis=1,
            )

        for k in range(planes):
            cot_rows = cot(c, 3 * k)[...]
            cot_cols = ext(3 * k + 1)
            cot_mixed = ext(3 * k + 2)
            across = row_up(cot_mixed) - row_down(cot_mixed)
            rows_part = row_up(cot_rows) + row_down(cot_rows) - 2.0 * cot_rows
            cols_part = col_next(cot_cols) + col_prev(cot_cols) - 2.0 * cot_cols[:, EDGE:-EDGE]
            grad = rows_part + cols_part + (col_next(across) - col_prev(across))
            for part in range(max(1, width // out)):
                place = c * width + part * out
                size = min(out, width)
                start = place % out
                out_ref[place // out, k, :, start : start + size] = grad[
                    :, part * out : part * out + size
                ]


def combine_kernel(in_ref, out_ref):
    slabs, planes, _, width = in_ref.shape
    blank = jnp.zeros((R - 2, width), F32)
    for k in range(planes):
        for s in range(slabs):
            halo = jnp.concatenate(
                [in_ref[(s - 1) % slabs, k, 6:7], blank, in_ref[(s + 1) % slabs, k, 7:8]], axis=0
            )
            out_ref[k, R * s : R * (s + 1), :] = in_ref[s, k, 0:R] + halo


def shape(*dims):
    return jax.ShapeDtypeStruct(dims, F32)


def params():
    return pltpu.CompilerParams(vmem_limit_bytes=VMEM_LIMIT)


SCALARS = pl.BlockSpec(memory_space=pltpu.SMEM)
WHOLE = pl.BlockSpec(memory_space=pltpu.VMEM)


def on_device(potential, mixing, lens_weight, observed, noise_weight):
    groups = lax.axis_size("plane")
    slabs = lax.axis_size("slab")
    planes, rows, width = potential.shape
    assert rows == R * slabs and width % EDGE == 0
    columns = width * slabs
    tiles = width // EDGE
    length = tiles * slabs // CHUNKS
    span = SPAN * EDGE
    steps = length // SPAN

    def climb(x, hop):
        return lax.ppermute(x, "plane", [(i, i + 1) for i in range(hop, groups - 1)])

    def descend(x, hop):
        return lax.ppermute(x, "plane", [(groups - 1 - hop, groups - 2 - hop)])

    coef = jnp.stack([lens_weight, mixing])
    packed, weights = pl.pallas_call(
        pack_kernel,
        out_shape=(shape(slabs, tiles, planes, SUB, EDGE), shape(planes, SUB, EDGE)),
        in_specs=[SCALARS, WHOLE],
        out_specs=(WHOLE, WHOLE),
        compiler_params=params(),
        name="pack",
    )(coef, potential)
    own = lax.all_to_all(packed, "slab", split_axis=0, concat_axis=0, tiled=True)
    own = own.reshape(slabs * tiles, planes, SUB, EDGE)
    pieces = pl.pallas_call(
        split_kernel,
        out_shape=tuple(
            shape(length + (c == 0), planes, SUB, EDGE) for c in range(CHUNKS)
        ),
        in_specs=[SCALARS, WHOLE],
        out_specs=(WHOLE,) * CHUNKS,
        compiler_params=params(),
        name="split",
    )(coef, own)
    strips = [[piece] for piece in pieces]
    for turn in range(CHUNKS + groups - 2):
        for c in range(CHUNKS):
            if 0 <= turn - c < groups - 1:
                strips[c].insert(0, climb(strips[c][0], turn - c))
    beside, excess = pl.pallas_call(
        edges_kernel,
        out_shape=(
            shape(CHUNKS, groups * planes, SUB, EDGE),
            shape(groups * planes, SUB, EDGE),
        ),
        in_specs=[WHOLE] * groups,
        out_specs=(WHOLE, WHOLE),
        compiler_params=params(),
        name="edges",
    )(*strips[0])

    sequence = list(reversed(range(2, CHUNKS))) + [0, 1]
    maps = [None] * CHUNKS
    work = [None] * CHUNKS
    for c in sequence:
        if c == 1:
            strips[1][0] = lax.optimization_barrier((strips[1][0], work[0][-1]))[0]
        maps[c], *work[c] = pl.pallas_call(
            functools.partial(forward_kernel, groups, planes, c, length),
            out_shape=(
                shape(steps, 5 * planes, SUB, span),
                shape(steps, 3 * planes, SUB, span),
                shape(steps, 4 * planes, SUB, span),
                shape(steps, 3 * planes, SUB, span),
                shape(steps, R, SUB, span),
            ),
            in_specs=[WHOLE] * (groups + 4),
            out_specs=(WHOLE,) * 5,
            compiler_params=params(),
            name="forward",
        )(*strips[c], beside, excess, observed, noise_weight)

    events = [[] for c in range(CHUNKS)]
    cots = [None] * CHUNKS
    for place, c in enumerate(sequence):
        matrices, states, sources, b = work[c]
        arrived = [descend(b, 0)]
        for hop in range(1, groups - 1):
            incoming = arrived[-1]
            if place >= WAVE:
                ahead = events[sequence[place - WAVE]]
                incoming = lax.optimization_barrier((incoming, ahead[hop]))[0]
            outgoing = pl.pallas_call(
                functools.partial(carry_kernel, planes, groups - 1 - hop),
                out_shape=shape(steps, R, SUB, span),
                in_specs=[WHOLE] * 4,
                out_specs=WHOLE,
                compiler_params=params(),
                name="carry",
            )(incoming, excess, b, matrices)
            events[c].append(outgoing)
            arrived.append(descend(outgoing, hop))
        cots[c] = pl.pallas_call(
            functools.partial(cotangent_kernel, planes),
            out_shape=shape(steps, 3 * planes, SUB, span),
            in_specs=[WHOLE] * (groups + 4),
            out_specs=WHOLE,
            compiler_params=params(),
            name="cotangent",
        )(excess, weights, sources, matrices, states, *arrived)
        events[c].append(cots[c])

    partial = pl.pallas_call(
        functools.partial(stencil_kernel, planes),
        out_shape=shape(slabs, planes, SUB, width),
        in_specs=[WHOLE] * CHUNKS,
        out_specs=WHOLE,
        compiler_params=params(),
        name="stencil",
    )(*cots)
    returned = lax.all_to_all(partial, "slab", split_axis=0, concat_axis=0, tiled=True)
    deflection, shear = pl.pallas_call(
        assemble_kernel,
        out_shape=(shape(planes, 2, R, columns), shape(planes, 3, R, columns)),
        in_specs=[WHOLE] * CHUNKS,
        out_specs=(WHOLE, WHOLE),
        compiler_params=params(),
        name="assemble",
    )(*maps)
    potential_grad = pl.pallas_call(
        combine_kernel,
        out_shape=shape(planes, rows, width),
        in_specs=[WHOLE],
        out_specs=WHOLE,
        compiler_params=params(),
        name="combine",
    )(returned)
    return (deflection, shear, potential_grad)


def solution(mesh):
    placed = (
        P("plane", None, "slab"),
        P("plane"),
        P("plane"),
        P("plane", None, "slab", None),
        P("plane", "slab", None),
    )
    return jax.shard_map(
        on_device,
        mesh=mesh,
        in_specs=placed,
        out_specs=(
            P("plane", None, "slab", None),
            P("plane", None, "slab", None),
            P("plane", None, "slab"),
        ),
        check_vma=False,
    )
```

```python
import functools

import jax
import jax.numpy as jnp
from jax import lax
from jax.experimental import pallas as pl
from jax.experimental.pallas import tpu as pltpu
from jax.sharding import PartitionSpec as P

R = 6
SUB = 8
EDGE = 128
F32 = jnp.float32
VMEM_LIMIT = 16 * 1024 * 1024
CHUNKS = 4
WAVE = 2
SPAN = 4
MIX_LANE = 64


def pack_kernel(coef_ref, p_ref, out_ref, weight_ref):
    planes, rows, width = p_ref.shape
    for k in range(planes):
        w = coef_ref[0, k]
        weight_ref[k] = jnp.full((SUB, EDGE), w, F32)
        for s in range(out_ref.shape[0]):
            before = (R * s - 1) % rows
            after = (R * (s + 1)) % rows
            strip = w * jnp.concatenate(
                [
                    p_ref[k, R * s : R * (s + 1), :],
                    p_ref[k, after : after + 1, :],
                    p_ref[k, before : before + 1, :],
                ],
                axis=0,
            )
            for t in range(width // EDGE):
                out_ref[s, t, k] = strip[:, EDGE * t : EDGE * (t + 1)]


def split_kernel(coef_ref, in_ref, *outs):
    tiles, planes = in_ref.shape[0:2]
    length = tiles // len(outs)
    lane = lax.broadcasted_iota(jnp.int32, (SUB, EDGE), 1)
    for c, out_ref in enumerate(outs):
        out_ref[0:length] = in_ref[length * c : length * (c + 1)]
    for k in range(planes):
        edge = jnp.where(lane == MIX_LANE, coef_ref[1, k] - 1.0, 0.0)
        for c in range(len(outs)):
            after = in_ref[(length * (c + 1)) % tiles, k]
            before = in_ref[(length * c - 1) % tiles, k]
            edge = jnp.where(lane == 2 * c, pltpu.roll(after, 2 * c, 1), edge)
            edge = jnp.where(lane == (2 * c - 1) % EDGE, pltpu.roll(before, 2 * c, 1), edge)
        outs[0][length, k] = edge


def edges_kernel(*refs):
    strips = refs[:-2]
    beside_ref, excess_ref = refs[-2:]
    for group, strip_ref in enumerate(strips):
        planes = strip_ref.shape[1]
        for k in range(planes):
            edge = strip_ref[strip_ref.shape[0] - 1, k]
            at = group * planes + k
            excess_ref[at] = jnp.broadcast_to(edge[:, MIX_LANE : MIX_LANE + 1], edge.shape)
            for c in range(CHUNKS):
                beside_ref[c, at] = pltpu.roll(edge, (EDGE - 2 * c) % EDGE, 1)


def row_up(x):
    return pltpu.roll(x, SUB - 1, 0)


def row_down(x):
    return pltpu.roll(x, 1, 0)


def col_prev(x):
    return pltpu.roll(x, 1, 1)[:, EDGE:-EDGE]


def col_next(x):
    return pltpu.roll(x, x.shape[1] - 1, 1)[:, EDGE:-EDGE]


def transposed_step(m0, m1, off, p, q, keep):
    new_p = [
        m0 * p[0] + off * p[2] + q[0],
        m0 * p[1] + off * p[3] + q[1],
        off * p[0] + m1 * p[2] + q[2],
        off * p[1] + m1 * p[3] + q[3],
    ]
    return (new_p, [keep * x for x in p])


def pack_state(out_ref, step, fields, extra_ref=None):
    for j in range(R):
        tile = jnp.concatenate(
            [fields[j], fields[6][j : j + 1], fields[7][j : j + 1]], axis=0
        )
        out_ref[step, j] = tile if extra_ref is None else tile + extra_ref[step, j]


def unpack_state(arrived, step):
    tiles = [sum(in_ref[step, j] for in_ref in arrived) for j in range(R)]
    fields = [t[0:R] for t in tiles]
    fields.append(jnp.concatenate([t[6:7] for t in tiles], axis=0))
    fields.append(jnp.concatenate([t[7:8] for t in tiles], axis=0))
    return fields


def forward_block(groups, planes, chunk, length, step, *refs):
    strips = refs[:groups]
    beside_ref, excess_ref, obs_ref, noise_ref = refs[groups : groups + 4]
    map_ref, m_ref, a_ref, src_ref, b_ref = refs[-5:]
    width = m_ref.shape[-1]
    span = width // EDGE
    first = step * span
    start = EDGE * (chunk * length + first)
    one = jnp.ones((SUB, width), F32)
    zero = jnp.zeros((SUB, width), F32)
    a = [one, zero, zero, one]
    a_before = a
    psi = jnp.zeros((SUB, width + 2 * EDGE), F32)
    psi_before = psi
    keeps = []
    for group in range(groups):
        strip_ref = strips[group]
        own = group == groups - 1
        for k in range(planes):
            beside = beside_ref[chunk, group * planes + k]
            excess_tile = excess_ref[group * planes + k]
            excess_ext = jnp.concatenate([excess_tile] * (span + 2), axis=1)
            excess = excess_ext[:, EDGE:-EDGE]
            mix_ext = jnp.concatenate([1.0 + excess_tile] * (span + 2), axis=1)
            mix = mix_ext[:, EDGE:-EDGE]
            left = strip_ref[first - 1, k] if first > 0 else beside
            right = strip_ref[first + span, k] if first + span < length else beside
            tiles = [strip_ref[first + t, k] for t in range(span)]
            mid = jnp.concatenate(tiles, axis=1)
            ext = jnp.concatenate([left] + tiles + [right], axis=1)
            up = row_up(ext)
            down = row_down(ext)
            across = up - down
            twice = 2.0 * mid
            m0 = mix - ((up + down)[:, EDGE:-EDGE] - twice)
            m1 = mix - (col_next(ext) + col_prev(ext) - twice)
            off = 0.25 * (col_prev(across) - col_next(across))
            if own:
                m_ref[step, 3 * k] = m0
                m_ref[step, 3 * k + 1] = m1
                m_ref[step, 3 * k + 2] = off
                keeps.append(-excess[0:R])
                for j in range(4):
                    a_ref[step, 4 * k + j] = a[j]
            new_a = [
                m0 * a[0] + off * a[2] - excess * a_before[0],
                m0 * a[1] + off * a[3] - excess * a_before[1],
                off * a[0] + m1 * a[2] - excess * a_before[2],
                off * a[1] + m1 * a[3] - excess * a_before[3],
            ]
            a_before, a = (a, new_a)
            psi, psi_before = (mix_ext * psi - excess_ext * psi_before - ext, psi)
            if own:
                slope_rows = 0.5 * (row_up(psi) - row_down(psi))[:, EDGE:-EDGE]
                slope_cols = 0.5 * (col_next(psi) - col_prev(psi))
                shear = [
                    1.0 - 0.5 * (a[0] + a[3]),
                    0.5 * (a[3] - a[0]),
                    -0.5 * (a[1] + a[2]),
                ]
                for j, field in enumerate([slope_rows, slope_cols] + shear):
                    map_ref[step, 5 * k + j] = field
                noise = -0.5 * noise_ref[k, :, start : start + width]
                r = [
                    noise * (shear[j][0:R] - obs_ref[k, j, :, start : start + width])
                    for j in range(3)
                ]
                src_ref[step, 3 * k, 0:R] = r[0] + r[1]
                src_ref[step, 3 * k + 1, 0:R] = r[2]
                src_ref[step, 3 * k + 2, 0:R] = r[0] - r[1]
    none = jnp.zeros((R, width), F32)
    p = [none] * 4
    q = [none] * 4
    for k in reversed(range(planes)):
        s0, s1, s3 = (src_ref[step, 3 * k + j, 0:R] for j in range(3))
        p = [p[0] + s0, p[1] + s1, p[2] + s1, p[3] + s3]
        m0, m1, off = (m_ref[step, 3 * k + j, 0:R] for j in range(3))
        p, q = transposed_step(m0, m1, off, p, q, keeps[k])
    pack_state(b_ref, step, p + q)


def forward_kernel(groups, planes, chunk, length, *refs):
    for step in range(refs[-1].shape[0]):
        forward_block(groups, planes, chunk, length, step, *refs)


def assemble_kernel(*refs):
    maps = refs[:-2]
    defl_ref, shear_ref = refs[-2:]
    steps, width = (maps[0].shape[0], maps[0].shape[-1])
    for c, map_ref in enumerate(maps):
        for i in range(steps):
            start = (c * steps + i) * width
            for k in range(defl_ref.shape[0]):
                for j in range(2):
                    defl_ref[k, j, :, start : start + width] = map_ref[i, 5 * k + j, 0:R]
                for j in range(3):
                    shear_ref[k, j, :, start : start + width] = map_ref[i, 5 * k + 2 + j, 0:R]


def own_tile(ref, k, planes, like):
    tile = ref[ref.shape[0] - planes + k, 0:R]
    return jnp.concatenate([tile] * (like.shape[1] // EDGE), axis=1)


def carry_kernel(planes, sender, in_ref, excess_ref, b_ref, m_ref, out_ref):
    @pl.when(lax.axis_index("plane") == sender)
    def _():
        for step in range(out_ref.shape[0]):
            fields = unpack_state([in_ref], step)
            p, q = (fields[0:4], fields[4:8])
            for k in reversed(range(planes)):
                m0, m1, off = (m_ref[step, 3 * k + j, 0:R] for j in range(3))
                p, q = transposed_step(m0, m1, off, p, q, -own_tile(excess_ref, k, planes, m0))
            pack_state(out_ref, step, p + q, b_ref)


def cotangent_kernel(planes, excess_ref, weight_ref, src_ref, m_ref, a_ref, *refs):
    arrived, cot_ref = (refs[:-1], refs[-1])
    blank = jnp.zeros((SUB - R, cot_ref.shape[-1]), F32)
    for step in range(cot_ref.shape[0]):
        fields = unpack_state(arrived, step)
        p, q = (fields[0:4], fields[4:8])
        for k in reversed(range(planes)):
            s0, s1, s3 = (src_ref[step, 3 * k + j, 0:R] for j in range(3))
            p = [p[0] + s0, p[1] + s1, p[2] + s1, p[3] + s3]
            a = [a_ref[step, 4 * k + j, 0:R] for j in range(4)]
            w = -own_tile(weight_ref, k, planes, s0)
            cots = [
                w * (p[0] * a[0] + p[1] * a[1]),
                w * (p[2] * a[2] + p[3] * a[3]),
                (0.25 * w) * (p[0] * a[2] + p[1] * a[3] + p[2] * a[0] + p[3] * a[1]),
            ]
            for j in range(3):
                cot_ref[step, 3 * k + j] = jnp.concatenate([cots[j], blank], axis=0)
            m0, m1, off = (m_ref[step, 3 * k + j, 0:R] for j in range(3))
            p, q = transposed_step(m0, m1, off, p, q, -own_tile(excess_ref, k, planes, m0))


def stencil_kernel(planes, *refs):
    cots, out_ref = (refs[:-1], refs[-1])
    out = out_ref.shape[-1]
    steps, width = (cots[0].shape[0], cots[0].shape[-1])
    blocks = len(cots) * steps

    def cot(block, field):
        return cots[block // steps].at[block % steps, field]

    for c in range(blocks):
        before = (c - 1) % blocks
        after = (c + 1) % blocks

        def ext(field):
            return jnp.concatenate(
                [
                    cot(before, field)[:, width - EDGE :],
                    cot(c, field)[...],
                    cot(after, field)[:, 0:EDGE],
                ],
                axis=1,
            )

        for k in range(planes):
            cot_rows = cot(c, 3 * k)[...]
            cot_cols = ext(3 * k + 1)
            cot_mixed = ext(3 * k + 2)
            across = row_up(cot_mixed) - row_down(cot_mixed)
            rows_part = row_up(cot_rows) + row_down(cot_rows) - 2.0 * cot_rows
            cols_part = col_next(cot_cols) + col_prev(cot_cols) - 2.0 * cot_cols[:, EDGE:-EDGE]
            grad = rows_part + cols_part + (col_next(across) - col_prev(across))
            for part in range(max(1, width // out)):
                place = c * width + part * out
                size = min(out, width)
                start = place % out
                out_ref[place // out, k, :, start : start + size] = grad[
                    :, part * out : part * out + size
                ]


def combine_kernel(in_ref, out_ref):
    slabs, planes, _, width = in_ref.shape
    blank = jnp.zeros((R - 2, width), F32)
    for k in range(planes):
        for s in range(slabs):
            halo = jnp.concatenate(
                [in_ref[(s - 1) % slabs, k, 6:7], blank, in_ref[(s + 1) % slabs, k, 7:8]], axis=0
            )
            out_ref[k, R * s : R * (s + 1), :] = in_ref[s, k, 0:R] + halo


def shape(*dims):
    return jax.ShapeDtypeStruct(dims, F32)


def params():
    return pltpu.CompilerParams(vmem_limit_bytes=VMEM_LIMIT)


SCALARS = pl.BlockSpec(memory_space=pltpu.SMEM)
WHOLE = pl.BlockSpec(memory_space=pltpu.VMEM)


def on_device(potential, mixing, lens_weight, observed, noise_weight):
    groups = lax.axis_size("plane")
    slabs = lax.axis_size("slab")
    planes, rows, width = potential.shape
    assert rows == R * slabs and width % EDGE == 0
    columns = width * slabs
    tiles = width // EDGE
    length = tiles * slabs // CHUNKS
    span = SPAN * EDGE
    steps = length // SPAN

    def climb(x, hop):
        return lax.ppermute(x, "plane", [(i, i + 1) for i in range(hop, groups - 1)])

    def descend(x, hop):
        return lax.ppermute(x, "plane", [(groups - 1 - hop, groups - 2 - hop)])

    coef = jnp.stack([lens_weight, mixing])
    packed, weights = pl.pallas_call(
        pack_kernel,
        out_shape=(shape(slabs, tiles, planes, SUB, EDGE), shape(planes, SUB, EDGE)),
        in_specs=[SCALARS, WHOLE],
        out_specs=(WHOLE, WHOLE),
        compiler_params=params(),
        name="pack",
    )(coef, potential)
    own = lax.all_to_all(packed, "slab", split_axis=0, concat_axis=0, tiled=True)
    own = own.reshape(slabs * tiles, planes, SUB, EDGE)
    pieces = pl.pallas_call(
        split_kernel,
        out_shape=tuple(
            shape(length + (c == 0), planes, SUB, EDGE) for c in range(CHUNKS)
        ),
        in_specs=[SCALARS, WHOLE],
        out_specs=(WHOLE,) * CHUNKS,
        compiler_params=params(),
        name="split",
    )(coef, own)
    strips = [[piece] for piece in pieces]
    for turn in range(CHUNKS + groups - 2):
        for c in range(CHUNKS):
            if 0 <= turn - c < groups - 1:
                strips[c].insert(0, climb(strips[c][0], turn - c))
    beside, excess = pl.pallas_call(
        edges_kernel,
        out_shape=(
            shape(CHUNKS, groups * planes, SUB, EDGE),
            shape(groups * planes, SUB, EDGE),
        ),
        in_specs=[WHOLE] * groups,
        out_specs=(WHOLE, WHOLE),
        compiler_params=params(),
        name="edges",
    )(*strips[0])

    sequence = list(reversed(range(2, CHUNKS))) + [0, 1]
    maps = [None] * CHUNKS
    work = [None] * CHUNKS
    for c in sequence:
        if c == 1:
            strips[1][0] = lax.optimization_barrier((strips[1][0], work[0][-1]))[0]
        maps[c], *work[c] = pl.pallas_call(
            functools.partial(forward_kernel, groups, planes, c, length),
            out_shape=(
                shape(steps, 5 * planes, SUB, span),
                shape(steps, 3 * planes, SUB, span),
                shape(steps, 4 * planes, SUB, span),
                shape(steps, 3 * planes, SUB, span),
                shape(steps, R, SUB, span),
            ),
            in_specs=[WHOLE] * (groups + 4),
            out_specs=(WHOLE,) * 5,
            compiler_params=params(),
            name="forward",
        )(*strips[c], beside, excess, observed, noise_weight)

    events = [[] for c in range(CHUNKS)]
    cots = [None] * CHUNKS
    for place, c in enumerate(sequence):
        matrices, states, sources, b = work[c]
        arrived = [descend(b, 0)]
        for hop in range(1, groups - 1):
            incoming = arrived[-1]
            if place > 0:
                ahead = events[sequence[place - 1]]
                incoming = lax.optimization_barrier((incoming, ahead[hop - 1]))[0]
            if place >= WAVE:
                ahead = events[sequence[place - WAVE]]
                incoming = lax.optimization_barrier((incoming, ahead[hop]))[0]
            outgoing = pl.pallas_call(
                functools.partial(carry_kernel, planes, groups - 1 - hop),
                out_shape=shape(steps, R, SUB, span),
                in_specs=[WHOLE] * 4,
                out_specs=WHOLE,
                compiler_params=params(),
                name="carry",
            )(incoming, excess, b, matrices)
            events[c].append(outgoing)
            arrived.append(descend(outgoing, hop))
        if place > 0:
            ahead = cots[sequence[place - 1]]
            arrived[-1] = lax.optimization_barrier((arrived[-1], ahead))[0]
        cots[c] = pl.pallas_call(
            functools.partial(cotangent_kernel, planes),
            out_shape=shape(steps, 3 * planes, SUB, span),
            in_specs=[WHOLE] * (groups + 4),
            out_specs=WHOLE,
            compiler_params=params(),
            name="cotangent",
        )(excess, weights, sources, matrices, states, *arrived)
        events[c].append(cots[c])

    partial = pl.pallas_call(
        functools.partial(stencil_kernel, planes),
        out_shape=shape(slabs, planes, SUB, width),
        in_specs=[WHOLE] * CHUNKS,
        out_specs=WHOLE,
        compiler_params=params(),
        name="stencil",
    )(*cots)
    returned = lax.all_to_all(partial, "slab", split_axis=0, concat_axis=0, tiled=True)
    deflection, shear = pl.pallas_call(
        assemble_kernel,
        out_shape=(shape(planes, 2, R, columns), shape(planes, 3, R, columns)),
        in_specs=[WHOLE] * CHUNKS,
        out_specs=(WHOLE, WHOLE),
        compiler_params=params(),
        name="assemble",
    )(*maps)
    potential_grad = pl.pallas_call(
        combine_kernel,
        out_shape=shape(planes, rows, width),
        in_specs=[WHOLE],
        out_specs=WHOLE,
        compiler_params=params(),
        name="combine",
    )(returned)
    return (deflection, shear, potential_grad)


def solution(mesh):
    placed = (
        P("plane", None, "slab"),
        P("plane"),
        P("plane"),
        P("plane", None, "slab", None),
        P("plane", "slab", None),
    )
    return jax.shard_map(
        on_device,
        mesh=mesh,
        in_specs=placed,
        out_specs=(
            P("plane", None, "slab", None),
            P("plane", None, "slab", None),
            P("plane", None, "slab"),
        ),
        check_vma=False,
    )
```

```python
import functools

import jax
import jax.numpy as jnp
from jax import lax
from jax.experimental import pallas as pl
from jax.experimental.pallas import tpu as pltpu
from jax.sharding import PartitionSpec as P

R = 6
SUB = 8
EDGE = 128
F32 = jnp.float32
VMEM_LIMIT = 16 * 1024 * 1024
CHUNKS = 4
SPAN = 4
MIX_LANE = 64


def pack_kernel(coef_ref, p_ref, out_ref, weight_ref):
    planes, rows, width = p_ref.shape
    for k in range(planes):
        w = coef_ref[0, k]
        weight_ref[k] = jnp.full((SUB, EDGE), w, F32)
        for s in range(out_ref.shape[0]):
            before = (R * s - 1) % rows
            after = (R * (s + 1)) % rows
            strip = w * jnp.concatenate(
                [
                    p_ref[k, R * s : R * (s + 1), :],
                    p_ref[k, after : after + 1, :],
                    p_ref[k, before : before + 1, :],
                ],
                axis=0,
            )
            for t in range(width // EDGE):
                out_ref[s, t, k] = strip[:, EDGE * t : EDGE * (t + 1)]


def split_kernel(coef_ref, in_ref, *outs):
    tiles, planes = in_ref.shape[0:2]
    length = tiles // len(outs)
    lane = lax.broadcasted_iota(jnp.int32, (SUB, EDGE), 1)
    for c, out_ref in enumerate(outs):
        out_ref[0:length] = in_ref[length * c : length * (c + 1)]
    for k in range(planes):
        edge = jnp.where(lane == MIX_LANE, coef_ref[1, k] - 1.0, 0.0)
        for c in range(len(outs)):
            after = in_ref[(length * (c + 1)) % tiles, k]
            before = in_ref[(length * c - 1) % tiles, k]
            edge = jnp.where(lane == 2 * c, pltpu.roll(after, 2 * c, 1), edge)
            edge = jnp.where(lane == (2 * c - 1) % EDGE, pltpu.roll(before, 2 * c, 1), edge)
        outs[0][length, k] = edge


def edges_kernel(*refs):
    strips = refs[:-2]
    beside_ref, excess_ref = refs[-2:]
    for group, strip_ref in enumerate(strips):
        planes = strip_ref.shape[1]
        for k in range(planes):
            edge = strip_ref[strip_ref.shape[0] - 1, k]
            at = group * planes + k
            excess_ref[at] = jnp.broadcast_to(edge[:, MIX_LANE : MIX_LANE + 1], edge.shape)
            for c in range(CHUNKS):
                beside_ref[c, at] = pltpu.roll(edge, (EDGE - 2 * c) % EDGE, 1)


def row_up(x):
    return pltpu.roll(x, SUB - 1, 0)


def row_down(x):
    return pltpu.roll(x, 1, 0)


def col_prev(x):
    return pltpu.roll(x, 1, 1)[:, EDGE:-EDGE]


def col_next(x):
    return pltpu.roll(x, x.shape[1] - 1, 1)[:, EDGE:-EDGE]


def transposed_step(m0, m1, off, p, q, keep):
    new_p = [
        m0 * p[0] + off * p[2] + q[0],
        m0 * p[1] + off * p[3] + q[1],
        off * p[0] + m1 * p[2] + q[2],
        off * p[1] + m1 * p[3] + q[3],
    ]
    return (new_p, [keep * x for x in p])


def pack_state(out_ref, step, fields, extra_ref=None):
    for j in range(R):
        tile = jnp.concatenate(
            [fields[j], fields[6][j : j + 1], fields[7][j : j + 1]], axis=0
        )
        out_ref[step, j] = tile if extra_ref is None else tile + extra_ref[step, j]


def unpack_state(arrived, step):
    tiles = [sum(in_ref[step, j] for in_ref in arrived) for j in range(R)]
    fields = [t[0:R] for t in tiles]
    fields.append(jnp.concatenate([t[6:7] for t in tiles], axis=0))
    fields.append(jnp.concatenate([t[7:8] for t in tiles], axis=0))
    return fields


def forward_block(groups, planes, chunk, length, step, *refs):
    strips = refs[:groups]
    beside_ref, excess_ref, obs_ref, noise_ref = refs[groups : groups + 4]
    map_ref, m_ref, a_ref, src_ref, b_ref = refs[-5:]
    width = m_ref.shape[-1]
    span = width // EDGE
    first = step * span
    start = EDGE * (chunk * length + first)
    one = jnp.ones((SUB, width), F32)
    zero = jnp.zeros((SUB, width), F32)
    a = [one, zero, zero, one]
    a_before = a
    psi = jnp.zeros((SUB, width + 2 * EDGE), F32)
    psi_before = psi
    keeps = []
    for group in range(groups):
        strip_ref = strips[group]
        own = group == groups - 1
        for k in range(planes):
            beside = beside_ref[chunk, group * planes + k]
            excess_tile = excess_ref[group * planes + k]
            excess_ext = jnp.concatenate([excess_tile] * (span + 2), axis=1)
            excess = excess_ext[:, EDGE:-EDGE]
            mix_ext = jnp.concatenate([1.0 + excess_tile] * (span + 2), axis=1)
            mix = mix_ext[:, EDGE:-EDGE]
            left = strip_ref[first - 1, k] if first > 0 else beside
            right = strip_ref[first + span, k] if first + span < length else beside
            tiles = [strip_ref[first + t, k] for t in range(span)]
            mid = jnp.concatenate(tiles, axis=1)
            ext = jnp.concatenate([left] + tiles + [right], axis=1)
            up = row_up(ext)
            down = row_down(ext)
            across = up - down
            twice = 2.0 * mid
            m0 = mix - ((up + down)[:, EDGE:-EDGE] - twice)
            m1 = mix - (col_next(ext) + col_prev(ext) - twice)
            off = 0.25 * (col_prev(across) - col_next(across))
            if own:
                m_ref[step, 3 * k] = m0
                m_ref[step, 3 * k + 1] = m1
                m_ref[step, 3 * k + 2] = off
                keeps.append(-excess[0:R])
                for j in range(4):
                    a_ref[step, 4 * k + j] = a[j]
            new_a = [
                m0 * a[0] + off * a[2] - excess * a_before[0],
                m0 * a[1] + off * a[3] - excess * a_before[1],
                off * a[0] + m1 * a[2] - excess * a_before[2],
                off * a[1] + m1 * a[3] - excess * a_before[3],
            ]
            a_before, a = (a, new_a)
            psi, psi_before = (mix_ext * psi - excess_ext * psi_before - ext, psi)
            if own:
                slope_rows = 0.5 * (row_up(psi) - row_down(psi))[:, EDGE:-EDGE]
                slope_cols = 0.5 * (col_next(psi) - col_prev(psi))
                shear = [
                    1.0 - 0.5 * (a[0] + a[3]),
                    0.5 * (a[3] - a[0]),
                    -0.5 * (a[1] + a[2]),
                ]
                for j, field in enumerate([slope_rows, slope_cols] + shear):
                    map_ref[step, 5 * k + j] = field
                noise = -0.5 * noise_ref[k, :, start : start + width]
                r = [
                    noise * (shear[j][0:R] - obs_ref[k, j, :, start : start + width])
                    for j in range(3)
                ]
                src_ref[step, 3 * k, 0:R] = r[0] + r[1]
                src_ref[step, 3 * k + 1, 0:R] = r[2]
                src_ref[step, 3 * k + 2, 0:R] = r[0] - r[1]
    none = jnp.zeros((R, width), F32)
    p = [none] * 4
    q = [none] * 4
    for k in reversed(range(planes)):
        s0, s1, s3 = (src_ref[step, 3 * k + j, 0:R] for j in range(3))
        p = [p[0] + s0, p[1] + s1, p[2] + s1, p[3] + s3]
        m0, m1, off = (m_ref[step, 3 * k + j, 0:R] for j in range(3))
        p, q = transposed_step(m0, m1, off, p, q, keeps[k])
    pack_state(b_ref, step, p + q)


def forward_kernel(groups, planes, chunk, length, *refs):
    for step in range(refs[-1].shape[0]):
        forward_block(groups, planes, chunk, length, step, *refs)


def assemble_kernel(*refs):
    maps = refs[:-2]
    defl_ref, shear_ref = refs[-2:]
    steps, width = (maps[0].shape[0], maps[0].shape[-1])
    for c, map_ref in enumerate(maps):
        for i in range(steps):
            start = (c * steps + i) * width
            for k in range(defl_ref.shape[0]):
                for j in range(2):
                    defl_ref[k, j, :, start : start + width] = map_ref[i, 5 * k + j, 0:R]
                for j in range(3):
                    shear_ref[k, j, :, start : start + width] = map_ref[i, 5 * k + 2 + j, 0:R]


def own_tile(ref, k, planes, like):
    tile = ref[ref.shape[0] - planes + k, 0:R]
    return jnp.concatenate([tile] * (like.shape[1] // EDGE), axis=1)


def carry_kernel(planes, sender, in_ref, excess_ref, b_ref, m_ref, out_ref):
    @pl.when(lax.axis_index("plane") == sender)
    def _():
        for step in range(out_ref.shape[0]):
            fields = unpack_state([in_ref], step)
            p, q = (fields[0:4], fields[4:8])
            for k in reversed(range(planes)):
                m0, m1, off = (m_ref[step, 3 * k + j, 0:R] for j in range(3))
                p, q = transposed_step(m0, m1, off, p, q, -own_tile(excess_ref, k, planes, m0))
            pack_state(out_ref, step, p + q, b_ref)


def cotangent_kernel(planes, excess_ref, weight_ref, src_ref, m_ref, a_ref, *refs):
    arrived, cot_ref = (refs[:-1], refs[-1])
    blank = jnp.zeros((SUB - R, cot_ref.shape[-1]), F32)
    for step in range(cot_ref.shape[0]):
        fields = unpack_state(arrived, step)
        p, q = (fields[0:4], fields[4:8])
        for k in reversed(range(planes)):
            s0, s1, s3 = (src_ref[step, 3 * k + j, 0:R] for j in range(3))
            p = [p[0] + s0, p[1] + s1, p[2] + s1, p[3] + s3]
            a = [a_ref[step, 4 * k + j, 0:R] for j in range(4)]
            w = -own_tile(weight_ref, k, planes, s0)
            cots = [
                w * (p[0] * a[0] + p[1] * a[1]),
                w * (p[2] * a[2] + p[3] * a[3]),
                (0.25 * w) * (p[0] * a[2] + p[1] * a[3] + p[2] * a[0] + p[3] * a[1]),
            ]
            for j in range(3):
                cot_ref[step, 3 * k + j] = jnp.concatenate([cots[j], blank], axis=0)
            m0, m1, off = (m_ref[step, 3 * k + j, 0:R] for j in range(3))
            p, q = transposed_step(m0, m1, off, p, q, -own_tile(excess_ref, k, planes, m0))


def stencil_kernel(planes, *refs):
    cots, out_ref = (refs[:-1], refs[-1])
    out = out_ref.shape[-1]
    steps, width = (cots[0].shape[0], cots[0].shape[-1])
    blocks = len(cots) * steps

    def cot(block, field):
        return cots[block // steps].at[block % steps, field]

    for c in range(blocks):
        before = (c - 1) % blocks
        after = (c + 1) % blocks

        def ext(field):
            return jnp.concatenate(
                [
                    cot(before, field)[:, width - EDGE :],
                    cot(c, field)[...],
                    cot(after, field)[:, 0:EDGE],
                ],
                axis=1,
            )

        for k in range(planes):
            cot_rows = cot(c, 3 * k)[...]
            cot_cols = ext(3 * k + 1)
            cot_mixed = ext(3 * k + 2)
            across = row_up(cot_mixed) - row_down(cot_mixed)
            rows_part = row_up(cot_rows) + row_down(cot_rows) - 2.0 * cot_rows
            cols_part = col_next(cot_cols) + col_prev(cot_cols) - 2.0 * cot_cols[:, EDGE:-EDGE]
            grad = rows_part + cols_part + (col_next(across) - col_prev(across))
            for part in range(max(1, width // out)):
                place = c * width + part * out
                size = min(out, width)
                start = place % out
                out_ref[place // out, k, :, start : start + size] = grad[
                    :, part * out : part * out + size
                ]


def combine_kernel(in_ref, out_ref):
    slabs, planes, _, width = in_ref.shape
    blank = jnp.zeros((R - 2, width), F32)
    for k in range(planes):
        for s in range(slabs):
            halo = jnp.concatenate(
                [in_ref[(s - 1) % slabs, k, 6:7], blank, in_ref[(s + 1) % slabs, k, 7:8]], axis=0
            )
            out_ref[k, R * s : R * (s + 1), :] = in_ref[s, k, 0:R] + halo


def shape(*dims):
    return jax.ShapeDtypeStruct(dims, F32)


def params():
    return pltpu.CompilerParams(vmem_limit_bytes=VMEM_LIMIT)


SCALARS = pl.BlockSpec(memory_space=pltpu.SMEM)
WHOLE = pl.BlockSpec(memory_space=pltpu.VMEM)


def on_device(potential, mixing, lens_weight, observed, noise_weight):
    groups = lax.axis_size("plane")
    slabs = lax.axis_size("slab")
    planes, rows, width = potential.shape
    assert rows == R * slabs and width % EDGE == 0
    columns = width * slabs
    tiles = width // EDGE
    length = tiles * slabs // CHUNKS
    span = SPAN * EDGE
    steps = length // SPAN

    def climb(x, hop):
        return lax.ppermute(x, "plane", [(i, i + 1) for i in range(hop, groups - 1)])

    def descend(x, hop):
        return lax.ppermute(x, "plane", [(groups - 1 - hop, groups - 2 - hop)])

    coef = jnp.stack([lens_weight, mixing])
    packed, weights = pl.pallas_call(
        pack_kernel,
        out_shape=(shape(slabs, tiles, planes, SUB, EDGE), shape(planes, SUB, EDGE)),
        in_specs=[SCALARS, WHOLE],
        out_specs=(WHOLE, WHOLE),
        compiler_params=params(),
        name="pack",
    )(coef, potential)
    own = lax.all_to_all(packed, "slab", split_axis=0, concat_axis=0, tiled=True)
    own = own.reshape(slabs * tiles, planes, SUB, EDGE)
    pieces = pl.pallas_call(
        split_kernel,
        out_shape=tuple(
            shape(length + (c == 0), planes, SUB, EDGE) for c in range(CHUNKS)
        ),
        in_specs=[SCALARS, WHOLE],
        out_specs=(WHOLE,) * CHUNKS,
        compiler_params=params(),
        name="split",
    )(coef, own)
    strips = [[piece] for piece in pieces]
    for turn in range(CHUNKS + groups - 2):
        for c in range(CHUNKS):
            if 0 <= turn - c < groups - 1:
                strips[c].insert(0, climb(strips[c][0], turn - c))
    beside, excess = pl.pallas_call(
        edges_kernel,
        out_shape=(
            shape(CHUNKS, groups * planes, SUB, EDGE),
            shape(groups * planes, SUB, EDGE),
        ),
        in_specs=[WHOLE] * groups,
        out_specs=(WHOLE, WHOLE),
        compiler_params=params(),
        name="edges",
    )(*strips[0])

    maps = [None] * CHUNKS
    work = [None] * CHUNKS
    for c in range(CHUNKS):
        maps[c], *work[c] = pl.pallas_call(
            functools.partial(forward_kernel, groups, planes, c, length),
            out_shape=(
                shape(steps, 5 * planes, SUB, span),
                shape(steps, 3 * planes, SUB, span),
                shape(steps, 4 * planes, SUB, span),
                shape(steps, 3 * planes, SUB, span),
                shape(steps, R, SUB, span),
            ),
            in_specs=[WHOLE] * (groups + 4),
            out_specs=(WHOLE,) * 5,
            compiler_params=params(),
            name="forward",
        )(*strips[c], beside, excess, observed, noise_weight)

    cots = [None] * CHUNKS
    for c in range(CHUNKS):
        matrices, states, sources, b = work[c]
        arrived = [descend(b, 0)]
        for hop in range(1, groups - 1):
            outgoing = pl.pallas_call(
                functools.partial(carry_kernel, planes, groups - 1 - hop),
                out_shape=shape(steps, R, SUB, span),
                in_specs=[WHOLE] * 4,
                out_specs=WHOLE,
                compiler_params=params(),
                name="carry",
            )(arrived[-1], excess, b, matrices)
            arrived.append(descend(outgoing, hop))
        cots[c] = pl.pallas_call(
            functools.partial(cotangent_kernel, planes),
            out_shape=shape(steps, 3 * planes, SUB, span),
            in_specs=[WHOLE] * (groups + 4),
            out_specs=WHOLE,
            compiler_params=params(),
            name="cotangent",
        )(excess, weights, sources, matrices, states, *arrived)

    partial = pl.pallas_call(
        functools.partial(stencil_kernel, planes),
        out_shape=shape(slabs, planes, SUB, width),
        in_specs=[WHOLE] * CHUNKS,
        out_specs=WHOLE,
        compiler_params=params(),
        name="stencil",
    )(*cots)
    returned = lax.all_to_all(partial, "slab", split_axis=0, concat_axis=0, tiled=True)
    deflection, shear = pl.pallas_call(
        assemble_kernel,
        out_shape=(shape(planes, 2, R, columns), shape(planes, 3, R, columns)),
        in_specs=[WHOLE] * CHUNKS,
        out_specs=(WHOLE, WHOLE),
        compiler_params=params(),
        name="assemble",
    )(*maps)
    potential_grad = pl.pallas_call(
        combine_kernel,
        out_shape=shape(planes, rows, width),
        in_specs=[WHOLE],
        out_specs=WHOLE,
        compiler_params=params(),
        name="combine",
    )(returned)
    return (deflection, shear, potential_grad)


def solution(mesh):
    placed = (
        P("plane", None, "slab"),
        P("plane"),
        P("plane"),
        P("plane", None, "slab", None),
        P("plane", "slab", None),
    )
    return jax.shard_map(
        on_device,
        mesh=mesh,
        in_specs=placed,
        out_specs=(
            P("plane", None, "slab", None),
            P("plane", None, "slab", None),
            P("plane", None, "slab"),
        ),
        check_vma=False,
    )
```

```python
import functools

import jax
import jax.numpy as jnp
from jax import lax
from jax.experimental import pallas as pl
from jax.experimental.pallas import tpu as pltpu
from jax.sharding import PartitionSpec as P

R = 6
SUB = 8
EDGE = 128
F32 = jnp.float32
VMEM_LIMIT = 16 * 1024 * 1024
CHUNKS = 4
SPAN = 4
MIX_LANE = 64


def pack_kernel(coef_ref, p_ref, out_ref, weight_ref):
    planes, rows, width = p_ref.shape
    for k in range(planes):
        w = coef_ref[0, k]
        weight_ref[k] = jnp.full((SUB, EDGE), w, F32)
        for s in range(out_ref.shape[0]):
            before = (R * s - 1) % rows
            after = (R * (s + 1)) % rows
            strip = w * jnp.concatenate(
                [
                    p_ref[k, R * s : R * (s + 1), :],
                    p_ref[k, after : after + 1, :],
                    p_ref[k, before : before + 1, :],
                ],
                axis=0,
            )
            for t in range(width // EDGE):
                out_ref[s, t, k] = strip[:, EDGE * t : EDGE * (t + 1)]


def split_kernel(coef_ref, in_ref, *outs):
    tiles, planes = in_ref.shape[0:2]
    length = tiles // len(outs)
    lane = lax.broadcasted_iota(jnp.int32, (SUB, EDGE), 1)
    for c, out_ref in enumerate(outs):
        out_ref[0:length] = in_ref[length * c : length * (c + 1)]
    for k in range(planes):
        edge = jnp.where(lane == MIX_LANE, coef_ref[1, k] - 1.0, 0.0)
        for c in range(len(outs)):
            after = in_ref[(length * (c + 1)) % tiles, k]
            before = in_ref[(length * c - 1) % tiles, k]
            edge = jnp.where(lane == 2 * c, pltpu.roll(after, 2 * c, 1), edge)
            edge = jnp.where(lane == (2 * c - 1) % EDGE, pltpu.roll(before, 2 * c, 1), edge)
        outs[0][length, k] = edge


def edges_kernel(*refs):
    strips = refs[:-2]
    beside_ref, excess_ref = refs[-2:]
    for group, strip_ref in enumerate(strips):
        planes = strip_ref.shape[1]
        for k in range(planes):
            edge = strip_ref[strip_ref.shape[0] - 1, k]
            at = group * planes + k
            excess_ref[at] = jnp.broadcast_to(edge[:, MIX_LANE : MIX_LANE + 1], edge.shape)
            for c in range(CHUNKS):
                beside_ref[c, at] = pltpu.roll(edge, (EDGE - 2 * c) % EDGE, 1)


def row_up(x):
    return pltpu.roll(x, SUB - 1, 0)


def row_down(x):
    return pltpu.roll(x, 1, 0)


def col_prev(x):
    return pltpu.roll(x, 1, 1)[:, EDGE:-EDGE]


def col_next(x):
    return pltpu.roll(x, x.shape[1] - 1, 1)[:, EDGE:-EDGE]


def transposed_step(m0, m1, off, p, q, keep):
    new_p = [
        m0 * p[0] + off * p[2] + q[0],
        m0 * p[1] + off * p[3] + q[1],
        off * p[0] + m1 * p[2] + q[2],
        off * p[1] + m1 * p[3] + q[3],
    ]
    return (new_p, [keep * x for x in p])


def pack_state(out_ref, step, fields, extra_ref=None):
    for j in range(R):
        tile = jnp.concatenate(
            [fields[j], fields[6][j : j + 1], fields[7][j : j + 1]], axis=0
        )
        out_ref[step, j] = tile if extra_ref is None else tile + extra_ref[step, j]


def unpack_state(arrived, step):
    tiles = [sum(in_ref[step, j] for in_ref in arrived) for j in range(R)]
    fields = [t[0:R] for t in tiles]
    fields.append(jnp.concatenate([t[6:7] for t in tiles], axis=0))
    fields.append(jnp.concatenate([t[7:8] for t in tiles], axis=0))
    return fields


def forward_block(groups, planes, chunk, length, step, *refs):
    strips = refs[:groups]
    beside_ref, excess_ref, obs_ref, noise_ref = refs[groups : groups + 4]
    map_ref, m_ref, a_ref, src_ref, b_ref = refs[-5:]
    width = m_ref.shape[-1]
    span = width // EDGE
    first = step * span
    start = EDGE * (chunk * length + first)
    one = jnp.ones((SUB, width), F32)
    zero = jnp.zeros((SUB, width), F32)
    a = [one, zero, zero, one]
    a_before = a
    psi = jnp.zeros((SUB, width + 2 * EDGE), F32)
    psi_before = psi
    keeps = []
    for group in range(groups):
        strip_ref = strips[group]
        own = group == groups - 1
        for k in range(planes):
            beside = beside_ref[chunk, group * planes + k]
            excess_tile = excess_ref[group * planes + k]
            excess_ext = jnp.concatenate([excess_tile] * (span + 2), axis=1)
            excess = excess_ext[:, EDGE:-EDGE]
            mix_ext = jnp.concatenate([1.0 + excess_tile] * (span + 2), axis=1)
            mix = mix_ext[:, EDGE:-EDGE]
            left = strip_ref[first - 1, k] if first > 0 else beside
            right = strip_ref[first + span, k] if first + span < length else beside
            tiles = [strip_ref[first + t, k] for t in range(span)]
            mid = jnp.concatenate(tiles, axis=1)
            ext = jnp.concatenate([left] + tiles + [right], axis=1)
            up = row_up(ext)
            down = row_down(ext)
            across = up - down
            twice = 2.0 * mid
            m0 = mix - ((up + down)[:, EDGE:-EDGE] - twice)
            m1 = mix - (col_next(ext) + col_prev(ext) - twice)
            off = 0.25 * (col_prev(across) - col_next(across))
            if own:
                m_ref[step, 3 * k] = m0
                m_ref[step, 3 * k + 1] = m1
                m_ref[step, 3 * k + 2] = off
                keeps.append(-excess[0:R])
                for j in range(4):
                    a_ref[step, 4 * k + j] = a[j]
            new_a = [
                m0 * a[0] + off * a[2] - excess * a_before[0],
                m0 * a[1] + off * a[3] - excess * a_before[1],
                off * a[0] + m1 * a[2] - excess * a_before[2],
                off * a[1] + m1 * a[3] - excess * a_before[3],
            ]
            a_before, a = (a, new_a)
            psi, psi_before = (mix_ext * psi - excess_ext * psi_before - ext, psi)
            if own:
                slope_rows = 0.5 * (row_up(psi) - row_down(psi))[:, EDGE:-EDGE]
                slope_cols = 0.5 * (col_next(psi) - col_prev(psi))
                shear = [
                    1.0 - 0.5 * (a[0] + a[3]),
                    0.5 * (a[3] - a[0]),
                    -0.5 * (a[1] + a[2]),
                ]
                for j, field in enumerate([slope_rows, slope_cols] + shear):
                    map_ref[step, 5 * k + j] = field
                noise = -0.5 * noise_ref[k, :, start : start + width]
                r = [
                    noise * (shear[j][0:R] - obs_ref[k, j, :, start : start + width])
                    for j in range(3)
                ]
                src_ref[step, 3 * k, 0:R] = r[0] + r[1]
                src_ref[step, 3 * k + 1, 0:R] = r[2]
                src_ref[step, 3 * k + 2, 0:R] = r[0] - r[1]
    none = jnp.zeros((R, width), F32)
    p = [none] * 4
    q = [none] * 4
    for k in reversed(range(planes)):
        s0, s1, s3 = (src_ref[step, 3 * k + j, 0:R] for j in range(3))
        p = [p[0] + s0, p[1] + s1, p[2] + s1, p[3] + s3]
        m0, m1, off = (m_ref[step, 3 * k + j, 0:R] for j in range(3))
        p, q = transposed_step(m0, m1, off, p, q, keeps[k])
    pack_state(b_ref, step, p + q)


def forward_kernel(groups, planes, chunk, length, *refs):
    for step in range(refs[-1].shape[0]):
        forward_block(groups, planes, chunk, length, step, *refs)


def assemble_kernel(*refs):
    maps = refs[:-2]
    defl_ref, shear_ref = refs[-2:]
    steps, width = (maps[0].shape[0], maps[0].shape[-1])
    for c, map_ref in enumerate(maps):
        for i in range(steps):
            start = (c * steps + i) * width
            for k in range(defl_ref.shape[0]):
                for j in range(2):
                    defl_ref[k, j, :, start : start + width] = map_ref[i, 5 * k + j, 0:R]
                for j in range(3):
                    shear_ref[k, j, :, start : start + width] = map_ref[i, 5 * k + 2 + j, 0:R]


def own_tile(ref, k, planes, like):
    tile = ref[ref.shape[0] - planes + k, 0:R]
    return jnp.concatenate([tile] * (like.shape[1] // EDGE), axis=1)


def carry_kernel(planes, sender, in_ref, excess_ref, b_ref, m_ref, out_ref):
    @pl.when(lax.axis_index("plane") == sender)
    def _():
        for step in range(out_ref.shape[0]):
            fields = unpack_state([in_ref], step)
            p, q = (fields[0:4], fields[4:8])
            for k in reversed(range(planes)):
                m0, m1, off = (m_ref[step, 3 * k + j, 0:R] for j in range(3))
                p, q = transposed_step(m0, m1, off, p, q, -own_tile(excess_ref, k, planes, m0))
            pack_state(out_ref, step, p + q, b_ref)


def cotangent_kernel(planes, excess_ref, weight_ref, src_ref, m_ref, a_ref, *refs):
    arrived, cot_ref = (refs[:-1], refs[-1])
    blank = jnp.zeros((SUB - R, cot_ref.shape[-1]), F32)
    for step in range(cot_ref.shape[0]):
        fields = unpack_state(arrived, step)
        p, q = (fields[0:4], fields[4:8])
        for k in reversed(range(planes)):
            s0, s1, s3 = (src_ref[step, 3 * k + j, 0:R] for j in range(3))
            p = [p[0] + s0, p[1] + s1, p[2] + s1, p[3] + s3]
            a = [a_ref[step, 4 * k + j, 0:R] for j in range(4)]
            w = -own_tile(weight_ref, k, planes, s0)
            cots = [
                w * (p[0] * a[0] + p[1] * a[1]),
                w * (p[2] * a[2] + p[3] * a[3]),
                (0.25 * w) * (p[0] * a[2] + p[1] * a[3] + p[2] * a[0] + p[3] * a[1]),
            ]
            for j in range(3):
                cot_ref[step, 3 * k + j] = jnp.concatenate([cots[j], blank], axis=0)
            m0, m1, off = (m_ref[step, 3 * k + j, 0:R] for j in range(3))
            p, q = transposed_step(m0, m1, off, p, q, -own_tile(excess_ref, k, planes, m0))


def stencil_kernel(planes, *refs):
    cots, out_ref = (refs[:-1], refs[-1])
    out = out_ref.shape[-1]
    steps, width = (cots[0].shape[0], cots[0].shape[-1])
    blocks = len(cots) * steps

    def cot(block, field):
        return cots[block // steps].at[block % steps, field]

    for c in range(blocks):
        before = (c - 1) % blocks
        after = (c + 1) % blocks

        def ext(field):
            return jnp.concatenate(
                [
                    cot(before, field)[:, width - EDGE :],
                    cot(c, field)[...],
                    cot(after, field)[:, 0:EDGE],
                ],
                axis=1,
            )

        for k in range(planes):
            cot_rows = cot(c, 3 * k)[...]
            cot_cols = ext(3 * k + 1)
            cot_mixed = ext(3 * k + 2)
            across = row_up(cot_mixed) - row_down(cot_mixed)
            rows_part = row_up(cot_rows) + row_down(cot_rows) - 2.0 * cot_rows
            cols_part = col_next(cot_cols) + col_prev(cot_cols) - 2.0 * cot_cols[:, EDGE:-EDGE]
            grad = rows_part + cols_part + (col_next(across) - col_prev(across))
            for part in range(max(1, width // out)):
                place = c * width + part * out
                size = min(out, width)
                start = place % out
                out_ref[place // out, k, :, start : start + size] = grad[
                    :, part * out : part * out + size
                ]


def combine_kernel(in_ref, out_ref):
    slabs, planes, _, width = in_ref.shape
    blank = jnp.zeros((R - 2, width), F32)
    for k in range(planes):
        for s in range(slabs):
            halo = jnp.concatenate(
                [in_ref[(s - 1) % slabs, k, 6:7], blank, in_ref[(s + 1) % slabs, k, 7:8]], axis=0
            )
            out_ref[k, R * s : R * (s + 1), :] = in_ref[s, k, 0:R] + halo


def shape(*dims):
    return jax.ShapeDtypeStruct(dims, F32)


def params():
    return pltpu.CompilerParams(vmem_limit_bytes=VMEM_LIMIT)


SCALARS = pl.BlockSpec(memory_space=pltpu.SMEM)
WHOLE = pl.BlockSpec(memory_space=pltpu.VMEM)


def on_device(potential, mixing, lens_weight, observed, noise_weight):
    groups = lax.axis_size("plane")
    slabs = lax.axis_size("slab")
    planes, rows, width = potential.shape
    assert rows == R * slabs and width % EDGE == 0
    columns = width * slabs
    tiles = width // EDGE
    length = tiles * slabs // CHUNKS
    span = SPAN * EDGE
    steps = length // SPAN

    def climb(x, hop):
        return lax.ppermute(x, "plane", [(i, i + 1) for i in range(hop, groups - 1)])

    def descend(x, hop):
        return lax.ppermute(x, "plane", [(groups - 1 - hop, groups - 2 - hop)])

    coef = jnp.stack([lens_weight, mixing])
    packed, weights = pl.pallas_call(
        pack_kernel,
        out_shape=(shape(slabs, tiles, planes, SUB, EDGE), shape(planes, SUB, EDGE)),
        in_specs=[SCALARS, WHOLE],
        out_specs=(WHOLE, WHOLE),
        compiler_params=params(),
        name="pack",
    )(coef, potential)
    own = lax.all_to_all(packed, "slab", split_axis=0, concat_axis=0, tiled=True)
    own = own.reshape(slabs * tiles, planes, SUB, EDGE)
    pieces = pl.pallas_call(
        split_kernel,
        out_shape=tuple(
            shape(length + (c == 0), planes, SUB, EDGE) for c in range(CHUNKS)
        ),
        in_specs=[SCALARS, WHOLE],
        out_specs=(WHOLE,) * CHUNKS,
        compiler_params=params(),
        name="split",
    )(coef, own)
    strips = [[piece] for piece in pieces]
    for turn in range(CHUNKS + groups - 2):
        for c in range(CHUNKS):
            if 0 <= turn - c < groups - 1:
                strips[c].insert(0, climb(strips[c][0], turn - c))
    beside, excess = pl.pallas_call(
        edges_kernel,
        out_shape=(
            shape(CHUNKS, groups * planes, SUB, EDGE),
            shape(groups * planes, SUB, EDGE),
        ),
        in_specs=[WHOLE] * groups,
        out_specs=(WHOLE, WHOLE),
        compiler_params=params(),
        name="edges",
    )(*strips[0])

    maps = [None] * CHUNKS
    work = [None] * CHUNKS
    for c in range(CHUNKS):
        if c == CHUNKS - 1:
            strips[c][0] = lax.optimization_barrier((strips[c][0], work[0][-1]))[0]
        maps[c], *work[c] = pl.pallas_call(
            functools.partial(forward_kernel, groups, planes, c, length),
            out_shape=(
                shape(steps, 5 * planes, SUB, span),
                shape(steps, 3 * planes, SUB, span),
                shape(steps, 4 * planes, SUB, span),
                shape(steps, 3 * planes, SUB, span),
                shape(steps, R, SUB, span),
            ),
            in_specs=[WHOLE] * (groups + 4),
            out_specs=(WHOLE,) * 5,
            compiler_params=params(),
            name="forward",
        )(*strips[c], beside, excess, observed, noise_weight)

    cots = [None] * CHUNKS
    for c in range(CHUNKS):
        matrices, states, sources, b = work[c]
        arrived = [descend(b, 0)]
        for hop in range(1, groups - 1):
            outgoing = pl.pallas_call(
                functools.partial(carry_kernel, planes, groups - 1 - hop),
                out_shape=shape(steps, R, SUB, span),
                in_specs=[WHOLE] * 4,
                out_specs=WHOLE,
                compiler_params=params(),
                name="carry",
            )(arrived[-1], excess, b, matrices)
            arrived.append(descend(outgoing, hop))
        cots[c] = pl.pallas_call(
            functools.partial(cotangent_kernel, planes),
            out_shape=shape(steps, 3 * planes, SUB, span),
            in_specs=[WHOLE] * (groups + 4),
            out_specs=WHOLE,
            compiler_params=params(),
            name="cotangent",
        )(excess, weights, sources, matrices, states, *arrived)

    partial = pl.pallas_call(
        functools.partial(stencil_kernel, planes),
        out_shape=shape(slabs, planes, SUB, width),
        in_specs=[WHOLE] * CHUNKS,
        out_specs=WHOLE,
        compiler_params=params(),
        name="stencil",
    )(*cots)
    returned = lax.all_to_all(partial, "slab", split_axis=0, concat_axis=0, tiled=True)
    deflection, shear = pl.pallas_call(
        assemble_kernel,
        out_shape=(shape(planes, 2, R, columns), shape(planes, 3, R, columns)),
        in_specs=[WHOLE] * CHUNKS,
        out_specs=(WHOLE, WHOLE),
        compiler_params=params(),
        name="assemble",
    )(*maps)
    potential_grad = pl.pallas_call(
        combine_kernel,
        out_shape=shape(planes, rows, width),
        in_specs=[WHOLE],
        out_specs=WHOLE,
        compiler_params=params(),
        name="combine",
    )(returned)
    return (deflection, shear, potential_grad)


def solution(mesh):
    placed = (
        P("plane", None, "slab"),
        P("plane"),
        P("plane"),
        P("plane", None, "slab", None),
        P("plane", "slab", None),
    )
    return jax.shard_map(
        on_device,
        mesh=mesh,
        in_specs=placed,
        out_specs=(
            P("plane", None, "slab", None),
            P("plane", None, "slab", None),
            P("plane", None, "slab"),
        ),
        check_vma=False,
    )
```

```python
import functools

import jax
import jax.numpy as jnp
from jax import lax
from jax.experimental import pallas as pl
from jax.experimental.pallas import tpu as pltpu
from jax.sharding import PartitionSpec as P

R = 6
SUB = 8
EDGE = 128
F32 = jnp.float32
VMEM_LIMIT = 16 * 1024 * 1024
CHUNKS = 4
SPAN = 4
MIX_LANE = 64


def pack_kernel(coef_ref, p_ref, out_ref, weight_ref):
    planes, rows, width = p_ref.shape
    for k in range(planes):
        w = coef_ref[0, k]
        weight_ref[k] = jnp.full((SUB, EDGE), w, F32)
        for s in range(out_ref.shape[0]):
            before = (R * s - 1) % rows
            after = (R * (s + 1)) % rows
            strip = w * jnp.concatenate(
                [
                    p_ref[k, R * s : R * (s + 1), :],
                    p_ref[k, after : after + 1, :],
                    p_ref[k, before : before + 1, :],
                ],
                axis=0,
            )
            for t in range(width // EDGE):
                out_ref[s, t, k] = strip[:, EDGE * t : EDGE * (t + 1)]


def split_kernel(coef_ref, in_ref, *outs):
    tiles, planes = in_ref.shape[0:2]
    length = tiles // len(outs)
    lane = lax.broadcasted_iota(jnp.int32, (SUB, EDGE), 1)
    for c, out_ref in enumerate(outs):
        out_ref[0:length] = in_ref[length * c : length * (c + 1)]
    for k in range(planes):
        edge = jnp.where(lane == MIX_LANE, coef_ref[1, k] - 1.0, 0.0)
        for c in range(len(outs)):
            after = in_ref[(length * (c + 1)) % tiles, k]
            before = in_ref[(length * c - 1) % tiles, k]
            edge = jnp.where(lane == 2 * c, pltpu.roll(after, 2 * c, 1), edge)
            edge = jnp.where(lane == (2 * c - 1) % EDGE, pltpu.roll(before, 2 * c, 1), edge)
        outs[0][length, k] = edge


def edges_kernel(*refs):
    strips = refs[:-2]
    beside_ref, excess_ref = refs[-2:]
    for group, strip_ref in enumerate(strips):
        planes = strip_ref.shape[1]
        for k in range(planes):
            edge = strip_ref[strip_ref.shape[0] - 1, k]
            at = group * planes + k
            excess_ref[at] = jnp.broadcast_to(edge[:, MIX_LANE : MIX_LANE + 1], edge.shape)
            for c in range(CHUNKS):
                beside_ref[c, at] = pltpu.roll(edge, (EDGE - 2 * c) % EDGE, 1)


def row_up(x):
    return pltpu.roll(x, SUB - 1, 0)


def row_down(x):
    return pltpu.roll(x, 1, 0)


def col_prev(x):
    return pltpu.roll(x, 1, 1)[:, EDGE:-EDGE]


def col_next(x):
    return pltpu.roll(x, x.shape[1] - 1, 1)[:, EDGE:-EDGE]


def transposed_step(m0, m1, off, p, q, keep):
    new_p = [
        m0 * p[0] + off * p[2] + q[0],
        m0 * p[1] + off * p[3] + q[1],
        off * p[0] + m1 * p[2] + q[2],
        off * p[1] + m1 * p[3] + q[3],
    ]
    return (new_p, [keep * x for x in p])


def pack_state(out_ref, step, fields, extra_ref=None):
    for j in range(R):
        tile = jnp.concatenate(
            [fields[j], fields[6][j : j + 1], fields[7][j : j + 1]], axis=0
        )
        out_ref[step, j] = tile if extra_ref is None else tile + extra_ref[step, j]


def unpack_state(arrived, step):
    tiles = [sum(in_ref[step, j] for in_ref in arrived) for j in range(R)]
    fields = [t[0:R] for t in tiles]
    fields.append(jnp.concatenate([t[6:7] for t in tiles], axis=0))
    fields.append(jnp.concatenate([t[7:8] for t in tiles], axis=0))
    return fields


def forward_block(groups, planes, chunk, length, step, *refs):
    strips = refs[:groups]
    beside_ref, excess_ref, obs_ref, noise_ref = refs[groups : groups + 4]
    map_ref, m_ref, a_ref, src_ref, b_ref = refs[-5:]
    width = m_ref.shape[-1]
    span = width // EDGE
    first = step * span
    start = EDGE * (chunk * length + first)
    one = jnp.ones((SUB, width), F32)
    zero = jnp.zeros((SUB, width), F32)
    a = [one, zero, zero, one]
    a_before = a
    psi = jnp.zeros((SUB, width + 2 * EDGE), F32)
    psi_before = psi
    keeps = []
    for group in range(groups):
        strip_ref = strips[group]
        own = group == groups - 1
        for k in range(planes):
            beside = beside_ref[chunk, group * planes + k]
            excess_tile = excess_ref[group * planes + k]
            excess_ext = jnp.concatenate([excess_tile] * (span + 2), axis=1)
            excess = excess_ext[:, EDGE:-EDGE]
            mix_ext = jnp.concatenate([1.0 + excess_tile] * (span + 2), axis=1)
            mix = mix_ext[:, EDGE:-EDGE]
            left = strip_ref[first - 1, k] if first > 0 else beside
            right = strip_ref[first + span, k] if first + span < length else beside
            tiles = [strip_ref[first + t, k] for t in range(span)]
            mid = jnp.concatenate(tiles, axis=1)
            ext = jnp.concatenate([left] + tiles + [right], axis=1)
            up = row_up(ext)
            down = row_down(ext)
            across = up - down
            twice = 2.0 * mid
            m0 = mix - ((up + down)[:, EDGE:-EDGE] - twice)
            m1 = mix - (col_next(ext) + col_prev(ext) - twice)
            off = 0.25 * (col_prev(across) - col_next(across))
            if own:
                m_ref[step, 3 * k] = m0
                m_ref[step, 3 * k + 1] = m1
                m_ref[step, 3 * k + 2] = off
                keeps.append(-excess[0:R])
                for j in range(4):
                    a_ref[step, 4 * k + j] = a[j]
            new_a = [
                m0 * a[0] + off * a[2] - excess * a_before[0],
                m0 * a[1] + off * a[3] - excess * a_before[1],
                off * a[0] + m1 * a[2] - excess * a_before[2],
                off * a[1] + m1 * a[3] - excess * a_before[3],
            ]
            a_before, a = (a, new_a)
            psi, psi_before = (mix_ext * psi - excess_ext * psi_before - ext, psi)
            if own:
                slope_rows = 0.5 * (row_up(psi) - row_down(psi))[:, EDGE:-EDGE]
                slope_cols = 0.5 * (col_next(psi) - col_prev(psi))
                shear = [
                    1.0 - 0.5 * (a[0] + a[3]),
                    0.5 * (a[3] - a[0]),
                    -0.5 * (a[1] + a[2]),
                ]
                for j, field in enumerate([slope_rows, slope_cols] + shear):
                    map_ref[step, 5 * k + j] = field
                noise = -0.5 * noise_ref[k, :, start : start + width]
                r = [
                    noise * (shear[j][0:R] - obs_ref[k, j, :, start : start + width])
                    for j in range(3)
                ]
                src_ref[step, 3 * k, 0:R] = r[0] + r[1]
                src_ref[step, 3 * k + 1, 0:R] = r[2]
                src_ref[step, 3 * k + 2, 0:R] = r[0] - r[1]
    none = jnp.zeros((R, width), F32)
    p = [none] * 4
    q = [none] * 4
    for k in reversed(range(planes)):
        s0, s1, s3 = (src_ref[step, 3 * k + j, 0:R] for j in range(3))
        p = [p[0] + s0, p[1] + s1, p[2] + s1, p[3] + s3]
        m0, m1, off = (m_ref[step, 3 * k + j, 0:R] for j in range(3))
        p, q = transposed_step(m0, m1, off, p, q, keeps[k])
    pack_state(b_ref, step, p + q)


def forward_kernel(groups, planes, chunk, length, *refs):
    for step in range(refs[-1].shape[0]):
        forward_block(groups, planes, chunk, length, step, *refs)


def assemble_kernel(*refs):
    maps = refs[:-2]
    defl_ref, shear_ref = refs[-2:]
    steps, width = (maps[0].shape[0], maps[0].shape[-1])
    for c, map_ref in enumerate(maps):
        for i in range(steps):
            start = (c * steps + i) * width
            for k in range(defl_ref.shape[0]):
                for j in range(2):
                    defl_ref[k, j, :, start : start + width] = map_ref[i, 5 * k + j, 0:R]
                for j in range(3):
                    shear_ref[k, j, :, start : start + width] = map_ref[i, 5 * k + 2 + j, 0:R]


def own_tile(ref, k, planes, like):
    tile = ref[ref.shape[0] - planes + k, 0:R]
    return jnp.concatenate([tile] * (like.shape[1] // EDGE), axis=1)


def carry_kernel(planes, sender, in_ref, excess_ref, b_ref, m_ref, out_ref):
    @pl.when(lax.axis_index("plane") == sender)
    def _():
        for step in range(out_ref.shape[0]):
            fields = unpack_state([in_ref], step)
            p, q = (fields[0:4], fields[4:8])
            for k in reversed(range(planes)):
                m0, m1, off = (m_ref[step, 3 * k + j, 0:R] for j in range(3))
                p, q = transposed_step(m0, m1, off, p, q, -own_tile(excess_ref, k, planes, m0))
            pack_state(out_ref, step, p + q, b_ref)


def cotangent_kernel(planes, excess_ref, weight_ref, src_ref, m_ref, a_ref, *refs):
    arrived, cot_ref = (refs[:-1], refs[-1])
    blank = jnp.zeros((SUB - R, cot_ref.shape[-1]), F32)
    for step in range(cot_ref.shape[0]):
        fields = unpack_state(arrived, step)
        p, q = (fields[0:4], fields[4:8])
        for k in reversed(range(planes)):
            s0, s1, s3 = (src_ref[step, 3 * k + j, 0:R] for j in range(3))
            p = [p[0] + s0, p[1] + s1, p[2] + s1, p[3] + s3]
            a = [a_ref[step, 4 * k + j, 0:R] for j in range(4)]
            w = -own_tile(weight_ref, k, planes, s0)
            cots = [
                w * (p[0] * a[0] + p[1] * a[1]),
                w * (p[2] * a[2] + p[3] * a[3]),
                (0.25 * w) * (p[0] * a[2] + p[1] * a[3] + p[2] * a[0] + p[3] * a[1]),
            ]
            for j in range(3):
                cot_ref[step, 3 * k + j] = jnp.concatenate([cots[j], blank], axis=0)
            m0, m1, off = (m_ref[step, 3 * k + j, 0:R] for j in range(3))
            p, q = transposed_step(m0, m1, off, p, q, -own_tile(excess_ref, k, planes, m0))


def stencil_kernel(planes, *refs):
    cots, out_ref = (refs[:-1], refs[-1])
    out = out_ref.shape[-1]
    steps, width = (cots[0].shape[0], cots[0].shape[-1])
    blocks = len(cots) * steps

    def cot(block, field):
        return cots[block // steps].at[block % steps, field]

    for c in range(blocks):
        before = (c - 1) % blocks
        after = (c + 1) % blocks

        def ext(field):
            return jnp.concatenate(
                [
                    cot(before, field)[:, width - EDGE :],
                    cot(c, field)[...],
                    cot(after, field)[:, 0:EDGE],
                ],
                axis=1,
            )

        for k in range(planes):
            cot_rows = cot(c, 3 * k)[...]
            cot_cols = ext(3 * k + 1)
            cot_mixed = ext(3 * k + 2)
            across = row_up(cot_mixed) - row_down(cot_mixed)
            rows_part = row_up(cot_rows) + row_down(cot_rows) - 2.0 * cot_rows
            cols_part = col_next(cot_cols) + col_prev(cot_cols) - 2.0 * cot_cols[:, EDGE:-EDGE]
            grad = rows_part + cols_part + (col_next(across) - col_prev(across))
            for part in range(max(1, width // out)):
                place = c * width + part * out
                size = min(out, width)
                start = place % out
                out_ref[place // out, k, :, start : start + size] = grad[
                    :, part * out : part * out + size
                ]


def combine_kernel(in_ref, out_ref):
    slabs, planes, _, width = in_ref.shape
    blank = jnp.zeros((R - 2, width), F32)
    for k in range(planes):
        for s in range(slabs):
            halo = jnp.concatenate(
                [in_ref[(s - 1) % slabs, k, 6:7], blank, in_ref[(s + 1) % slabs, k, 7:8]], axis=0
            )
            out_ref[k, R * s : R * (s + 1), :] = in_ref[s, k, 0:R] + halo


def shape(*dims):
    return jax.ShapeDtypeStruct(dims, F32)


def params():
    return pltpu.CompilerParams(vmem_limit_bytes=VMEM_LIMIT)


SCALARS = pl.BlockSpec(memory_space=pltpu.SMEM)
WHOLE = pl.BlockSpec(memory_space=pltpu.VMEM)


def on_device(potential, mixing, lens_weight, observed, noise_weight):
    groups = lax.axis_size("plane")
    slabs = lax.axis_size("slab")
    planes, rows, width = potential.shape
    assert rows == R * slabs and width % EDGE == 0
    columns = width * slabs
    tiles = width // EDGE
    length = tiles * slabs // CHUNKS
    span = SPAN * EDGE
    steps = length // SPAN

    def climb(x, hop):
        return lax.ppermute(x, "plane", [(i, i + 1) for i in range(hop, groups - 1)])

    def descend(x, hop):
        return lax.ppermute(x, "plane", [(groups - 1 - hop, groups - 2 - hop)])

    coef = jnp.stack([lens_weight, mixing])
    packed, weights = pl.pallas_call(
        pack_kernel,
        out_shape=(shape(slabs, tiles, planes, SUB, EDGE), shape(planes, SUB, EDGE)),
        in_specs=[SCALARS, WHOLE],
        out_specs=(WHOLE, WHOLE),
        compiler_params=params(),
        name="pack",
    )(coef, potential)
    own = lax.all_to_all(packed, "slab", split_axis=0, concat_axis=0, tiled=True)
    own = own.reshape(slabs * tiles, planes, SUB, EDGE)
    pieces = pl.pallas_call(
        split_kernel,
        out_shape=tuple(
            shape(length + (c == 0), planes, SUB, EDGE) for c in range(CHUNKS)
        ),
        in_specs=[SCALARS, WHOLE],
        out_specs=(WHOLE,) * CHUNKS,
        compiler_params=params(),
        name="split",
    )(coef, own)
    strips = [[piece] for piece in pieces]
    for turn in range(CHUNKS + groups - 2):
        for c in range(CHUNKS):
            if 0 <= turn - c < groups - 1:
                strips[c].insert(0, climb(strips[c][0], turn - c))
    beside, excess = pl.pallas_call(
        edges_kernel,
        out_shape=(
            shape(CHUNKS, groups * planes, SUB, EDGE),
            shape(groups * planes, SUB, EDGE),
        ),
        in_specs=[WHOLE] * groups,
        out_specs=(WHOLE, WHOLE),
        compiler_params=params(),
        name="edges",
    )(*strips[0])

    maps = [None] * CHUNKS
    work = [None] * CHUNKS
    for c in range(CHUNKS):
        if c == CHUNKS - 1:
            strips[c][0] = lax.optimization_barrier((strips[c][0], work[0][-1]))[0]
        maps[c], *work[c] = pl.pallas_call(
            functools.partial(forward_kernel, groups, planes, c, length),
            out_shape=(
                shape(steps, 5 * planes, SUB, span),
                shape(steps, 3 * planes, SUB, span),
                shape(steps, 4 * planes, SUB, span),
                shape(steps, 3 * planes, SUB, span),
                shape(steps, R, SUB, span),
            ),
            in_specs=[WHOLE] * (groups + 4),
            out_specs=(WHOLE,) * 5,
            compiler_params=params(),
            name="forward",
        )(*strips[c], beside, excess, observed, noise_weight)

    cots = [None] * CHUNKS
    for c in list(range(1, CHUNKS)) + [0]:
        matrices, states, sources, b = work[c]
        arrived = [descend(b, 0)]
        for hop in range(1, groups - 1):
            outgoing = pl.pallas_call(
                functools.partial(carry_kernel, planes, groups - 1 - hop),
                out_shape=shape(steps, R, SUB, span),
                in_specs=[WHOLE] * 4,
                out_specs=WHOLE,
                compiler_params=params(),
                name="carry",
            )(arrived[-1], excess, b, matrices)
            arrived.append(descend(outgoing, hop))
        cots[c] = pl.pallas_call(
            functools.partial(cotangent_kernel, planes),
            out_shape=shape(steps, 3 * planes, SUB, span),
            in_specs=[WHOLE] * (groups + 4),
            out_specs=WHOLE,
            compiler_params=params(),
            name="cotangent",
        )(excess, weights, sources, matrices, states, *arrived)

    partial = pl.pallas_call(
        functools.partial(stencil_kernel, planes),
        out_shape=shape(slabs, planes, SUB, width),
        in_specs=[WHOLE] * CHUNKS,
        out_specs=WHOLE,
        compiler_params=params(),
        name="stencil",
    )(*cots)
    returned = lax.all_to_all(partial, "slab", split_axis=0, concat_axis=0, tiled=True)
    deflection, shear = pl.pallas_call(
        assemble_kernel,
        out_shape=(shape(planes, 2, R, columns), shape(planes, 3, R, columns)),
        in_specs=[WHOLE] * CHUNKS,
        out_specs=(WHOLE, WHOLE),
        compiler_params=params(),
        name="assemble",
    )(*maps)
    potential_grad = pl.pallas_call(
        combine_kernel,
        out_shape=shape(planes, rows, width),
        in_specs=[WHOLE],
        out_specs=WHOLE,
        compiler_params=params(),
        name="combine",
    )(returned)
    return (deflection, shear, potential_grad)


def solution(mesh):
    placed = (
        P("plane", None, "slab"),
        P("plane"),
        P("plane"),
        P("plane", None, "slab", None),
        P("plane", "slab", None),
    )
    return jax.shard_map(
        on_device,
        mesh=mesh,
        in_specs=placed,
        out_specs=(
            P("plane", None, "slab", None),
            P("plane", None, "slab", None),
            P("plane", None, "slab"),
        ),
        check_vma=False,
    )
```
